32 devices in a mesh: row: 4 (over y, x), col: 8 (over z, core).
Axes of the slice: x: 2, y: 2, z: 4, core: 2. Of those that a mesh axis runs over, the one named last changes fastest.
Arguments:
- features: bfloat16 [16384, 512], P(('row', 'col')), may hold values from -6 to 6
- tile_cols: int32 [4, 8, 16, 8], P('row', 'col'), may hold values from 0 to 31, as said below
- tile_masks: bfloat16 [4, 8, 16, 8, 128, 128], P('row', 'col'), may hold values from 0 to 1, as said below
- degree: int32 [16384], P(('row', 'col')), may hold values from 8 to 32
- owner_nodes: int32 [16384], P(('row', 'col')), may hold values from 0 to 16383, as said below
- owner_position: int32 [16384], P(('row', 'col')), may hold values from 0 to 16383, as said below
- self_weight: bfloat16 [512, 512], replicated, may hold values from -0.25 to 0.25
- neigh_weight: bfloat16 [512, 512], replicated, may hold values from -0.25 to 0.25
- cotangent: bfloat16 [16384, 512], P(('row', 'col')), may hold values from -6 to 6
Outputs:
- hidden: bfloat16 [16384, 512], P(('row', 'col'))
- grad_features: bfloat16 [16384, 512], P(('row', 'col'))
- grad_self: float32 [512, 512], replicated
- grad_neigh: float32 [512, 512], replicated
The draws below stay inside these ranges and needn't reach their ends.
Inputs may be any that keep to these rules, and one draw needn't show every extreme that they name: `tile_cols`: in each grid cell, the 8 entries of one tile row are different tile columns. `tile_masks`: entries are 0 or 1. `owner_nodes`: A permutation of the node numbers. For any two devices, the number of nodes of the first one's block that the second one holds in the owner layout is 0 or exactly 32. `owner_position`: the inverse permutation of owner_nodes.
All inputs are finite; a program needn't handle non-finite values.
Results may differ from the reference program's by a relative error of at most 0.013.
Values may be sent and summed in bfloat16 or wider, within the bound.
No kernel may reach another device: no remote copies, remote signals or barrier semaphores. Data moves between devices by JAX's collectives and lax.ppermute only.
A program may use at most 128 MiB of HBM per device.

```python
import math
import jax
import jax.numpy as jnp
from jax import lax

F = 512
TILE = 128
ROWS_DEV = 512
TPR = 8
NODES = 16384
CAP = 32
TROWS = 16
TCOLS = 32
N_ROW = 4
N_COL = 8


def relay_tables(key):
    devices = NODES // ROWS_DEV
    relay_key = jax.random.fold_in(key, 17)
    key_list = jax.random.split(relay_key, 4)
    labels = jax.random.permutation(key_list[0], devices).astype(jnp.int32)
    inverse = jnp.zeros((devices,), jnp.int32).at[labels].set(jnp.arange(devices, dtype=jnp.int32))
    shifts = jax.random.permutation(key_list[1], devices)[:devices // 2].astype(jnp.int32)
    orders = jax.vmap(lambda one_key: jax.random.permutation(one_key, ROWS_DEV))(jax.random.split(key_list[2], devices)).astype(jnp.int32)
    placements = jax.vmap(lambda one_key: jax.random.permutation(one_key, ROWS_DEV))(jax.random.split(key_list[3], devices)).astype(jnp.int32)
    group_index = orders // CAP
    sources = jnp.arange(devices, dtype=jnp.int32)[:, None]
    owner_device = inverse[(labels[sources] + shifts[group_index]) % devices]
    position = owner_device * ROWS_DEV + placements[owner_device, orders]
    owner_position = position.reshape(-1).astype(jnp.int32)
    owner_nodes = jnp.zeros((NODES,), jnp.int32).at[owner_position].set(jnp.arange(NODES, dtype=jnp.int32))
    return (owner_nodes, owner_position)


def draw_owner_nodes(key, part):
    return relay_tables(key)[0]


def draw_owner_position(key, part):
    return relay_tables(key)[1]


def draw_tile_cols(key, part):
    cols_key = jax.random.fold_in(key, 11)
    key_list = jax.random.split(cols_key, N_ROW * N_COL * TROWS)
    picks = jax.vmap(lambda one_key: jax.random.permutation(one_key, TCOLS)[:TPR])(key_list)
    return picks.reshape(N_ROW, N_COL, TROWS, TPR).astype(jnp.int32)


def draw_tile_masks(key, part):
    mask_key = jax.random.fold_in(key, 13)
    key_pair = jax.random.split(mask_key, 2)
    shape_lead = (N_ROW, N_COL, TROWS, TPR, 1, 1)
    entries_row = float(TILE * TPR)
    expected = jax.random.uniform(key_pair[0], shape_lead, jnp.float32, 8.0, 32.0)
    density = jnp.minimum(expected / entries_row, 1.0)
    uniform_draw = jax.random.uniform(key_pair[1], (N_ROW, N_COL, TROWS, TPR, TILE, TILE), jnp.float32)
    return (uniform_draw < density).astype(jnp.float32).astype(jnp.bfloat16)


def place_ends(drawn, own_key, least, top_value):
    extent = drawn.shape
    index_at = [jax.random.randint(jax.random.fold_in(own_key, axis), (), 0, extent[axis]) for axis in range(len(extent))]
    drawn = drawn.at[tuple(index_at)].set(least)
    longest = extent.index(max(extent))
    index_at[longest] = (index_at[longest] + 1) % extent[longest]
    return drawn.at[tuple(index_at)].set(top_value)


def level_of(key, shape, cuts, low, top_value):
    level, own = 1.0, jax.random.fold_in(key, 6)
    for dim, blocks in cuts:
        steps = jnp.exp(jax.random.uniform(jax.random.fold_in(own, dim), (blocks,), jnp.float32, low / len(cuts), top_value / len(cuts)))
        level = level * jnp.repeat(steps, shape[dim] // blocks).reshape([-1 if axis == dim else 1 for axis in range(len(shape))])
    return level


def centred(own_key, dims, scale, limit, cuts=(), kind=jnp.bfloat16):
    array = scale * jax.random.normal(own_key, dims, jnp.float32)
    if cuts:
        array = array * level_of(own_key, dims, cuts, -0.22, 0.18)
    return jnp.clip(array, -limit, limit).astype(kind)


def setup_inputs(seed: int = 0) -> dict:
    streams_of = jax.random.split(jax.random.key(seed), 10)
    features = centred(streams_of[0], (NODES, F), 1.0, 6.0, ((0, 32),))
    tile_cols = draw_tile_cols(jax.random.fold_in(streams_of[9], 71), 0)
    tile_masks = draw_tile_masks(jax.random.fold_in(streams_of[9], 71), 0)
    degree = place_ends(jax.random.randint(streams_of[3], (NODES,), 8, 33), jax.random.fold_in(streams_of[3], 1), 8, 32).astype(jnp.int32)
    owner_nodes = draw_owner_nodes(jax.random.fold_in(streams_of[9], 71), 0)
    owner_position = draw_owner_position(jax.random.fold_in(streams_of[9], 71), 0)
    self_weight = centred(streams_of[6], (F, F), F ** -0.5, 0.25)
    neigh_weight = centred(streams_of[7], (F, F), F ** -0.5, 0.25)
    cotangent = centred(streams_of[8], (NODES, F), 1.0, 6.0, ((0, 32),))
    return {"features": features, "tile_cols": tile_cols, "tile_masks": tile_masks, "degree": degree, "owner_nodes": owner_nodes, "owner_position": owner_position, "self_weight": self_weight, "neigh_weight": neigh_weight, "cotangent": cotangent}


def forward_cell(pattern, columns, column_rows):
    row_tiles = column_rows.reshape(-1, TILE, F)
    chosen = row_tiles[columns]
    result = jnp.einsum('tkij,tkjf->tif', pattern.astype(jnp.float32), chosen.astype(jnp.float32), precision=lax.Precision.HIGHEST)
    return result.reshape(-1, F)

def backward_cell(pattern, columns, spread_rows):
    pieces = jnp.einsum('tkij,tif->tkjf', pattern.astype(jnp.float32), spread_rows.reshape(-1, TILE, F).astype(jnp.float32), precision=lax.Precision.HIGHEST)
    totals = jnp.zeros((TCOLS, TILE, F), jnp.float32).at[columns.reshape(-1)].add(pieces.reshape(-1, TILE, F))
    return totals.reshape(-1, F)

def rounded(values):
    return lax.optimization_barrier(values.astype(jnp.bfloat16)).astype(jnp.float32)

def reference(features, tile_cols, tile_masks, degree, owner_nodes, owner_position, self_weight, neigh_weight, cotangent):
    node_feats = features[owner_position]
    grid_feats = node_feats.reshape(N_ROW, N_COL * ROWS_DEV, F)

    def forward_column(col_index):

        def add_row(totals, row_index):
            partial_value = forward_cell(tile_masks[row_index, col_index], tile_cols[row_index, col_index], grid_feats[row_index])
            return (totals + rounded(partial_value), None)
        start_zero = jnp.zeros((N_ROW * ROWS_DEV, F), jnp.float32)
        return lax.scan(add_row, start_zero, jnp.arange(N_ROW, dtype=jnp.int32))[0]
    by_column = lax.map(forward_column, jnp.arange(N_COL, dtype=jnp.int32))
    summed_node = by_column.reshape(N_COL, N_ROW, ROWS_DEV, F).transpose(1, 0, 2, 3).reshape(NODES, F)
    summed = summed_node[owner_nodes]
    degrees = degree.astype(jnp.float32)[:, None]
    aggregate = (summed / degrees).astype(jnp.bfloat16)
    preact = jnp.dot(features, self_weight, preferred_element_type=jnp.float32) + jnp.dot(aggregate, neigh_weight, preferred_element_type=jnp.float32)
    hidden = jax.nn.silu(preact).astype(jnp.bfloat16)
    gate_value = jax.nn.sigmoid(preact)
    slopes = (cotangent.astype(jnp.float32) * gate_value * (1.0 + preact * (1.0 - gate_value))).astype(jnp.bfloat16)
    grad_scale = 1.0 / math.sqrt(NODES)
    grad_self = jnp.dot(features.T, slopes, preferred_element_type=jnp.float32) * grad_scale
    grad_neigh = jnp.dot(aggregate.T, slopes, preferred_element_type=jnp.float32) * grad_scale
    own_back = jnp.dot(slopes, self_weight.T, preferred_element_type=jnp.float32)
    spread = (jnp.dot(slopes, neigh_weight.T, preferred_element_type=jnp.float32) / degrees).astype(jnp.bfloat16)
    grid_spread = spread[owner_position].reshape(N_ROW, N_COL, ROWS_DEV, F)

    def backward_row(row_index):

        def add_col(totals, col_index):
            partial_value = backward_cell(tile_masks[row_index, col_index], tile_cols[row_index, col_index], grid_spread[:, col_index].reshape(-1, F))
            return (totals + rounded(partial_value), None)
        start_zero = jnp.zeros((N_COL * ROWS_DEV, F), jnp.float32)
        return lax.scan(add_col, start_zero, jnp.arange(N_COL, dtype=jnp.int32))[0]
    neigh_node = lax.map(backward_row, jnp.arange(N_ROW, dtype=jnp.int32)).reshape(NODES, F)
    grad_features = (own_back + neigh_node[owner_nodes]).astype(jnp.bfloat16)
    return (hidden, grad_features, grad_self, grad_neigh)
```

```python
import functools
import math

import jax
import jax.numpy as jnp
from jax import lax
from jax.experimental import pallas as pl
from jax.experimental.pallas import tpu as pltpu
from jax.sharding import PartitionSpec as P

BF = jnp.bfloat16
F32 = jnp.float32
VMEM = pl.BlockSpec(memory_space=pltpu.VMEM)
LIMIT = 56 * 1024 * 1024


def params():
    return pltpu.CompilerParams(vmem_limit_bytes=LIMIT)


def cost(flops, nbytes):
    return pl.CostEstimate(flops=int(flops), bytes_accessed=int(nbytes), transcendentals=0)


def dot(a, b, ca=1, cb=0):
    return lax.dot_general(a, b, (((ca,), (cb,)), ((), ())), preferred_element_type=F32)


def as_column(row):
    return jnp.broadcast_to(row, (128, row.shape[1])).T


def block_of(index, size):
    if size & (size - 1) == 0:
        return lax.shift_right_logical(index, size.bit_length() - 1)
    return lax.div(index, jnp.full_like(index, size))


def rank_row(group_row, order_row):
    n = group_row.shape[1]
    group_col = as_column(group_row)[:, :1]
    order_col = as_column(order_row)[:, :1]
    earlier = (group_col == group_row) & (order_col < order_row)
    return jnp.sum(jnp.where(earlier, 1.0, 0.0), axis=0, keepdims=True).astype(jnp.int32)


def slots_onehot(flat_row, slots):
    iota = lax.broadcasted_iota(jnp.int32, (slots, flat_row.shape[1]), 0)
    return jnp.where(iota == flat_row, 1.0, 0.0).astype(BF)


def entries_onehot(flat_col, slots):
    iota = lax.broadcasted_iota(jnp.int32, (flat_col.shape[0], slots), 1)
    return jnp.where(flat_col[:, :1] == iota, 1.0, 0.0).astype(BF)


def own_slots(nodes_row, cap):
    n = nodes_row.shape[1]
    dest = block_of(nodes_row, n)
    rank = rank_row(dest, lax.broadcasted_iota(jnp.int32, (1, n), 1))
    return dest, rank


def pack_kernel(cap, nodes_ref, value_ref, out_ref):
    dest, rank = own_slots(nodes_ref[...], cap)
    out_ref[...] = dot(slots_onehot(dest * cap + rank, out_ref.shape[0]), value_ref[...]).astype(BF)


def index_kernel(cap, nodes_ref, position_ref, degree_ref, cot_ref, cot_out, degree_out, own_col, node_row, node_col):
    devices, _ = degree_out.shape
    n = nodes_ref.shape[1]
    dest, rank = own_slots(nodes_ref[...], cap)
    flat = dest * cap + rank
    own_col[...] = as_column(flat)
    cot_out[...] = dot(slots_onehot(flat, cot_out.shape[0]), cot_ref[...]).astype(BF)
    by_dest = jnp.where(lax.broadcasted_iota(jnp.int32, (devices, n), 0) == dest, degree_ref[...].astype(F32), 0.0)
    by_rank = entries_onehot(as_column(rank), cap)
    degree_out[...] = dot(by_dest.astype(BF), by_rank)
    position = position_ref[...]
    source = block_of(position, n)
    place = source * cap + rank_row(source, position)
    node_row[...] = jnp.broadcast_to(place, node_row.shape)
    node_col[...] = as_column(place)


def unpack_kernel(col_ref, value_ref, out_ref):
    out_ref[...] = dot(entries_onehot(col_ref[...], value_ref.shape[0]), value_ref[...]).astype(BF)


def spmm_kernel(ways, cols_ref, group_ref, x_ref, *refs):
    masks, outs = refs[:ways], refs[ways:]
    q = pl.program_id(0)
    depth = pl.num_programs(0)
    _, breadth, tile, _ = masks[0].shape
    for s in range(ways):
        base = (group_ref[s] * depth + q) * breadth
        total = None
        for p in range(0, breadth, 2):
            width = min(2, breadth - p)
            left = jnp.concatenate([masks[s][0, p + w] for w in range(width)], axis=1)
            right = jnp.concatenate(
                [x_ref[pl.ds(pl.multiple_of(cols_ref[base + p + w] * tile, tile), tile), :] for w in range(width)], axis=0
            )
            term = dot(left, right)
            total = term if total is None else total + term
        outs[s][...] = total.astype(BF)


def spmm_back_kernel(ways, cols_ref, group_ref, *refs):
    spreads, masks, out_ref, total = refs[:ways], refs[ways : 2 * ways], refs[2 * ways], refs[2 * ways + 1]
    q = pl.program_id(0)
    depth = pl.num_programs(0)
    _, breadth, tile, _ = masks[0].shape

    @pl.when(q == 0)
    def _():
        total[...] = jnp.zeros_like(total)

    for s in range(ways):
        base = (group_ref[s] * depth + q) * breadth
        rows = spreads[s][...]
        for k in range(breadth):
            at = pl.ds(pl.multiple_of(cols_ref[base + k] * tile, tile), tile)
            total[at, :] += dot(masks[s][0, k], rows, 0, 0)

    @pl.when(q == depth - 1)
    def _():
        out_ref[...] = total[...].astype(BF)


def layer_kernel(ways, *refs):
    terms = refs[:ways]
    (x_ref, cot_ref, degree_ref, col_ref, self_ref, neigh_ref, hidden_out, slopes_out, agg_out, spread_out) = refs[ways:]
    devices, cap = degree_ref.shape
    slots = cot_ref.shape[0]
    place = col_ref[...][:, :1]
    rows = place.shape[0]
    summed = terms[0][...].astype(F32)
    for s in range(1, ways):
        summed = summed + terms[s][...].astype(F32)
    source = block_of(place, cap)
    rank = place - source * cap
    by_source = entries_onehot(source, devices)
    degrees = dot(by_source, degree_ref[...].astype(BF))
    picked = lax.broadcasted_iota(jnp.int32, (rows, cap), 1) == rank
    degrees = jnp.sum(jnp.where(picked, degrees, 0.0), axis=1, keepdims=True)
    agg = (summed / degrees).astype(BF)
    agg_out[...] = agg
    preact = dot(x_ref[...], self_ref[...]) + dot(agg, neigh_ref[...])
    gate = jax.nn.sigmoid(preact)
    hidden_out[...] = (preact * gate).astype(BF)
    cot = dot(entries_onehot(place, slots), cot_ref[...])
    slopes = (cot * gate * (1.0 + preact * (1.0 - gate))).astype(BF)
    slopes_out[...] = slopes
    spread_out[...] = (dot(slopes, neigh_ref[...], 1, 1) / degrees).astype(BF)


def terms_kernel(x_ref, agg_ref, slopes_ref, hidden_ref, self_ref, row_ref, grads_out, back_out, packed_out):
    width = x_ref.shape[1]
    slopes = slopes_ref[...]
    packed_out[...] = dot(slots_onehot(row_ref[...][:1], packed_out.shape[0]), hidden_ref[...]).astype(BF)
    grads_out[:width, :] = dot(x_ref[...], slopes, 0, 0).astype(BF)
    grads_out[width:, :] = dot(agg_ref[...], slopes, 0, 0).astype(BF)
    back_out[...] = dot(slopes, self_ref[...], 1, 1)


def join_kernel(own_ref, neigh_ref, row_ref, out_ref):
    joined = (own_ref[...] + neigh_ref[...].astype(F32)).astype(BF)
    out_ref[...] = dot(slots_onehot(row_ref[...][:1], out_ref.shape[0]), joined).astype(BF)


def on_device(
    features,
    tile_cols,
    tile_masks,
    degree,
    owner_nodes,
    owner_position,
    self_weight,
    neigh_weight,
    cotangent,
):
    rows, width = features.shape
    row_devices = lax.axis_size("row")
    col_devices = lax.axis_size("col")
    devices = row_devices * col_devices
    cap = 2 * rows // devices
    slots = devices * cap
    masks = tile_masks[0, 0]
    tile = masks.shape[-1]
    breadth = masks.shape[1]
    depth = rows // tile
    cols = tile_cols[0, 0].reshape(-1)
    me = lax.axis_index("row")
    ways = row_devices
    groups = jnp.bitwise_xor(me, jnp.arange(ways, dtype=jnp.int32)).astype(jnp.int32)
    everyone = ("row", "col")
    call = functools.partial(pl.pallas_call, compiler_params=params())

    def shape(r, c, dtype=BF):
        return jax.ShapeDtypeStruct((r, c), dtype)

    def relay(packed):
        there = packed.reshape(devices, cap, -1)
        return lax.all_to_all(there, everyone, split_axis=0, concat_axis=0, tiled=True).reshape(slots, -1)

    def across(value, s):
        return lax.ppermute(value, "row", [(i, i ^ s) for i in range(ways)])

    nodes = owner_nodes.reshape(1, rows)
    slab = rows * width
    packed = call(
        functools.partial(pack_kernel, cap),
        out_shape=shape(slots, width),
        in_specs=[VMEM] * 2,
        out_specs=VMEM,
        cost_estimate=cost(2 * slots * slab, 6 * slab),
        name="pack_features",
    )(nodes, features)
    inbound = relay(packed)
    cot_packed, degree_packed, own_col, node_row, node_col = call(
        functools.partial(index_kernel, cap),
        out_shape=(
            shape(slots, width),
            shape(devices, cap, F32),
            shape(rows, 128, jnp.int32),
            shape(8, rows, jnp.int32),
            shape(rows, 128, jnp.int32),
        ),
        in_specs=[VMEM] * 4,
        out_specs=(VMEM,) * 5,
        cost_estimate=cost(2 * slots * slab, 6 * slab),
        name="index_cotangent",
    )(nodes, owner_position.reshape(1, rows), degree.reshape(1, rows), cotangent)
    degree_in = lax.all_to_all(degree_packed, everyone, split_axis=0, concat_axis=0, tiled=True)
    cot_in = relay(cot_packed)
    x_node = call(
        unpack_kernel,
        out_shape=shape(rows, width),
        in_specs=[VMEM] * 2,
        out_specs=VMEM,
        cost_estimate=cost(2 * slots * slab, 6 * slab),
        name="unpack_features",
    )(node_col, inbound)
    x_cols = lax.all_gather(x_node, "col", axis=0, tiled=True)

    def mask_spec(s):
        return pl.BlockSpec((1, breadth, tile, tile), lambda q, c, g, s=s: (g[s] * depth + q, 0, 0, 0))

    spmm_flops = 2 * masks.size * width
    partials = call(
        functools.partial(spmm_kernel, ways),
        grid_spec=pltpu.PrefetchScalarGridSpec(
            num_scalar_prefetch=2,
            grid=(depth,),
            in_specs=[VMEM] + [mask_spec(s) for s in range(ways)],
            out_specs=[pl.BlockSpec((tile, width), lambda q, c, g: (q, 0)) for s in range(ways)],
        ),
        out_shape=[shape(rows, width) for s in range(ways)],
        cost_estimate=cost(spmm_flops, 2 * masks.size + 2 * x_cols.size + 2 * ways * slab),
        name="spmm",
    )(cols, groups, x_cols, *([masks] * ways))
    terms = [partials[0]] + [across(partials[s], s) for s in range(1, ways)]
    row_block = rows // 2

    def by_rows(c):
        return pl.BlockSpec((row_block, c), lambda i: (i, 0))

    hidden, slopes, agg, spread = call(
        functools.partial(layer_kernel, ways),
        grid=(2,),
        out_shape=(shape(rows, width),) * 4,
        in_specs=[by_rows(width)] * (ways + 1) + [VMEM] * 2 + [by_rows(128)] + [VMEM] * 2,
        out_specs=(by_rows(width),) * 4,
        cost_estimate=cost(10 * slab * width, 2 * slab * (ways + 9)),
        name="layer",
    )(*terms, x_node, cot_in, degree_in, node_col, self_weight, neigh_weight)
    spreads = [spread] + [across(spread, s) for s in range(1, ways)]
    grads, own_back, hidden_packed = call(
        terms_kernel,
        out_shape=(shape(2 * width, width), shape(rows, width, F32), shape(slots, width)),
        in_specs=[VMEM] * 6,
        out_specs=(VMEM,) * 3,
        cost_estimate=cost(10 * slab * width, 2 * slab * 11),
        name="terms",
    )(x_node, agg, slopes, hidden, self_weight, node_row)
    hidden_in = relay(hidden_packed)
    back = call(
        functools.partial(spmm_back_kernel, ways),
        grid_spec=pltpu.PrefetchScalarGridSpec(
            num_scalar_prefetch=2,
            grid=(depth,),
            in_specs=[pl.BlockSpec((tile, width), lambda q, c, g: (q, 0)) for s in range(ways)]
            + [mask_spec(s) for s in range(ways)],
            out_specs=VMEM,
            scratch_shapes=[pltpu.VMEM(x_cols.shape, F32)],
        ),
        out_shape=shape(*x_cols.shape),
        cost_estimate=cost(spmm_flops, 2 * masks.size + 2 * x_cols.size + 2 * ways * slab),
        name="spmm_back",
    )(cols, groups, *spreads, *([masks] * ways))
    neigh_back = lax.psum_scatter(back, "col", scatter_dimension=0, tiled=True)
    grad_packed = call(
        join_kernel,
        out_shape=shape(slots, width),
        in_specs=[VMEM] * 3,
        out_specs=VMEM,
        cost_estimate=cost(2 * slots * slab, 8 * slab),
        name="join_pack",
    )(own_back, neigh_back, node_row)
    grad_in = relay(grad_packed)

    def unpack_own(value):
        return call(
            unpack_kernel,
            out_shape=shape(rows, width),
            in_specs=[VMEM] * 2,
            out_specs=VMEM,
            cost_estimate=cost(2 * slots * slab, 6 * slab),
            name="unpack_owner",
        )(own_col, value)

    hidden_own = unpack_own(hidden_in)
    grad_own = unpack_own(grad_in)

    parts = grads.reshape(ways, -1, width)
    kept = lax.dynamic_index_in_dim(parts, me, 0, keepdims=False).astype(F32)
    for s in range(1, ways):
        kept = kept + across(lax.dynamic_index_in_dim(parts, groups[s], 0, keepdims=False), s).astype(F32)
    pieces = kept.astype(BF).reshape(col_devices, -1, width)
    pieces = lax.all_to_all(pieces, "col", split_axis=0, concat_axis=0, tiled=True)
    scale = 1.0 / math.sqrt(rows * devices)
    mine = (jnp.sum(pieces.astype(F32), axis=0) * scale).astype(BF)
    whole = lax.all_gather(mine, ("row", "col"), axis=0, tiled=True).astype(F32)
    return (hidden_own, grad_own, whole[:width], whole[width:])


def solution(mesh):
    placed = (
        P(("row", "col"), None),
        P("row", "col", None, None),
        P("row", "col", None, None, None, None),
        P(("row", "col")),
        P(("row", "col")),
        P(("row", "col")),
        P(),
        P(),
        P(("row", "col"), None),
    )
    return jax.shard_map(
        on_device,
        mesh=mesh,
        in_specs=placed,
        out_specs=(P(("row", "col"), None), P(("row", "col"), None), P(), P()),
        check_vma=False,
    )
```

```python
import functools
import math

import jax
import jax.numpy as jnp
from jax import lax
from jax.experimental import pallas as pl
from jax.experimental.pallas import tpu as pltpu
from jax.sharding import PartitionSpec as P

BF = jnp.bfloat16
F32 = jnp.float32
VMEM = pl.BlockSpec(memory_space=pltpu.VMEM)
LIMIT = 56 * 1024 * 1024


def params():
    return pltpu.CompilerParams(vmem_limit_bytes=LIMIT)


def cost(flops, nbytes):
    return pl.CostEstimate(flops=int(flops), bytes_accessed=int(nbytes), transcendentals=0)


def dot(a, b, ca=1, cb=0):
    return lax.dot_general(a, b, (((ca,), (cb,)), ((), ())), preferred_element_type=F32)


def as_column(row):
    return jnp.broadcast_to(row, (128, row.shape[1])).T


def block_of(index, size):
    if size & (size - 1) == 0:
        return lax.shift_right_logical(index, size.bit_length() - 1)
    return lax.div(index, jnp.full_like(index, size))


def rank_row(group_row, order_row):
    n = group_row.shape[1]
    group_col = as_column(group_row)[:, :1]
    order_col = as_column(order_row)[:, :1]
    earlier = (group_col == group_row) & (order_col < order_row)
    return jnp.sum(jnp.where(earlier, 1.0, 0.0), axis=0, keepdims=True).astype(jnp.int32)


def slots_onehot(flat_row, slots):
    iota = lax.broadcasted_iota(jnp.int32, (slots, flat_row.shape[1]), 0)
    return jnp.where(iota == flat_row, 1.0, 0.0).astype(BF)


def entries_onehot(flat_col, slots):
    iota = lax.broadcasted_iota(jnp.int32, (flat_col.shape[0], slots), 1)
    return jnp.where(flat_col[:, :1] == iota, 1.0, 0.0).astype(BF)


def own_slots(nodes_row, cap):
    n = nodes_row.shape[1]
    dest = block_of(nodes_row, n)
    rank = rank_row(dest, lax.broadcasted_iota(jnp.int32, (1, n), 1))
    return dest, rank


def pack_kernel(cap, nodes_ref, value_ref, out_ref):
    dest, rank = own_slots(nodes_ref[...], cap)
    out_ref[...] = dot(slots_onehot(dest * cap + rank, out_ref.shape[0]), value_ref[...]).astype(BF)


def index_kernel(cap, nodes_ref, position_ref, degree_ref, cot_ref, cot_out, own_col, node_row, node_col):
    n = nodes_ref.shape[1]
    width = cot_ref.shape[1]
    dest, rank = own_slots(nodes_ref[...], cap)
    flat = dest * cap + rank
    own_col[...] = as_column(flat)
    packing = slots_onehot(flat, cot_out.shape[0])
    cot_out[:, :width] = dot(packing, cot_ref[...]).astype(BF)
    cot_out[:, width:] = dot(packing, as_column(degree_ref[...].astype(F32)).astype(BF)).astype(BF)
    position = position_ref[...]
    source = block_of(position, n)
    place = source * cap + rank_row(source, position)
    node_row[...] = jnp.broadcast_to(place, node_row.shape)
    node_col[...] = as_column(place)


def unpack_kernel(col_ref, value_ref, out_ref):
    out_ref[...] = dot(entries_onehot(col_ref[...], value_ref.shape[0]), value_ref[...]).astype(BF)


def spmm_kernel(way, cols_ref, group_ref, x_ref, masks_ref, out_ref):
    q = pl.program_id(0)
    depth = pl.num_programs(0)
    _, breadth, tile, _ = masks_ref.shape
    base = (group_ref[way] * depth + q) * breadth
    total = None
    for p in range(0, breadth, 2):
        width = min(2, breadth - p)
        left = jnp.concatenate([masks_ref[0, p + w] for w in range(width)], axis=1)
        right = jnp.concatenate(
            [x_ref[pl.ds(pl.multiple_of(cols_ref[base + p + w] * tile, tile), tile), :] for w in range(width)], axis=0
        )
        term = dot(left, right)
        total = term if total is None else total + term
    out_ref[...] = total.astype(BF)


def spmm_back_kernel(ways, cols_ref, group_ref, *refs):
    spreads, masks, out_ref, total = refs[:ways], refs[ways : 2 * ways], refs[2 * ways], refs[2 * ways + 1]
    q = pl.program_id(0)
    depth = pl.num_programs(0)
    _, breadth, tile, _ = masks[0].shape

    @pl.when(q == 0)
    def _():
        total[...] = jnp.zeros_like(total)

    for s in range(ways):
        base = (group_ref[s] * depth + q) * breadth
        rows = spreads[s][...]
        for k in range(breadth):
            at = pl.ds(pl.multiple_of(cols_ref[base + k] * tile, tile), tile)
            total[at, :] += dot(masks[s][0, k], rows, 0, 0)

    @pl.when(q == depth - 1)
    def _():
        out_ref[...] = total[...].astype(BF)


def layer_kernel(ways, *refs):
    terms = refs[:ways]
    (x_ref, cot_ref, col_ref, self_ref, neigh_ref, hidden_out, slopes_out, agg_out, spread_out) = refs[ways:]
    width = x_ref.shape[1]
    summed = terms[0][...].astype(F32)
    for s in range(1, ways):
        summed = summed + terms[s][...].astype(F32)
    cot = dot(entries_onehot(col_ref[...], cot_ref.shape[0]), cot_ref[...])
    degrees = cot[:, width : width + 1]
    agg = (summed / degrees).astype(BF)
    agg_out[...] = agg
    preact = dot(x_ref[...], self_ref[...]) + dot(agg, neigh_ref[...])
    gate = jax.nn.sigmoid(preact)
    hidden_out[...] = (preact * gate).astype(BF)
    slopes = (cot[:, :width] * gate * (1.0 + preact * (1.0 - gate))).astype(BF)
    slopes_out[...] = slopes
    spread_out[...] = (dot(slopes, neigh_ref[...], 1, 1) / degrees).astype(BF)


def terms_kernel(x_ref, agg_ref, slopes_ref, hidden_ref, self_ref, row_ref, grads_out, back_out, packed_out):
    width = x_ref.shape[1]
    slopes = slopes_ref[...]
    packed_out[...] = dot(slots_onehot(row_ref[...][:1], packed_out.shape[0]), hidden_ref[...]).astype(BF)
    grads_out[:width, :] = dot(x_ref[...], slopes, 0, 0).astype(BF)
    grads_out[width:, :] = dot(agg_ref[...], slopes, 0, 0).astype(BF)
    back_out[...] = dot(slopes, self_ref[...], 1, 1)


def join_kernel(own_ref, neigh_ref, row_ref, out_ref):
    joined = (own_ref[...] + neigh_ref[...].astype(F32)).astype(BF)
    out_ref[...] = dot(slots_onehot(row_ref[...][:1], out_ref.shape[0]), joined).astype(BF)


def on_device(
    features,
    tile_cols,
    tile_masks,
    degree,
    owner_nodes,
    owner_position,
    self_weight,
    neigh_weight,
    cotangent,
):
    rows, width = features.shape
    row_devices = lax.axis_size("row")
    col_devices = lax.axis_size("col")
    devices = row_devices * col_devices
    cap = 2 * rows // devices
    slots = devices * cap
    masks = tile_masks[0, 0]
    tile = masks.shape[-1]
    breadth = masks.shape[1]
    depth = rows // tile
    cols = tile_cols[0, 0].reshape(-1)
    me = lax.axis_index("row")
    ways = row_devices
    groups = jnp.bitwise_xor(me, jnp.arange(ways, dtype=jnp.int32)).astype(jnp.int32)
    everyone = ("row", "col")
    call = functools.partial(pl.pallas_call, compiler_params=params())

    def shape(r, c, dtype=BF):
        return jax.ShapeDtypeStruct((r, c), dtype)

    def relay(packed):
        there = packed.reshape(devices, cap, -1)
        return lax.all_to_all(there, everyone, split_axis=0, concat_axis=0, tiled=True).reshape(slots, -1)

    def across(value, s):
        return lax.ppermute(value, "row", [(i, i ^ s) for i in range(ways)])

    nodes = owner_nodes.reshape(1, rows)
    slab = rows * width
    packed = call(
        functools.partial(pack_kernel, cap),
        out_shape=shape(slots, width),
        in_specs=[VMEM] * 2,
        out_specs=VMEM,
        cost_estimate=cost(2 * slots * slab, 6 * slab),
        name="pack_features",
    )(nodes, features)
    inbound = relay(packed)
    cot_packed, own_col, node_row, node_col = call(
        functools.partial(index_kernel, cap),
        out_shape=(
            shape(slots, width + 128),
            shape(rows, 128, jnp.int32),
            shape(8, rows, jnp.int32),
            shape(rows, 128, jnp.int32),
        ),
        in_specs=[VMEM] * 4,
        out_specs=(VMEM,) * 4,
        cost_estimate=cost(2 * slots * slab, 6 * slab),
        name="index_cotangent",
    )(nodes, owner_position.reshape(1, rows), degree.reshape(1, rows), cotangent)
    x_node = call(
        unpack_kernel,
        out_shape=shape(rows, width),
        in_specs=[VMEM] * 2,
        out_specs=VMEM,
        cost_estimate=cost(2 * slots * slab, 6 * slab),
        name="unpack_features",
    )(node_col, inbound)
    x_cols = lax.all_gather(x_node, "col", axis=0, tiled=True)
    x_cols, cot_packed = lax.optimization_barrier((x_cols, cot_packed))
    cot_in = relay(cot_packed)

    def mask_spec(s):
        return pl.BlockSpec((1, breadth, tile, tile), lambda q, c, g, s=s: (g[s] * depth + q, 0, 0, 0))

    spmm_flops = 2 * masks.size * width
    def spmm(way):
        partial = call(
            functools.partial(spmm_kernel, way),
            grid_spec=pltpu.PrefetchScalarGridSpec(
                num_scalar_prefetch=2,
                grid=(depth,),
                in_specs=[VMEM, mask_spec(way)],
                out_specs=pl.BlockSpec((tile, width), lambda q, c, g: (q, 0)),
            ),
            out_shape=shape(rows, width),
            cost_estimate=cost(spmm_flops // ways, 2 * masks.size // ways + 2 * x_cols.size + 2 * slab),
            name="spmm_%d" % way,
        )(cols, groups, x_cols, masks)
        return across(partial, way) if way else partial

    terms = [spmm(way) for way in range(ways - 1, -1, -1)]
    row_block = rows // 2

    def by_rows(c):
        return pl.BlockSpec((row_block, c), lambda i: (i, 0))

    hidden, slopes, agg, spread = call(
        functools.partial(layer_kernel, ways),
        grid=(2,),
        out_shape=(shape(rows, width),) * 4,
        in_specs=[by_rows(width)] * (ways + 1) + [VMEM, by_rows(128)] + [VMEM] * 2,
        out_specs=(by_rows(width),) * 4,
        cost_estimate=cost(10 * slab * width, 2 * slab * (ways + 9)),
        name="layer",
    )(*terms, x_node, cot_in, node_col, self_weight, neigh_weight)
    grads, own_back, hidden_packed = call(
        terms_kernel,
        out_shape=(shape(2 * width, width), shape(rows, width, F32), shape(slots, width)),
        in_specs=[VMEM] * 6,
        out_specs=(VMEM,) * 3,
        cost_estimate=cost(10 * slab * width, 2 * slab * 11),
        name="terms",
    )(x_node, agg, slopes, hidden, self_weight, node_row)
    hidden_in = relay(hidden_packed)
    spreads = [spread] + [across(spread, s) for s in range(1, ways)]
    *spreads, own_back = lax.optimization_barrier((*spreads, own_back))
    back = call(
        functools.partial(spmm_back_kernel, ways),
        grid_spec=pltpu.PrefetchScalarGridSpec(
            num_scalar_prefetch=2,
            grid=(depth,),
            in_specs=[pl.BlockSpec((tile, width), lambda q, c, g: (q, 0)) for s in range(ways)]
            + [mask_spec(s) for s in range(ways)],
            out_specs=VMEM,
            scratch_shapes=[pltpu.VMEM(x_cols.shape, F32)],
        ),
        out_shape=shape(*x_cols.shape),
        cost_estimate=cost(spmm_flops, 2 * masks.size + 2 * x_cols.size + 2 * ways * slab),
        name="spmm_back",
    )(cols, groups, *spreads, *([masks] * ways))
    back, grads, hidden_in = lax.optimization_barrier((back, grads, hidden_in))
    neigh_back = lax.psum_scatter(back, "col", scatter_dimension=0, tiled=True)
    grad_packed = call(
        join_kernel,
        out_shape=shape(slots, width),
        in_specs=[VMEM] * 3,
        out_specs=VMEM,
        cost_estimate=cost(2 * slots * slab, 8 * slab),
        name="join_pack",
    )(own_back, neigh_back, node_row)
    grad_in = relay(grad_packed)

    def unpack_own(value):
        return call(
            unpack_kernel,
            out_shape=shape(rows, width),
            in_specs=[VMEM] * 2,
            out_specs=VMEM,
            cost_estimate=cost(2 * slots * slab, 6 * slab),
            name="unpack_owner",
        )(own_col, value)

    hidden_own = unpack_own(hidden_in)
    grad_own = unpack_own(grad_in)

    place = lax.axis_index("col")
    others = jnp.bitwise_xor(place, jnp.arange(col_devices, dtype=jnp.int32)).astype(jnp.int32)

    def along(value, s):
        return lax.ppermute(value, "col", [(i, i ^ s) for i in range(col_devices)])

    def pick(value, at):
        return lax.dynamic_index_in_dim(value, at, 0, keepdims=False)

    parts = grads.reshape(ways, -1, width)
    kept = [pick(parts, me)] + [across(pick(parts, groups[s]), s) for s in range(1, ways)]
    kept = sum(term.astype(F32) for term in kept)
    pieces = kept.astype(BF).reshape(col_devices, -1, width)
    mine = [pick(pieces, place)] + [along(pick(pieces, others[s]), s) for s in range(1, col_devices)]
    scale = 1.0 / math.sqrt(rows * devices)
    mine = (sum(term.astype(F32) for term in mine) * scale).astype(BF)
    in_row = jnp.stack([mine] + [along(mine, s) for s in range(1, col_devices)])[others].reshape(-1, width)
    whole = jnp.stack([in_row] + [across(in_row, s) for s in range(1, ways)])[groups].reshape(-1, width).astype(F32)
    return (hidden_own, grad_own, whole[:width], whole[width:])


def solution(mesh):
    placed = (
        P(("row", "col"), None),
        P("row", "col", None, None),
        P("row", "col", None, None, None, None),
        P(("row", "col")),
        P(("row", "col")),
        P(("row", "col")),
        P(),
        P(),
        P(("row", "col"), None),
    )
    return jax.shard_map(
        on_device,
        mesh=mesh,
        in_specs=placed,
        out_specs=(P(("row", "col"), None), P(("row", "col"), None), P(), P()),
        check_vma=False,
    )
```

```python
import functools
import math

import jax
import jax.numpy as jnp
from jax import lax
from jax.experimental import pallas as pl
from jax.experimental.pallas import tpu as pltpu
from jax.sharding import PartitionSpec as P

BF = jnp.bfloat16
F32 = jnp.float32
VMEM = pl.BlockSpec(memory_space=pltpu.VMEM)
LIMIT = 56 * 1024 * 1024


def params():
    return pltpu.CompilerParams(vmem_limit_bytes=LIMIT)


def cost(flops, nbytes):
    return pl.CostEstimate(flops=int(flops), bytes_accessed=int(nbytes), transcendentals=0)


def dot(a, b, ca=1, cb=0):
    return lax.dot_general(a, b, (((ca,), (cb,)), ((), ())), preferred_element_type=F32)


def as_column(row):
    return jnp.broadcast_to(row, (128, row.shape[1])).T


def block_of(index, size):
    if size & (size - 1) == 0:
        return lax.shift_right_logical(index, size.bit_length() - 1)
    return lax.div(index, jnp.full_like(index, size))


def rank_row(group_row, order_row):
    n = group_row.shape[1]
    group_col = as_column(group_row)[:, :1]
    order_col = as_column(order_row)[:, :1]
    earlier = (group_col == group_row) & (order_col < order_row)
    return jnp.sum(jnp.where(earlier, 1.0, 0.0), axis=0, keepdims=True).astype(jnp.int32)


def slots_onehot(flat_row, slots):
    iota = lax.broadcasted_iota(jnp.int32, (slots, flat_row.shape[1]), 0)
    return jnp.where(iota == flat_row, 1.0, 0.0).astype(BF)


def entries_onehot(flat_col, slots):
    iota = lax.broadcasted_iota(jnp.int32, (flat_col.shape[0], slots), 1)
    return jnp.where(flat_col[:, :1] == iota, 1.0, 0.0).astype(BF)


def own_slots(nodes_row, cap):
    n = nodes_row.shape[1]
    dest = block_of(nodes_row, n)
    rank = rank_row(dest, lax.broadcasted_iota(jnp.int32, (1, n), 1))
    return dest, rank


def pack_kernel(cap, nodes_ref, value_ref, out_ref):
    dest, rank = own_slots(nodes_ref[...], cap)
    out_ref[...] = dot(slots_onehot(dest * cap + rank, out_ref.shape[0]), value_ref[...]).astype(BF)


def index_kernel(
    cap, ways, nodes_ref, position_ref, degree_ref, cot_ref, cot_out, own_col, node_row, node_col, turned_row, turned_col
):
    n = nodes_ref.shape[1]
    width = cot_ref.shape[1]
    dest, rank = own_slots(nodes_ref[...], cap)
    flat = dest * cap + rank
    own_col[...] = as_column(flat)
    packing = slots_onehot(flat, cot_out.shape[0])
    cot_out[:, :width] = dot(packing, cot_ref[...]).astype(BF)
    cot_out[:, width:] = dot(packing, as_column(degree_ref[...].astype(F32)).astype(BF)).astype(BF)
    position = position_ref[...]
    source = block_of(position, n)
    rank = rank_row(source, position)
    place = source * cap + rank
    node_row[...] = jnp.broadcast_to(place, node_row.shape)
    node_col[...] = as_column(place)
    across = cot_out.shape[0] // (cap * ways)
    down = block_of(source, across)
    turned = ((source - down * across) * ways + down) * cap + rank
    turned_row[...] = jnp.broadcast_to(turned, turned_row.shape)
    turned_col[...] = as_column(turned)


def unpack_kernel(col_ref, value_ref, out_ref):
    out_ref[...] = dot(entries_onehot(col_ref[...], value_ref.shape[0]), value_ref[...]).astype(BF)


def spmm_kernel(ways, cols_ref, group_ref, x_hbm, *refs):
    masks, outs = refs[:ways], refs[ways : 2 * ways]
    x_ref, sems = refs[2 * ways :]
    q = pl.program_id(0)
    depth = pl.num_programs(0)
    _, breadth, tile, _ = masks[0].shape

    @pl.when(q == 0)
    def _():
        count = sems.shape[0]
        share = x_ref.shape[0] // count
        copies = [
            pltpu.make_async_copy(x_hbm.at[pl.ds(i * share, share)], x_ref.at[pl.ds(i * share, share)], sems.at[i])
            for i in range(count)
        ]
        for copy in copies:
            copy.start()
        for copy in copies:
            copy.wait()

    for s in range(ways):
        base = (group_ref[s] * depth + q) * breadth
        total = None
        for p in range(0, breadth, 2):
            width = min(2, breadth - p)
            left = jnp.concatenate([masks[s][0, p + w] for w in range(width)], axis=1)
            right = jnp.concatenate(
                [x_ref[pl.ds(pl.multiple_of(cols_ref[base + p + w] * tile, tile), tile), :] for w in range(width)], axis=0
            )
            term = dot(left, right)
            total = term if total is None else total + term
        outs[s][...] = total.astype(BF)


def spmm_back_kernel(ways, cols_ref, group_ref, *refs):
    spreads, masks, out_ref, total = refs[:ways], refs[ways : 2 * ways], refs[2 * ways], refs[2 * ways + 1]
    q = pl.program_id(0)
    depth = pl.num_programs(0)
    _, breadth, tile, _ = masks[0].shape

    @pl.when(q == 0)
    def _():
        total[...] = jnp.zeros_like(total)

    for s in range(ways):
        base = (group_ref[s] * depth + q) * breadth
        rows = spreads[s][...]
        for k in range(breadth):
            at = pl.ds(pl.multiple_of(cols_ref[base + k] * tile, tile), tile)
            total[at, :] += dot(masks[s][0, k], rows, 0, 0)

    @pl.when(q == depth - 1)
    def _():
        out_ref[...] = total[...].astype(BF)


def layer_kernel(ways, *refs):
    terms = refs[:ways]
    (x_ref, cot_ref, col_ref, row_ref, self_ref, neigh_ref, packed_out, slopes_out, agg_out, spread_out) = refs[ways:]
    width = x_ref.shape[1]
    summed = terms[0][...].astype(F32)
    for s in range(1, ways):
        summed = summed + terms[s][...].astype(F32)
    cot = dot(entries_onehot(col_ref[...], cot_ref.shape[0]), cot_ref[...])
    degrees = cot[:, width : width + 1]
    agg = (summed / degrees).astype(BF)
    agg_out[...] = agg
    preact = dot(x_ref[...], self_ref[...]) + dot(agg, neigh_ref[...])
    gate = jax.nn.sigmoid(preact)
    hidden = (preact * gate).astype(BF)
    slopes = (cot[:, :width] * gate * (1.0 + preact * (1.0 - gate))).astype(BF)
    slopes_out[...] = slopes
    spread_out[...] = (dot(slopes, neigh_ref[...], 1, 1) / degrees).astype(BF)
    packed_out[...] = dot(slots_onehot(row_ref[...][:1], packed_out.shape[0]), hidden).astype(BF)


def terms_kernel(x_ref, agg_ref, slopes_ref, self_ref, grads_out, back_out):
    width = x_ref.shape[1]
    slopes = slopes_ref[...]
    grads_out[:width, :] = dot(x_ref[...], slopes, 0, 0).astype(BF)
    grads_out[width:, :] = dot(agg_ref[...], slopes, 0, 0).astype(BF)
    back_out[...] = dot(slopes, self_ref[...], 1, 1)


def place_kernel(index_ref, *refs):
    out_ref = refs[-1]
    for s, part in enumerate(refs[:-1]):
        out_ref[index_ref[s]] = part[...].astype(out_ref.dtype)


def join_kernel(own_ref, neigh_ref, row_ref, out_ref):
    joined = (own_ref[...] + neigh_ref[...].astype(F32)).astype(BF)
    out_ref[...] = dot(slots_onehot(row_ref[...][:1], out_ref.shape[0]), joined).astype(BF)


def on_device(
    features,
    tile_cols,
    tile_masks,
    degree,
    owner_nodes,
    owner_position,
    self_weight,
    neigh_weight,
    cotangent,
):
    rows, width = features.shape
    row_devices = lax.axis_size("row")
    col_devices = lax.axis_size("col")
    devices = row_devices * col_devices
    cap = 2 * rows // devices
    slots = devices * cap
    masks = tile_masks[0, 0]
    tile = masks.shape[-1]
    breadth = masks.shape[1]
    depth = rows // tile
    cols = tile_cols[0, 0].reshape(-1)
    me = lax.axis_index("row")
    ways = row_devices
    groups = jnp.bitwise_xor(me, jnp.arange(ways, dtype=jnp.int32)).astype(jnp.int32)
    everyone = ("row", "col")
    call = functools.partial(pl.pallas_call, compiler_params=params())

    def shape(r, c, dtype=BF):
        return jax.ShapeDtypeStruct((r, c), dtype)

    def relay(packed):
        there = packed.reshape(devices, cap, -1)
        return lax.all_to_all(there, everyone, split_axis=0, concat_axis=0, tiled=True).reshape(slots, -1)

    def row_phase(packed):
        there = packed.reshape(row_devices, col_devices * cap, -1)
        return lax.all_to_all(there, "row", split_axis=0, concat_axis=0, tiled=True).reshape(slots, -1)

    def col_phase(packed):
        there = packed.reshape(col_devices, row_devices * cap, -1)
        return lax.all_to_all(there, "col", split_axis=0, concat_axis=0, tiled=True).reshape(slots, -1)

    def turn(packed, first, second):
        return packed.reshape(first, second, cap, -1).transpose(1, 0, 2, 3).reshape(slots, -1)

    def across(value, s):
        return lax.ppermute(value, "row", [(i, i ^ s) for i in range(ways)])

    nodes = owner_nodes.reshape(1, rows)
    slab = rows * width
    packed = call(
        functools.partial(pack_kernel, cap),
        out_shape=shape(slots, width),
        in_specs=[VMEM] * 2,
        out_specs=VMEM,
        cost_estimate=cost(2 * slots * slab, 6 * slab),
        name="pack_features",
    )(nodes, features)
    inbound = relay(packed)
    cot_packed, own_col, node_row, node_col, turned_row, turned_col = call(
        functools.partial(index_kernel, cap, ways),
        out_shape=(
            shape(slots, width + 128),
            shape(rows, 128, jnp.int32),
            shape(8, rows, jnp.int32),
            shape(rows, 128, jnp.int32),
            shape(8, rows, jnp.int32),
            shape(rows, 128, jnp.int32),
        ),
        in_specs=[VMEM] * 4,
        out_specs=(VMEM,) * 6,
        cost_estimate=cost(2 * slots * slab, 6 * slab),
        name="index_cotangent",
    )(nodes, owner_position.reshape(1, rows), degree.reshape(1, rows), cotangent)
    x_node = call(
        unpack_kernel,
        out_shape=shape(rows, width),
        in_specs=[VMEM] * 2,
        out_specs=VMEM,
        cost_estimate=cost(2 * slots * slab, 6 * slab),
        name="unpack_features",
    )(node_col, inbound)
    cot_packed, x_node, cols, groups = lax.optimization_barrier((cot_packed, x_node, cols, groups))
    x_cols = lax.all_gather(x_node, "col", axis=0, tiled=True)
    cot_mid = turn(row_phase(cot_packed), row_devices, col_devices)
    x_cols, cot_mid = lax.optimization_barrier((x_cols, cot_mid))
    cot_in = col_phase(cot_mid)

    def mask_spec(s):
        return pl.BlockSpec((1, breadth, tile, tile), lambda q, c, g, s=s: (g[s] * depth + q, 0, 0, 0))

    spmm_flops = 2 * masks.size * width
    copies = 8
    partials = call(
        functools.partial(spmm_kernel, ways),
        grid_spec=pltpu.PrefetchScalarGridSpec(
            num_scalar_prefetch=2,
            grid=(depth,),
            in_specs=[pl.BlockSpec(memory_space=pl.ANY)] + [mask_spec(s) for s in range(ways)],
            out_specs=[pl.BlockSpec((tile, width), lambda q, c, g: (q, 0)) for s in range(ways)],
            scratch_shapes=[pltpu.VMEM(x_cols.shape, BF), pltpu.SemaphoreType.DMA((copies,))],
        ),
        out_shape=[shape(rows, width) for s in range(ways)],
        cost_estimate=cost(spmm_flops, 2 * masks.size + 2 * x_cols.size + 2 * ways * slab),
        name="spmm",
    )(cols, groups, x_cols, *([masks] * ways))
    terms = [partials[0]] + [across(partials[s], s) for s in range(1, ways)]
    hidden_packed, slopes, agg, spread = call(
        functools.partial(layer_kernel, ways),
        out_shape=(shape(slots, width),) + (shape(rows, width),) * 3,
        in_specs=[VMEM] * (ways + 6),
        out_specs=(VMEM,) * 4,
        cost_estimate=cost(10 * slab * width, 2 * slab * (ways + 9)),
        name="layer",
    )(*terms, x_node, cot_in, turned_col, turned_row, self_weight, neigh_weight)
    spreads = [spread] + [across(spread, s) for s in range(1, ways)]
    hidden_mid = col_phase(hidden_packed)
    grads, own_back = call(
        terms_kernel,
        out_shape=(shape(2 * width, width), shape(rows, width, F32)),
        in_specs=[VMEM] * 4,
        out_specs=(VMEM,) * 2,
        cost_estimate=cost(6 * slab * width, 2 * slab * 9),
        name="terms",
    )(x_node, agg, slopes, self_weight)
    *spreads, own_back, grads = lax.optimization_barrier((*spreads, own_back, grads))
    parts = grads.reshape(ways, -1, width)

    def pick(value, at):
        return lax.dynamic_index_in_dim(value, at, 0, keepdims=False)

    kept = [pick(parts, me)] + [across(pick(parts, groups[s]), s) for s in range(1, ways)]
    back = call(
        functools.partial(spmm_back_kernel, ways),
        grid_spec=pltpu.PrefetchScalarGridSpec(
            num_scalar_prefetch=2,
            grid=(depth,),
            in_specs=[pl.BlockSpec((tile, width), lambda q, c, g: (q, 0)) for s in range(ways)]
            + [mask_spec(s) for s in range(ways)],
            out_specs=VMEM,
            scratch_shapes=[pltpu.VMEM(x_cols.shape, F32)],
        ),
        out_shape=shape(*x_cols.shape),
        cost_estimate=cost(spmm_flops, 2 * masks.size + 2 * x_cols.size + 2 * ways * slab),
        name="spmm_back",
    )(cols, groups, *spreads, *([masks] * ways))
    back, hidden_mid, *kept = lax.optimization_barrier((back, hidden_mid, *kept))
    neigh_back = lax.psum_scatter(back, "col", scatter_dimension=0, tiled=True)
    hidden_in = row_phase(turn(hidden_mid, col_devices, row_devices))
    place = lax.axis_index("col")
    others = jnp.bitwise_xor(place, jnp.arange(col_devices, dtype=jnp.int32)).astype(jnp.int32)

    def along(value, s):
        return lax.ppermute(value, "col", [(i, i ^ s) for i in range(col_devices)])

    def in_place(index, arrays, dtype):
        count, (r, c) = len(arrays), arrays[0].shape
        return call(
            place_kernel,
            in_specs=[pl.BlockSpec(memory_space=pltpu.SMEM)] + [VMEM] * count,
            out_specs=VMEM,
            out_shape=jax.ShapeDtypeStruct((count, r, c), dtype),
            cost_estimate=cost(0, 6 * count * r * c),
            name="in_place",
        )(index, *arrays).reshape(count * r, c)

    kept = sum(term.astype(F32) for term in kept)
    pieces = kept.astype(BF).reshape(col_devices, -1, width)
    mine = [pick(pieces, place)] + [along(pick(pieces, others[s]), s) for s in range(1, col_devices)]
    scale = 1.0 / math.sqrt(rows * devices)
    mine = (sum(term.astype(F32) for term in mine) * scale).astype(BF)
    in_row = in_place(others, [mine] + [along(mine, s) for s in range(1, col_devices)], BF)
    whole = in_place(groups, [in_row] + [across(in_row, s) for s in range(1, ways)], F32)
    own_back, whole = lax.optimization_barrier((own_back, whole))
    grad_packed = call(
        join_kernel,
        out_shape=shape(slots, width),
        in_specs=[VMEM] * 3,
        out_specs=VMEM,
        cost_estimate=cost(2 * slots * slab, 8 * slab),
        name="join_pack",
    )(own_back, neigh_back, node_row)
    grad_in = relay(grad_packed)

    def unpack_own(value):
        return call(
            unpack_kernel,
            out_shape=shape(rows, width),
            in_specs=[VMEM] * 2,
            out_specs=VMEM,
            cost_estimate=cost(2 * slots * slab, 6 * slab),
            name="unpack_owner",
        )(own_col, value)

    hidden_own = unpack_own(hidden_in)
    grad_own = unpack_own(grad_in)
    return (hidden_own, grad_own, whole[:width], whole[width:])


def solution(mesh):
    placed = (
        P(("row", "col"), None),
        P("row", "col", None, None),
        P("row", "col", None, None, None, None),
        P(("row", "col")),
        P(("row", "col")),
        P(("row", "col")),
        P(),
        P(),
        P(("row", "col"), None),
    )
    return jax.shard_map(
        on_device,
        mesh=mesh,
        in_specs=placed,
        out_specs=(P(("row", "col"), None), P(("row", "col"), None), P(), P()),
        check_vma=False,
    )
```

```python
import functools
import math

import jax
import jax.numpy as jnp
from jax import lax
from jax.experimental import pallas as pl
from jax.experimental.pallas import tpu as pltpu
from jax.sharding import PartitionSpec as P

BF = jnp.bfloat16
F32 = jnp.float32
VMEM = pl.BlockSpec(memory_space=pltpu.VMEM)
MIB = 1024 * 1024


def params(mib=16):
    return pltpu.CompilerParams(vmem_limit_bytes=int(mib * MIB))


def cost(flops, nbytes):
    return pl.CostEstimate(flops=int(flops), bytes_accessed=int(nbytes), transcendentals=0)


def dot(a, b, ca=1, cb=0):
    return lax.dot_general(a, b, (((ca,), (cb,)), ((), ())), preferred_element_type=F32)


def as_column(row):
    return jnp.broadcast_to(row, (128, row.shape[1])).T


def block_of(index, size):
    if size & (size - 1) == 0:
        return lax.shift_right_logical(index, size.bit_length() - 1)
    return lax.div(index, jnp.full_like(index, size))


def rank_row(group_row, order_row):
    n = group_row.shape[1]
    group_col = as_column(group_row)[:, :1]
    order_col = as_column(order_row)[:, :1]
    earlier = (group_col == group_row) & (order_col < order_row)
    return jnp.sum(jnp.where(earlier, 1.0, 0.0), axis=0, keepdims=True).astype(jnp.int32)


def slots_onehot(flat_row, slots):
    iota = lax.broadcasted_iota(jnp.int32, (slots, flat_row.shape[1]), 0)
    return jnp.where(iota == flat_row, 1.0, 0.0).astype(BF)


def entries_onehot(flat_col, slots):
    iota = lax.broadcasted_iota(jnp.int32, (flat_col.shape[0], slots), 1)
    return jnp.where(flat_col[:, :1] == iota, 1.0, 0.0).astype(BF)


def own_slots(nodes_row, cap):
    n = nodes_row.shape[1]
    dest = block_of(nodes_row, n)
    rank = rank_row(dest, lax.broadcasted_iota(jnp.int32, (1, n), 1))
    return dest, rank


def pack_kernel(cap, nodes_ref, value_ref, out_ref):
    dest, rank = own_slots(nodes_ref[...], cap)
    out_ref[...] = dot(slots_onehot(dest * cap + rank, out_ref.shape[0]), value_ref[...]).astype(BF)


def index_kernel(
    cap, ways, nodes_ref, position_ref, degree_ref, cot_ref, cot_out, own_col, node_row, node_col, turned_row, turned_col
):
    n = nodes_ref.shape[1]
    width = cot_ref.shape[1]
    dest, rank = own_slots(nodes_ref[...], cap)
    flat = dest * cap + rank
    own_col[...] = as_column(flat)
    packing = slots_onehot(flat, cot_out.shape[0])
    cot_out[:, :width] = dot(packing, cot_ref[...]).astype(BF)
    cot_out[:, width:] = dot(packing, as_column(degree_ref[...].astype(F32)).astype(BF)).astype(BF)
    position = position_ref[...]
    source = block_of(position, n)
    rank = rank_row(source, position)
    place = source * cap + rank
    node_row[...] = jnp.broadcast_to(place, node_row.shape)
    node_col[...] = as_column(place)
    across = cot_out.shape[0] // (cap * ways)
    down = block_of(source, across)
    turned = ((source - down * across) * ways + down) * cap + rank
    turned_row[...] = jnp.broadcast_to(turned, turned_row.shape)
    turned_col[...] = as_column(turned)


def unpack_kernel(col_ref, value_ref, out_ref):
    out_ref[...] = dot(entries_onehot(col_ref[...], value_ref.shape[0]), value_ref[...]).astype(BF)


def spmm_kernel(ways, cols_ref, group_ref, x_hbm, *refs):
    masks, outs = refs[:ways], refs[ways : 2 * ways]
    x_ref, sems = refs[2 * ways :]
    q = pl.program_id(0)
    depth = pl.num_programs(0)
    _, breadth, tile, _ = masks[0].shape

    @pl.when(q == 0)
    def _():
        count = sems.shape[0]
        share = x_ref.shape[0] // count
        copies = [
            pltpu.make_async_copy(x_hbm.at[pl.ds(i * share, share)], x_ref.at[pl.ds(i * share, share)], sems.at[i])
            for i in range(count)
        ]
        for copy in copies:
            copy.start()
        for copy in copies:
            copy.wait()

    for s in range(ways):
        base = (group_ref[s] * depth + q) * breadth
        total = None
        for p in range(0, breadth, 2):
            width = min(2, breadth - p)
            left = jnp.concatenate([masks[s][0, p + w] for w in range(width)], axis=1)
            right = jnp.concatenate(
                [x_ref[pl.ds(pl.multiple_of(cols_ref[base + p + w] * tile, tile), tile), :] for w in range(width)], axis=0
            )
            term = dot(left, right)
            total = term if total is None else total + term
        outs[s][...] = total.astype(BF)


def spmm_back_kernel(ways, pieces, cols_ref, group_ref, *refs):
    given = sum(pieces)
    spreads, masks, out_ref, total = refs[:given], refs[given : given + ways], refs[-2], refs[-1]
    q = pl.program_id(0)
    depth = pl.num_programs(0)
    _, breadth, tile, _ = masks[0].shape

    @pl.when(q == 0)
    def _():
        total[...] = jnp.zeros_like(total)

    at_piece = 0
    for s in range(ways):
        base = (group_ref[s] * depth + q) * breadth
        rows = spreads[at_piece][...]
        for p in range(1, pieces[s]):
            rows = jnp.where(q * pieces[s] >= p * depth, spreads[at_piece + p][...], rows)
        at_piece += pieces[s]
        for k in range(breadth):
            at = pl.ds(pl.multiple_of(cols_ref[base + k] * tile, tile), tile)
            total[at, :] += dot(masks[s][0, k], rows, 0, 0)

    @pl.when(q == depth - 1)
    def _():
        out_ref[...] = total[...].astype(BF)


def pass_on_kernel(left_ref, right_ref, top_ref, bottom_ref, left_out, right_out):
    half = top_ref.shape[0]
    left_out[:half, :] = left_ref[:half, :]
    left_out[half:, :] = (left_ref[half:, :].astype(F32) + bottom_ref[...].astype(F32)).astype(BF)
    right_out[:half, :] = (right_ref[:half, :].astype(F32) + top_ref[...].astype(F32)).astype(BF)
    right_out[half:, :] = right_ref[half:, :]


def layer_kernel(ways, *refs):
    terms = refs[:ways]
    (x_ref, cot_ref, col_ref, row_ref, self_ref, neigh_ref, packed_out, slopes_out, agg_out, spread_out) = refs[ways:]
    width = x_ref.shape[1]
    summed = terms[0][...].astype(F32)
    for s in range(1, ways):
        summed = summed + terms[s][...].astype(F32)
    cot = dot(entries_onehot(col_ref[...], cot_ref.shape[0]), cot_ref[...])
    degrees = cot[:, width : width + 1]
    agg = (summed / degrees).astype(BF)
    agg_out[...] = agg
    preact = dot(x_ref[...], self_ref[...]) + dot(agg, neigh_ref[...])
    gate = jax.nn.sigmoid(preact)
    hidden = (preact * gate).astype(BF)
    slopes = (cot[:, :width] * gate * (1.0 + preact * (1.0 - gate))).astype(BF)
    slopes_out[...] = slopes
    spread_out[...] = (dot(slopes, neigh_ref[...], 1, 1) / degrees).astype(BF)
    packed_out[...] = dot(slots_onehot(row_ref[...][:1], packed_out.shape[0]), hidden).astype(BF)


def terms_kernel(core_ref, x_ref, agg_ref, slopes_ref, self_ref, kept_out, sent_out, back_out):
    slopes = slopes_ref[...]
    back_out[...] = dot(slopes, self_ref[...], 1, 1)
    grad_self = dot(x_ref[...], slopes, 0, 0).astype(BF)
    grad_neigh = dot(agg_ref[...], slopes, 0, 0).astype(BF)
    first = core_ref[0] == 0
    kept_out[...] = jnp.where(first, grad_self, grad_neigh)
    sent_out[...] = jnp.where(first, grad_neigh, grad_self)


def split_sum_kernel(count, scale, index_ref, *refs):
    terms, outs, total_ref = refs[:count], refs[count:-1], refs[-1]
    total = terms[0][...].astype(F32)
    for term in terms[1:]:
        total = total + term[...].astype(F32)
    total_ref[...] = total * scale
    size = outs[0].shape[0]
    for s, out in enumerate(outs):
        out[...] = total_ref[pl.ds(pl.multiple_of(index_ref[s] * size, size), size), :].astype(out.dtype)


def place_kernel(index_ref, *refs):
    out_ref = refs[-1]
    for s, part in enumerate(refs[:-1]):
        out_ref[index_ref[s]] = part[...].astype(out_ref.dtype)


def final_kernel(core_ref, kept_ref, came_ref, self_out, neigh_out):
    first = core_ref[0] == 0
    kept, came = kept_ref[...].astype(F32), came_ref[...].astype(F32)
    self_out[...] = jnp.where(first, kept, came)
    neigh_out[...] = jnp.where(first, came, kept)


def join_kernel(own_ref, neigh_ref, row_ref, out_ref):
    joined = (own_ref[...] + neigh_ref[...].astype(F32)).astype(BF)
    out_ref[...] = dot(slots_onehot(row_ref[...][:1], out_ref.shape[0]), joined).astype(BF)


def on_device(
    features,
    tile_cols,
    tile_masks,
    degree,
    owner_nodes,
    owner_position,
    self_weight,
    neigh_weight,
    cotangent,
):
    rows, width = features.shape
    row_devices = lax.axis_size("row")
    col_devices = lax.axis_size("col")
    devices = row_devices * col_devices
    cap = 2 * rows // devices
    slots = devices * cap
    masks = tile_masks[0, 0]
    tile = masks.shape[-1]
    breadth = masks.shape[1]
    depth = rows // tile
    cols = tile_cols[0, 0].reshape(-1)
    me = lax.axis_index("row")
    ways = row_devices
    groups = jnp.bitwise_xor(me, jnp.arange(ways, dtype=jnp.int32)).astype(jnp.int32)
    everyone = ("row", "col")
    place = lax.axis_index("col")
    lines = col_devices // 2
    core = jnp.full((1,), lax.rem(place, 2), jnp.int32)
    others = jnp.bitwise_xor(lax.div(place, 2), jnp.arange(lines, dtype=jnp.int32)).astype(jnp.int32)
    SMEM = pl.BlockSpec(memory_space=pltpu.SMEM)

    def call(*args, mib=16, **kwargs):
        return pl.pallas_call(*args, compiler_params=params(mib), **kwargs)

    def shape(r, c, dtype=BF):
        return jax.ShapeDtypeStruct((r, c), dtype)

    def relay(packed):
        there = packed.reshape(devices, cap, -1)
        return lax.all_to_all(there, everyone, split_axis=0, concat_axis=0, tiled=True).reshape(slots, -1)

    def row_phase(packed):
        there = packed.reshape(row_devices, col_devices * cap, -1)
        return lax.all_to_all(there, "row", split_axis=0, concat_axis=0, tiled=True).reshape(slots, -1)

    def col_phase(packed):
        there = packed.reshape(col_devices, row_devices * cap, -1)
        return lax.all_to_all(there, "col", split_axis=0, concat_axis=0, tiled=True).reshape(slots, -1)

    def turn(packed, first, second):
        return packed.reshape(first, second, cap, -1).transpose(1, 0, 2, 3).reshape(slots, -1)

    def across(value, s):
        return lax.ppermute(value, "row", [(i, i ^ s) for i in range(ways)])

    def along(value, s):
        return lax.ppermute(value, "col", [(i, i ^ (2 * s)) for i in range(col_devices)])

    def swap(value):
        return lax.ppermute(value, "col", [(i, i ^ 1) for i in range(col_devices)])

    def split_sum(index, arrays, pieces, scale=1.0):
        r, c = arrays[0].shape
        return call(
            functools.partial(split_sum_kernel, len(arrays), scale),
            in_specs=[SMEM] + [VMEM] * len(arrays),
            out_specs=[VMEM] * pieces,
            out_shape=[shape(r // pieces, c) for _ in range(pieces)],
            scratch_shapes=[pltpu.VMEM((r, c), F32)],
            cost_estimate=cost(r * c * len(arrays), 2 * r * c * (len(arrays) + 1)),
            name="split_sum",
        )(index, *arrays)

    def in_place(index, arrays):
        count, (r, c) = len(arrays), arrays[0].shape
        return call(
            place_kernel,
            in_specs=[SMEM] + [VMEM] * count,
            out_specs=VMEM,
            out_shape=jax.ShapeDtypeStruct((count, r, c), BF),
            cost_estimate=cost(0, 4 * count * r * c),
            name="in_place",
        )(index, *arrays).reshape(count * r, c)

    nodes = owner_nodes.reshape(1, rows)
    slab = rows * width
    packed = call(
        functools.partial(pack_kernel, cap),
        out_shape=shape(slots, width),
        in_specs=[VMEM] * 2,
        out_specs=VMEM,
        cost_estimate=cost(2 * slots * slab, 6 * slab),
        name="pack_features",
    )(nodes, features)
    inbound = relay(packed)
    cot_packed, own_col, node_row, node_col, turned_row, turned_col = call(
        functools.partial(index_kernel, cap, ways),
        out_shape=(
            shape(slots, width + 128),
            shape(rows, 128, jnp.int32),
            shape(8, rows, jnp.int32),
            shape(rows, 128, jnp.int32),
            shape(8, rows, jnp.int32),
            shape(rows, 128, jnp.int32),
        ),
        in_specs=[VMEM] * 4,
        out_specs=(VMEM,) * 6,
        cost_estimate=cost(2 * slots * slab, 6 * slab),
        name="index_cotangent",
    )(nodes, owner_position.reshape(1, rows), degree.reshape(1, rows), cotangent)
    x_node = call(
        unpack_kernel,
        out_shape=shape(rows, width),
        in_specs=[VMEM] * 2,
        out_specs=VMEM,
        cost_estimate=cost(2 * slots * slab, 6 * slab),
        name="unpack_features",
    )(node_col, inbound)
    cot_packed, x_node, cols, groups, core, others = lax.optimization_barrier(
        (cot_packed, x_node, cols, groups, core, others)
    )
    x_cols = lax.all_gather(x_node, "col", axis=0, tiled=True)
    cot_mid = turn(row_phase(cot_packed), row_devices, col_devices)
    x_cols, cot_mid = lax.optimization_barrier((x_cols, cot_mid))
    cot_in = col_phase(cot_mid)

    def mask_spec(s):
        return pl.BlockSpec((1, breadth, tile, tile), lambda q, c, g, s=s: (g[s] * depth + q, 0, 0, 0))

    def piece_spec(p, count):
        share = depth // count
        return pl.BlockSpec((tile, width), lambda q, c, g: (jnp.clip(q - p * share, 0, share - 1), 0))

    spmm_flops = 2 * masks.size * width
    copies = 8
    partials = call(
        functools.partial(spmm_kernel, ways),
        grid_spec=pltpu.PrefetchScalarGridSpec(
            num_scalar_prefetch=2,
            grid=(depth,),
            in_specs=[pl.BlockSpec(memory_space=pl.ANY)] + [mask_spec(s) for s in range(ways)],
            out_specs=[pl.BlockSpec((tile, width), lambda q, c, g: (q, 0)) for s in range(ways)],
            scratch_shapes=[pltpu.VMEM(x_cols.shape, BF), pltpu.SemaphoreType.DMA((copies,))],
        ),
        out_shape=[shape(rows, width) for s in range(ways)],
        cost_estimate=cost(spmm_flops, 2 * masks.size + 2 * x_cols.size + 2 * ways * slab),
        mib=12 + 3 * x_cols.size / MIB,
        name="spmm",
    )(cols, groups, x_cols, *([masks] * ways))
    if ways == 4:
        half = rows // 2
        top = across(partials[3][:half], 1)
        bottom = across(partials[3][half:], 2)
        left, right = call(
            pass_on_kernel,
            out_shape=(shape(rows, width),) * 2,
            in_specs=[VMEM] * 4,
            out_specs=(VMEM,) * 2,
            cost_estimate=cost(2 * slab, 10 * slab),
            name="pass_on",
        )(partials[1], partials[2], top, bottom)
        terms = [partials[0], across(left, 1), across(right, 2)]
    else:
        terms = [partials[0]] + [across(partials[s], s) for s in range(1, ways)]
    hidden_packed, slopes, agg, spread = call(
        functools.partial(layer_kernel, len(terms)),
        out_shape=(shape(slots, width),) + (shape(rows, width),) * 3,
        in_specs=[VMEM] * (len(terms) + 6),
        out_specs=(VMEM,) * 4,
        cost_estimate=cost(10 * slab * width, 2 * slab * (ways + 9)),
        mib=24,
        name="layer",
    )(*terms, x_node, cot_in, turned_col, turned_row, self_weight, neigh_weight)
    if ways == 4:
        left, right = across(spread, 1), across(spread, 2)
        left, right, hidden_packed = lax.optimization_barrier((left, right, hidden_packed))
        spreads = [spread, left, right, across(right[:half], 1), across(left[half:], 2)]
        pieces = (1, 1, 1, 2)
    else:
        spreads = [spread] + [across(spread, s) for s in range(1, ways)]
        pieces = (1,) * ways
    hidden_mid = col_phase(hidden_packed)
    grad_kept, grad_sent, own_back = call(
        terms_kernel,
        out_shape=(shape(width, width), shape(width, width), shape(rows, width, F32)),
        in_specs=[SMEM] + [VMEM] * 4,
        out_specs=(VMEM,) * 3,
        cost_estimate=cost(6 * slab * width, 2 * slab * 9),
        name="terms",
    )(core, x_node, agg, slopes, self_weight)
    *spreads, own_back, grad_kept, grad_sent = lax.optimization_barrier((*spreads, own_back, grad_kept, grad_sent))
    back = call(
        functools.partial(spmm_back_kernel, ways, pieces),
        grid_spec=pltpu.PrefetchScalarGridSpec(
            num_scalar_prefetch=2,
            grid=(depth,),
            in_specs=[piece_spec(p, count) for count in pieces for p in range(count)]
            + [mask_spec(s) for s in range(ways)],
            out_specs=VMEM,
            scratch_shapes=[pltpu.VMEM(x_cols.shape, F32)],
        ),
        out_shape=shape(*x_cols.shape),
        cost_estimate=cost(spmm_flops, 2 * masks.size + 2 * x_cols.size + 2 * ways * slab),
        mib=12 + 7 * x_cols.size / MIB,
        name="spmm_back",
    )(cols, groups, *spreads, *([masks] * ways))
    back, hidden_mid, grad_sent = lax.optimization_barrier((back, hidden_mid, grad_sent))
    neigh_back = lax.psum_scatter(back, "col", scatter_dimension=0, tiled=True)
    hidden_in = row_phase(turn(hidden_mid, col_devices, row_devices))
    pieces = split_sum(groups, [grad_kept, swap(grad_sent)], ways)
    pieces = split_sum(others, [pieces[0]] + [across(pieces[s], s) for s in range(1, ways)], lines)
    scale = 1.0 / math.sqrt(rows * devices)
    zero = jnp.zeros((1,), jnp.int32)
    (mine,) = split_sum(zero, [pieces[0]] + [along(pieces[s], s) for s in range(1, lines)], 1, scale)
    in_line = in_place(others, [mine] + [along(mine, s) for s in range(1, lines)])
    own_back, in_line = lax.optimization_barrier((own_back, in_line))
    grad_half = in_place(groups, [in_line] + [across(in_line, s) for s in range(1, ways)])
    grad_self, grad_neigh = call(
        final_kernel,
        in_specs=[SMEM] + [VMEM] * 2,
        out_specs=(VMEM,) * 2,
        out_shape=(shape(width, width, F32),) * 2,
        cost_estimate=cost(0, 12 * width * width),
        name="final",
    )(core, grad_half, swap(grad_half))
    grad_packed = call(
        join_kernel,
        out_shape=shape(slots, width),
        in_specs=[VMEM] * 3,
        out_specs=VMEM,
        cost_estimate=cost(2 * slots * slab, 8 * slab),
        name="join_pack",
    )(own_back, neigh_back, node_row)
    grad_in = relay(grad_packed)

    def unpack_own(value):
        return call(
            unpack_kernel,
            out_shape=shape(rows, width),
            in_specs=[VMEM] * 2,
            out_specs=VMEM,
            cost_estimate=cost(2 * slots * slab, 6 * slab),
            name="unpack_owner",
        )(own_col, value)

    hidden_own = unpack_own(hidden_in)
    grad_own = unpack_own(grad_in)
    return (hidden_own, grad_own, grad_self, grad_neigh)


def solution(mesh):
    placed = (
        P(("row", "col"), None),
        P("row", "col", None, None),
        P("row", "col", None, None, None, None),
        P(("row", "col")),
        P(("row", "col")),
        P(("row", "col")),
        P(),
        P(),
        P(("row", "col"), None),
    )
    return jax.shard_map(
        on_device,
        mesh=mesh,
        in_specs=placed,
        out_specs=(P(("row", "col"), None), P(("row", "col"), None), P(), P()),
        check_vma=False,
    )
```

```python
import functools
import math

import jax
import jax.numpy as jnp
from jax import lax
from jax.experimental import pallas as pl
from jax.experimental.pallas import tpu as pltpu
from jax.sharding import PartitionSpec as P

BF = jnp.bfloat16
F32 = jnp.float32
VMEM = pl.BlockSpec(memory_space=pltpu.VMEM)
MIB = 1024 * 1024
LARGE = 56


def params(mib=16):
    return pltpu.CompilerParams(vmem_limit_bytes=int(mib * MIB))


def cost(flops, nbytes):
    return pl.CostEstimate(flops=int(flops), bytes_accessed=int(nbytes), transcendentals=0)


def dot(a, b, ca=1, cb=0):
    return lax.dot_general(a, b, (((ca,), (cb,)), ((), ())), preferred_element_type=F32)


def as_column(row):
    return jnp.broadcast_to(row, (128, row.shape[1])).T


def block_of(index, size):
    if size & (size - 1) == 0:
        return lax.shift_right_logical(index, size.bit_length() - 1)
    return lax.div(index, jnp.full_like(index, size))


def rank_row(group_row, order_row):
    n = group_row.shape[1]
    group_col = as_column(group_row)[:, :1]
    order_col = as_column(order_row)[:, :1]
    earlier = (group_col == group_row) & (order_col < order_row)
    return jnp.sum(jnp.where(earlier, 1.0, 0.0), axis=0, keepdims=True).astype(jnp.int32)


def slots_onehot(flat_row, slots):
    iota = lax.broadcasted_iota(jnp.int32, (slots, flat_row.shape[1]), 0)
    return jnp.where(iota == flat_row, 1.0, 0.0).astype(BF)


def entries_onehot(flat_col, slots):
    iota = lax.broadcasted_iota(jnp.int32, (flat_col.shape[0], slots), 1)
    return jnp.where(flat_col[:, :1] == iota, 1.0, 0.0).astype(BF)


def own_slots(nodes_row, cap):
    n = nodes_row.shape[1]
    dest = block_of(nodes_row, n)
    rank = rank_row(dest, lax.broadcasted_iota(jnp.int32, (1, n), 1))
    return dest, rank


def pack_kernel(cap, nodes_ref, value_ref, out_ref):
    dest, rank = own_slots(nodes_ref[...], cap)
    out_ref[...] = dot(slots_onehot(dest * cap + rank, out_ref.shape[0]), value_ref[...]).astype(BF)


def index_kernel(
    cap, ways, nodes_ref, position_ref, degree_ref, cot_ref, cot_out, own_col, node_row, node_col, turned_row, turned_col
):
    n = nodes_ref.shape[1]
    width = cot_ref.shape[1]
    dest, rank = own_slots(nodes_ref[...], cap)
    flat = dest * cap + rank
    own_col[...] = as_column(flat)
    packing = slots_onehot(flat, cot_out.shape[0])
    cot_out[:, :width] = dot(packing, cot_ref[...]).astype(BF)
    cot_out[:, width:] = dot(packing, as_column(degree_ref[...].astype(F32)).astype(BF)).astype(BF)
    position = position_ref[...]
    source = block_of(position, n)
    rank = rank_row(source, position)
    place = source * cap + rank
    node_row[...] = jnp.broadcast_to(place, node_row.shape)
    node_col[...] = as_column(place)
    across = cot_out.shape[0] // (cap * ways)
    down = block_of(source, across)
    turned = ((source - down * across) * ways + down) * cap + rank
    turned_row[...] = jnp.broadcast_to(turned, turned_row.shape)
    turned_col[...] = as_column(turned)


def unpack_kernel(col_ref, value_ref, out_ref):
    out_ref[...] = dot(entries_onehot(col_ref[...], value_ref.shape[0]), value_ref[...]).astype(BF)


def load_masks(group_ref, masks_hbm, masks_ref, sems, ways, depth, q):
    return [
        pltpu.make_async_copy(masks_hbm.at[group_ref[s] * depth + q], masks_ref.at[q * ways + s], sems.at[q * ways + s])
        for s in range(ways)
    ]


def spmm_kernel(ways, halves, cols_ref, group_ref, core_ref, own_hbm, other_hbm, masks_hbm, *refs):
    outs = refs[:ways]
    x_ref, masks_ref, x_sems, mask_sems = refs[ways:]
    h, q = pl.program_id(0), pl.program_id(1)
    depth = pl.num_programs(1)
    steps = masks_ref.shape[0] // ways
    _, breadth, tile, _ = masks_ref.shape
    width = x_ref.shape[2]
    block = tile * steps
    lines = own_hbm.shape[0] // block

    def load_x(half):
        copies = []
        for j, source in enumerate((own_hbm, other_hbm)):
            for z in range(lines):
                to = pl.multiple_of((2 * z + jnp.bitwise_xor(core_ref[0], j)) * block, block)
                copies.append(
                    pltpu.make_async_copy(
                        source.at[pl.ds(z * block, block), pl.ds(half * width, width)],
                        x_ref.at[half, pl.ds(to, block), :],
                        x_sems.at[half, j * lines + z],
                    )
                )
        return copies

    @pl.when((h == 0) & (q == 0))
    def _():
        for copy in load_x(0):
            copy.start()
        for step in range(steps):
            for copy in load_masks(group_ref, masks_hbm, masks_ref, mask_sems, ways, steps, step):
                copy.start()
        for half in range(1, halves):
            for copy in load_x(half):
                copy.start()

    for half in range(halves):

        @pl.when((h == half) & (q == 0))
        def _():
            for copy in load_x(half):
                copy.wait()

    for step in range(steps):

        @pl.when((h == 0) & (q == step))
        def _():
            for copy in load_masks(group_ref, masks_hbm, masks_ref, mask_sems, ways, steps, step):
                copy.wait()

    for s in range(ways):
        base = (group_ref[s] * depth + q) * breadth
        at = q * ways + s
        total = None
        for p in range(0, breadth, 2):
            span = min(2, breadth - p)
            left = jnp.concatenate([masks_ref[at, p + w] for w in range(span)], axis=1)
            right = jnp.concatenate(
                [
                    x_ref[h, pl.ds(pl.multiple_of(cols_ref[base + p + w] * tile, tile), tile), :]
                    for w in range(span)
                ],
                axis=0,
            )
            term = dot(left, right)
            total = term if total is None else total + term
        outs[s][...] = total.astype(BF)


def spmm_back_kernel(ways, halves, pieces, cols_ref, group_ref, core_ref, *refs):
    given = sum(pieces)
    spreads = refs[:given]
    masks_hbm, own_hbm, other_hbm, total, ready, masks_ref, out_sems, mask_sems = refs[given:]
    h, q = pl.program_id(0), pl.program_id(1)
    depth = pl.num_programs(1)
    steps = masks_ref.shape[0] // ways
    _, breadth, tile, _ = masks_ref.shape
    width = total.shape[1]
    block = tile * steps
    lines = own_hbm.shape[0] // block

    def store(half):
        copies = []
        for j, target in enumerate((own_hbm, other_hbm)):
            for z in range(lines):
                at = pl.multiple_of((2 * z + jnp.bitwise_xor(core_ref[0], j)) * block, block)
                copies.append(
                    pltpu.make_async_copy(
                        ready.at[half, pl.ds(at, block), :],
                        target.at[pl.ds(z * block, block), pl.ds(half * width, width)],
                        out_sems.at[half, j * lines + z],
                    )
                )
        return copies

    @pl.when((h == 0) & (q == 0))
    def _():
        for step in range(steps):
            for copy in load_masks(group_ref, masks_hbm, masks_ref, mask_sems, ways, steps, step):
                copy.start()

    @pl.when(q == 0)
    def _():
        total[...] = jnp.zeros_like(total)

    for step in range(steps):

        @pl.when((h == 0) & (q == step))
        def _():
            for copy in load_masks(group_ref, masks_hbm, masks_ref, mask_sems, ways, steps, step):
                copy.wait()

    at_piece = 0
    for s in range(ways):
        base = (group_ref[s] * depth + q) * breadth
        rows = spreads[at_piece][...]
        for p in range(1, pieces[s]):
            rows = jnp.where(q * pieces[s] >= p * depth, spreads[at_piece + p][...], rows)
        at_piece += pieces[s]
        for k in range(breadth):
            at = pl.ds(pl.multiple_of(cols_ref[base + k] * tile, tile), tile)
            total[at, :] += dot(masks_ref[q * ways + s, k], rows, 0, 0)

    for half in range(halves):

        @pl.when((h == half) & (q == depth - 1))
        def _():
            ready[half] = total[...].astype(BF)
            for copy in store(half):
                copy.start()
            if half == halves - 1:
                for earlier in range(halves):
                    for copy in store(earlier):
                        copy.wait()


def pass_on_kernel(left_ref, right_ref, top_ref, bottom_ref, left_out, right_out):
    half = top_ref.shape[0]
    left_out[:half, :] = left_ref[:half, :]
    left_out[half:, :] = (left_ref[half:, :].astype(F32) + bottom_ref[...].astype(F32)).astype(BF)
    right_out[:half, :] = (right_ref[:half, :].astype(F32) + top_ref[...].astype(F32)).astype(BF)
    right_out[half:, :] = right_ref[half:, :]


def layer_kernel(ways, *refs):
    terms = refs[:ways]
    (x_ref, cot_ref, col_ref, row_ref, self_ref, neigh_ref, packed_out, slopes_out, agg_out, spread_out) = refs[ways:]
    width = x_ref.shape[1]
    summed = terms[0][...].astype(F32)
    for s in range(1, ways):
        summed = summed + terms[s][...].astype(F32)
    cot = dot(entries_onehot(col_ref[...], cot_ref.shape[0]), cot_ref[...])
    degrees = cot[:, width : width + 1]
    agg = (summed / degrees).astype(BF)
    agg_out[...] = agg
    preact = dot(x_ref[...], self_ref[...]) + dot(agg, neigh_ref[...])
    gate = jax.nn.sigmoid(preact)
    hidden = (preact * gate).astype(BF)
    slopes = (cot[:, :width] * gate * (1.0 + preact * (1.0 - gate))).astype(BF)
    slopes_out[...] = slopes
    spread_out[...] = (dot(slopes, neigh_ref[...], 1, 1) / degrees).astype(BF)
    packed_out[...] = dot(slots_onehot(row_ref[...][:1], packed_out.shape[0]), hidden).astype(BF)


def terms_kernel(core_ref, x_ref, agg_ref, slopes_ref, self_ref, kept_out, sent_out, back_out):
    slopes = slopes_ref[...]
    back_out[...] = dot(slopes, self_ref[...], 1, 1)
    grad_self = dot(x_ref[...], slopes, 0, 0).astype(BF)
    grad_neigh = dot(agg_ref[...], slopes, 0, 0).astype(BF)
    first = core_ref[0] == 0
    kept_out[...] = jnp.where(first, grad_self, grad_neigh)
    sent_out[...] = jnp.where(first, grad_neigh, grad_self)


def split_sum_kernel(count, scale, index_ref, *refs):
    terms, outs, total_ref = refs[:count], refs[count:-1], refs[-1]
    total = terms[0][...].astype(F32)
    for term in terms[1:]:
        total = total + term[...].astype(F32)
    total_ref[...] = total * scale
    size = outs[0].shape[0]
    for s, out in enumerate(outs):
        out[...] = total_ref[pl.ds(pl.multiple_of(index_ref[s] * size, size), size), :].astype(out.dtype)


def place_kernel(index_ref, *refs):
    out_ref = refs[-1]
    for s, part in enumerate(refs[:-1]):
        out_ref[index_ref[s]] = part[...].astype(out_ref.dtype)


def final_kernel(core_ref, kept_ref, came_ref, self_out, neigh_out):
    first = core_ref[0] == 0
    kept, came = kept_ref[...].astype(F32), came_ref[...].astype(F32)
    self_out[...] = jnp.where(first, kept, came)
    neigh_out[...] = jnp.where(first, came, kept)


def join_kernel(own_ref, neigh_ref, row_ref, out_ref):
    joined = (own_ref[...] + neigh_ref[...].astype(F32)).astype(BF)
    out_ref[...] = dot(slots_onehot(row_ref[...][:1], out_ref.shape[0]), joined).astype(BF)


def on_device(
    features,
    tile_cols,
    tile_masks,
    degree,
    owner_nodes,
    owner_position,
    self_weight,
    neigh_weight,
    cotangent,
):
    rows, width = features.shape
    row_devices = lax.axis_size("row")
    col_devices = lax.axis_size("col")
    devices = row_devices * col_devices
    cap = 2 * rows // devices
    slots = devices * cap
    masks = tile_masks[0, 0]
    tile = masks.shape[-1]
    breadth = masks.shape[1]
    depth = rows // tile
    cols = tile_cols[0, 0].reshape(-1)
    me = lax.axis_index("row")
    ways = row_devices
    groups = jnp.bitwise_xor(me, jnp.arange(ways, dtype=jnp.int32)).astype(jnp.int32)
    everyone = ("row", "col")
    place = lax.axis_index("col")
    lines = col_devices // 2
    core = jnp.full((1,), lax.rem(place, 2), jnp.int32)
    others = jnp.bitwise_xor(lax.div(place, 2), jnp.arange(lines, dtype=jnp.int32)).astype(jnp.int32)
    SMEM = pl.BlockSpec(memory_space=pltpu.SMEM)

    def call(*args, mib=16, **kwargs):
        return pl.pallas_call(*args, compiler_params=params(mib), **kwargs)

    def shape(r, c, dtype=BF):
        return jax.ShapeDtypeStruct((r, c), dtype)

    def relay(packed):
        there = packed.reshape(devices, cap, -1)
        return lax.all_to_all(there, everyone, split_axis=0, concat_axis=0, tiled=True).reshape(slots, -1)

    def row_phase(packed):
        there = packed.reshape(row_devices, col_devices * cap, -1)
        return lax.all_to_all(there, "row", split_axis=0, concat_axis=0, tiled=True).reshape(slots, -1)

    def col_phase(packed):
        there = packed.reshape(col_devices, row_devices * cap, -1)
        return lax.all_to_all(there, "col", split_axis=0, concat_axis=0, tiled=True).reshape(slots, -1)

    def turn(packed, first, second):
        return packed.reshape(first, second, cap, -1).transpose(1, 0, 2, 3).reshape(slots, -1)

    def across(value, s):
        return lax.ppermute(value, "row", [(i, i ^ s) for i in range(ways)])

    def along(value, s):
        return lax.ppermute(value, "col", [(i, i ^ (2 * s)) for i in range(col_devices)])

    def swap(value):
        return lax.ppermute(value, "col", [(i, i ^ 1) for i in range(col_devices)])

    def split_sum(index, arrays, pieces, scale=1.0):
        r, c = arrays[0].shape
        return call(
            functools.partial(split_sum_kernel, len(arrays), scale),
            in_specs=[SMEM] + [VMEM] * len(arrays),
            out_specs=[VMEM] * pieces,
            out_shape=[shape(r // pieces, c) for _ in range(pieces)],
            scratch_shapes=[pltpu.VMEM((r, c), F32)],
            cost_estimate=cost(r * c * len(arrays), 2 * r * c * (len(arrays) + 1)),
            name="split_sum",
        )(index, *arrays)

    def in_place(index, arrays):
        count, (r, c) = len(arrays), arrays[0].shape
        return call(
            place_kernel,
            in_specs=[SMEM] + [VMEM] * count,
            out_specs=VMEM,
            out_shape=jax.ShapeDtypeStruct((count, r, c), BF),
            cost_estimate=cost(0, 4 * count * r * c),
            name="in_place",
        )(index, *arrays).reshape(count * r, c)

    nodes = owner_nodes.reshape(1, rows)
    slab = rows * width
    packed = call(
        functools.partial(pack_kernel, cap),
        out_shape=shape(slots, width),
        in_specs=[VMEM] * 2,
        out_specs=VMEM,
        cost_estimate=cost(2 * slots * slab, 6 * slab),
        mib=LARGE,
        name="pack_features",
    )(nodes, features)
    inbound = relay(packed)
    cot_packed, own_col, node_row, node_col, turned_row, turned_col = call(
        functools.partial(index_kernel, cap, ways),
        out_shape=(
            shape(slots, width + 128),
            shape(rows, 128, jnp.int32),
            shape(8, rows, jnp.int32),
            shape(rows, 128, jnp.int32),
            shape(8, rows, jnp.int32),
            shape(rows, 128, jnp.int32),
        ),
        in_specs=[VMEM] * 4,
        out_specs=(VMEM,) * 6,
        cost_estimate=cost(2 * slots * slab, 6 * slab),
        mib=LARGE,
        name="index_cotangent",
    )(nodes, owner_position.reshape(1, rows), degree.reshape(1, rows), cotangent)
    x_node = call(
        unpack_kernel,
        out_shape=shape(rows, width),
        in_specs=[VMEM] * 2,
        out_specs=VMEM,
        cost_estimate=cost(2 * slots * slab, 6 * slab),
        name="unpack_features",
    )(node_col, inbound)
    cot_packed, x_node, cols, groups, core, others = lax.optimization_barrier(
        (cot_packed, x_node, cols, groups, core, others)
    )
    same_core = [list(range(k, col_devices, 2)) for k in range(2)]
    x_own = lax.all_gather(x_node, "col", axis_index_groups=same_core, axis=0, tiled=True)
    cot_mid = turn(row_phase(cot_packed), row_devices, col_devices)
    x_own, cot_mid = lax.optimization_barrier((x_own, cot_mid))
    x_other = swap(x_own)
    cot_in = col_phase(cot_mid)

    def piece_spec(p, count):
        share = depth // count
        return pl.BlockSpec((tile, part), lambda h, q, *_: (jnp.clip(q - p * share, 0, share - 1), h))

    halves = 2
    part = width // halves
    cell_rows = col_devices * rows
    ANY = pl.BlockSpec(memory_space=pl.ANY)
    masks_scratch = pltpu.VMEM(masks.shape, BF)
    mask_sems = pltpu.SemaphoreType.DMA((masks.shape[0],))
    x_sems = pltpu.SemaphoreType.DMA((halves, col_devices))

    spmm_flops = 2 * masks.size * width
    partials = call(
        functools.partial(spmm_kernel, ways, halves),
        grid_spec=pltpu.PrefetchScalarGridSpec(
            num_scalar_prefetch=3,
            grid=(halves, depth),
            in_specs=[ANY] * 3,
            out_specs=[pl.BlockSpec((tile, part), lambda h, q, *_: (q, h)) for s in range(ways)],
            scratch_shapes=[pltpu.VMEM((halves, cell_rows, part), BF), masks_scratch, x_sems, mask_sems],
        ),
        out_shape=[shape(rows, width) for s in range(ways)],
        cost_estimate=cost(spmm_flops, 2 * masks.size + 2 * cell_rows * width + 2 * ways * slab),
        mib=LARGE,
        name="spmm",
    )(cols, groups, core, x_own, x_other, masks)
    if ways == 4:
        half = rows // 2
        top = across(partials[3][:half], 1)
        bottom = across(partials[3][half:], 2)
        left, right = call(
            pass_on_kernel,
            out_shape=(shape(rows, width),) * 2,
            in_specs=[VMEM] * 4,
            out_specs=(VMEM,) * 2,
            cost_estimate=cost(2 * slab, 10 * slab),
            mib=LARGE,
            name="pass_on",
        )(partials[1], partials[2], top, bottom)
        terms = [partials[0], across(left, 1), across(right, 2)]
    else:
        terms = [partials[0]] + [across(partials[s], s) for s in range(1, ways)]
    hidden_packed, slopes, agg, spread = call(
        functools.partial(layer_kernel, len(terms)),
        out_shape=(shape(slots, width),) + (shape(rows, width),) * 3,
        in_specs=[VMEM] * (len(terms) + 6),
        out_specs=(VMEM,) * 4,
        cost_estimate=cost(10 * slab * width, 2 * slab * (ways + 9)),
        mib=LARGE,
        name="layer",
    )(*terms, x_node, cot_in, turned_col, turned_row, self_weight, neigh_weight)
    if ways == 4:
        left, right = across(spread, 1), across(spread, 2)
        spreads = [spread, left, right, across(right[:half], 1), across(left[half:], 2)]
        pieces = (1, 1, 1, 2)
    else:
        spreads = [spread] + [across(spread, s) for s in range(1, ways)]
        pieces = (1,) * ways
    hidden_mid = col_phase(hidden_packed)
    grad_kept, grad_sent, own_back = call(
        terms_kernel,
        out_shape=(shape(width, width), shape(width, width), shape(rows, width, F32)),
        in_specs=[SMEM] + [VMEM] * 4,
        out_specs=(VMEM,) * 3,
        cost_estimate=cost(6 * slab * width, 2 * slab * 9),
        mib=LARGE,
        name="terms",
    )(core, x_node, agg, slopes, self_weight)
    *spreads, own_back, grad_kept, grad_sent = lax.optimization_barrier((*spreads, own_back, grad_kept, grad_sent))
    back_own, back_other = call(
        functools.partial(spmm_back_kernel, ways, halves, pieces),
        grid_spec=pltpu.PrefetchScalarGridSpec(
            num_scalar_prefetch=3,
            grid=(halves, depth),
            in_specs=[piece_spec(p, count) for count in pieces for p in range(count)] + [ANY],
            out_specs=[ANY] * 2,
            scratch_shapes=[
                pltpu.VMEM((cell_rows, part), F32),
                pltpu.VMEM((halves, cell_rows, part), BF),
                masks_scratch,
                x_sems,
                mask_sems,
            ],
        ),
        out_shape=[shape(cell_rows // 2, width)] * 2,
        cost_estimate=cost(spmm_flops, 2 * masks.size + 2 * cell_rows * width + 2 * ways * slab),
        mib=LARGE,
        name="spmm_back",
    )(cols, groups, core, *spreads, masks)
    back_other, hidden_mid = lax.optimization_barrier((back_other, hidden_mid))
    back = (back_own.astype(F32) + swap(back_other).astype(F32)).astype(BF)
    back, hidden_mid, grad_sent = lax.optimization_barrier((back, hidden_mid, grad_sent))
    neigh_back = lax.psum_scatter(back, "col", scatter_dimension=0, axis_index_groups=same_core, tiled=True)
    hidden_in = row_phase(turn(hidden_mid, col_devices, row_devices))
    pieces = split_sum(groups, [grad_kept, swap(grad_sent)], ways)
    pieces = split_sum(others, [pieces[0]] + [across(pieces[s], s) for s in range(1, ways)], lines)
    scale = 1.0 / math.sqrt(rows * devices)
    zero = jnp.zeros((1,), jnp.int32)
    (mine,) = split_sum(zero, [pieces[0]] + [along(pieces[s], s) for s in range(1, lines)], 1, scale)
    in_line = in_place(others, [mine] + [along(mine, s) for s in range(1, lines)])
    own_back, in_line = lax.optimization_barrier((own_back, in_line))
    grad_half = in_place(groups, [in_line] + [across(in_line, s) for s in range(1, ways)])
    grad_self, grad_neigh = call(
        final_kernel,
        in_specs=[SMEM] + [VMEM] * 2,
        out_specs=(VMEM,) * 2,
        out_shape=(shape(width, width, F32),) * 2,
        cost_estimate=cost(0, 12 * width * width),
        name="final",
    )(core, grad_half, swap(grad_half))
    grad_packed = call(
        join_kernel,
        out_shape=shape(slots, width),
        in_specs=[VMEM] * 3,
        out_specs=VMEM,
        cost_estimate=cost(2 * slots * slab, 8 * slab),
        name="join_pack",
    )(own_back, neigh_back, node_row)
    grad_in = relay(grad_packed)

    def unpack_own(value):
        return call(
            unpack_kernel,
            out_shape=shape(rows, width),
            in_specs=[VMEM] * 2,
            out_specs=VMEM,
            cost_estimate=cost(2 * slots * slab, 6 * slab),
            name="unpack_owner",
        )(own_col, value)

    hidden_own = unpack_own(hidden_in)
    grad_own = unpack_own(grad_in)
    return (hidden_own, grad_own, grad_self, grad_neigh)


def solution(mesh):
    placed = (
        P(("row", "col"), None),
        P("row", "col", None, None),
        P("row", "col", None, None, None, None),
        P(("row", "col")),
        P(("row", "col")),
        P(("row", "col")),
        P(),
        P(),
        P(("row", "col"), None),
    )
    return jax.shard_map(
        on_device,
        mesh=mesh,
        in_specs=placed,
        out_specs=(P(("row", "col"), None), P(("row", "col"), None), P(), P()),
        check_vma=False,
    )
```

```python
import functools
import math

import jax
import jax.numpy as jnp
from jax import lax
from jax.experimental import pallas as pl
from jax.experimental.pallas import tpu as pltpu
from jax.sharding import PartitionSpec as P

BF = jnp.bfloat16
F32 = jnp.float32
VMEM = pl.BlockSpec(memory_space=pltpu.VMEM)
MIB = 1024 * 1024
LARGE = 56


def params(mib=16):
    return pltpu.CompilerParams(vmem_limit_bytes=int(mib * MIB))


def cost(flops, nbytes):
    return pl.CostEstimate(flops=int(flops), bytes_accessed=int(nbytes), transcendentals=0)


def dot(a, b, ca=1, cb=0):
    return lax.dot_general(a, b, (((ca,), (cb,)), ((), ())), preferred_element_type=F32)


def as_column(row):
    return jnp.broadcast_to(row, (128, row.shape[1])).T


def block_of(index, size):
    if size & (size - 1) == 0:
        return lax.shift_right_logical(index, size.bit_length() - 1)
    return lax.div(index, jnp.full_like(index, size))


def rank_row(group_row, order_row):
    n = group_row.shape[1]
    group_col = as_column(group_row)[:, :1]
    order_col = as_column(order_row)[:, :1]
    earlier = (group_col == group_row) & (order_col < order_row)
    return jnp.sum(jnp.where(earlier, 1.0, 0.0), axis=0, keepdims=True).astype(jnp.int32)


def slots_onehot(flat_row, slots):
    iota = lax.broadcasted_iota(jnp.int32, (slots, flat_row.shape[1]), 0)
    return jnp.where(iota == flat_row, 1.0, 0.0).astype(BF)


def entries_onehot(flat_col, slots):
    iota = lax.broadcasted_iota(jnp.int32, (flat_col.shape[0], slots), 1)
    return jnp.where(flat_col[:, :1] == iota, 1.0, 0.0).astype(BF)


def own_slots(nodes_row, cap):
    n = nodes_row.shape[1]
    dest = block_of(nodes_row, n)
    rank = rank_row(dest, lax.broadcasted_iota(jnp.int32, (1, n), 1))
    return dest, rank


def pack_kernel(cap, nodes_ref, value_ref, out_ref):
    dest, rank = own_slots(nodes_ref[...], cap)
    out_ref[...] = dot(slots_onehot(dest * cap + rank, out_ref.shape[0]), value_ref[...]).astype(BF)


def index_kernel(
    cap, ways, nodes_ref, position_ref, degree_ref, cot_ref, cot_out, own_col, node_row, node_col, turned_row, turned_col
):
    n = nodes_ref.shape[1]
    width = cot_ref.shape[1]
    dest, rank = own_slots(nodes_ref[...], cap)
    flat = dest * cap + rank
    own_col[...] = as_column(flat)
    packing = slots_onehot(flat, cot_out.shape[0])
    cot_out[:, :width] = dot(packing, cot_ref[...]).astype(BF)
    cot_out[:, width:] = dot(packing, as_column(degree_ref[...].astype(F32)).astype(BF)).astype(BF)
    position = position_ref[...]
    source = block_of(position, n)
    rank = rank_row(source, position)
    place = source * cap + rank
    node_row[...] = jnp.broadcast_to(place, node_row.shape)
    node_col[...] = as_column(place)
    across = cot_out.shape[0] // (cap * ways)
    down = block_of(source, across)
    turned = ((source - down * across) * ways + down) * cap + rank
    turned_row[...] = jnp.broadcast_to(turned, turned_row.shape)
    turned_col[...] = as_column(turned)


def unpack_kernel(col_ref, value_ref, out_ref):
    out_ref[...] = dot(entries_onehot(col_ref[...], value_ref.shape[0]), value_ref[...]).astype(BF)


def spmm_kernel(ways, cols_ref, group_ref, x_ref, *refs):
    masks, outs = refs[:ways], refs[ways:]
    q = pl.program_id(0)
    depth = pl.num_programs(0)
    _, breadth, tile, _ = masks[0].shape
    for s in range(ways):
        base = (group_ref[s] * depth + q) * breadth
        total = None
        for p in range(0, breadth, 2):
            span = range(p, min(p + 2, breadth))
            left = jnp.concatenate([masks[s][0, k] for k in span], axis=1)
            right = jnp.concatenate(
                [x_ref[pl.ds(pl.multiple_of(cols_ref[base + k] * tile, tile), tile), :] for k in span], axis=0
            )
            term = dot(left, right)
            total = term if total is None else total + term
        outs[s][...] = total.astype(BF)


def load_masks(group_ref, masks_hbm, masks_ref, sems, ways, depth, q):
    return [
        pltpu.make_async_copy(masks_hbm.at[group_ref[s] * depth + q], masks_ref.at[q * ways + s], sems.at[q * ways + s])
        for s in range(ways)
    ]


def spmm_back_kernel(ways, pieces, cols_ref, group_ref, *refs):
    given = sum(pieces)
    spreads = refs[:given]
    masks_hbm, out_hbm, total, ready, masks_ref, sems, mask_sems = refs[given:]
    h, q = pl.program_id(0), pl.program_id(1)
    halves, depth = sems.shape[0], pl.num_programs(1)
    steps = masks_ref.shape[0] // ways
    _, breadth, tile, _ = masks_ref.shape
    part = total.shape[0]
    blocks, _, rows = out_hbm.shape

    @pl.when((h == 0) & (q == 0))
    def _():
        for step in range(steps):
            for copy in load_masks(group_ref, masks_hbm, masks_ref, mask_sems, ways, steps, step):
                copy.start()

    @pl.when(q == 0)
    def _():
        total[...] = jnp.zeros_like(total)

    for step in range(steps):

        @pl.when((h == 0) & (q == step))
        def _():
            for copy in load_masks(group_ref, masks_hbm, masks_ref, mask_sems, ways, steps, step):
                copy.wait()

    at_piece = 0
    for s in range(ways):
        row = group_ref[s] * depth + q
        left = spreads[at_piece][...]
        for p in range(1, pieces[s]):
            left = jnp.where(h >= p, spreads[at_piece + p][...], left)
        at_piece += pieces[s]
        for p in range(0, breadth, 2):
            span = range(p, min(p + 2, breadth))
            term = dot(left, jnp.concatenate([masks_ref[q * ways + s, k] for k in span], axis=1))
            for k in span:
                at = pl.ds(pl.multiple_of(cols_ref[row * breadth + k] * tile, tile), tile)
                total[:, at] += term[:, (k - p) * tile : (k - p + 1) * tile]

    for half in range(halves):
        store = pltpu.make_async_copy(ready.at[half], out_hbm.at[:, pl.ds(half * part, part), :], sems.at[half])

        @pl.when((h == half) & (q == depth - 1))
        def _():
            for block in range(blocks):
                ready[half, block] = total[:, block * rows : (block + 1) * rows].astype(BF)
            store.start()

        @pl.when((h == halves - 1) & (q == depth - 1))
        def _():
            store.wait()


def pass_on_kernel(left_ref, right_ref, top_ref, bottom_ref, left_out, right_out):
    half = top_ref.shape[0]
    left_out[:half, :] = left_ref[:half, :]
    left_out[half:, :] = (left_ref[half:, :].astype(F32) + bottom_ref[...].astype(F32)).astype(BF)
    right_out[:half, :] = (right_ref[:half, :].astype(F32) + top_ref[...].astype(F32)).astype(BF)
    right_out[half:, :] = right_ref[half:, :]


def layer_kernel(ways, *refs):
    terms = refs[:ways]
    (x_ref, cot_ref, col_ref, row_ref, self_ref, neigh_ref, packed_out, slopes_out, agg_out, spread_out) = refs[ways:]
    width = x_ref.shape[1]
    summed = terms[0][...].astype(F32)
    for s in range(1, ways):
        summed = summed + terms[s][...].astype(F32)
    cot = dot(entries_onehot(col_ref[...], cot_ref.shape[0]), cot_ref[...])
    degrees = cot[:, width : width + 1]
    agg = (summed / degrees).astype(BF)
    agg_out[...] = agg
    preact = dot(x_ref[...], self_ref[...]) + dot(agg, neigh_ref[...])
    gate = jax.nn.sigmoid(preact)
    hidden = (preact * gate).astype(BF)
    slopes = (cot[:, :width] * gate * (1.0 + preact * (1.0 - gate))).astype(BF)
    slopes_out[...] = slopes
    degree_row = jnp.broadcast_to(degrees, (degrees.shape[0], 128)).T[:1]
    spread_out[...] = (dot(neigh_ref[...], slopes, 1, 1) / degree_row).astype(BF)
    packed_out[...] = dot(slots_onehot(row_ref[...][:1], packed_out.shape[0]), hidden).astype(BF)


def terms_kernel(core_ref, x_ref, agg_ref, slopes_ref, self_ref, kept_out, sent_out, back_out):
    slopes = slopes_ref[...]
    back_out[...] = dot(self_ref[...], slopes, 1, 1)
    grad_self = dot(x_ref[...], slopes, 0, 0).astype(BF)
    grad_neigh = dot(agg_ref[...], slopes, 0, 0).astype(BF)
    first = core_ref[0] == 0
    kept_out[...] = jnp.where(first, grad_self, grad_neigh)
    sent_out[...] = jnp.where(first, grad_neigh, grad_self)


def split_sum_kernel(count, scale, index_ref, *refs):
    terms, outs, total_ref = refs[:count], refs[count:-1], refs[-1]
    total = terms[0][...].astype(F32)
    for term in terms[1:]:
        total = total + term[...].astype(F32)
    total_ref[...] = total * scale
    size = outs[0].shape[0]
    for s, out in enumerate(outs):
        out[...] = total_ref[pl.ds(pl.multiple_of(index_ref[s] * size, size), size), :].astype(out.dtype)


def place_kernel(index_ref, *refs):
    out_ref = refs[-1]
    for s, part in enumerate(refs[:-1]):
        out_ref[index_ref[s]] = part[...].astype(out_ref.dtype)


def final_kernel(core_ref, kept_ref, came_ref, self_out, neigh_out):
    first = core_ref[0] == 0
    kept, came = kept_ref[...].astype(F32), came_ref[...].astype(F32)
    self_out[...] = jnp.where(first, kept, came)
    neigh_out[...] = jnp.where(first, came, kept)


def join_kernel(own_ref, neigh_ref, row_ref, out_ref):
    joined = (own_ref[...] + neigh_ref[...].astype(F32)).astype(BF)
    out_ref[...] = dot(slots_onehot(row_ref[...][:1], out_ref.shape[0]), joined, 1, 1).astype(BF)


def on_device(
    features,
    tile_cols,
    tile_masks,
    degree,
    owner_nodes,
    owner_position,
    self_weight,
    neigh_weight,
    cotangent,
):
    rows, width = features.shape
    row_devices = lax.axis_size("row")
    col_devices = lax.axis_size("col")
    devices = row_devices * col_devices
    cap = 2 * rows // devices
    slots = devices * cap
    masks = tile_masks[0, 0]
    tile = masks.shape[-1]
    breadth = masks.shape[1]
    depth = rows // tile
    ring = [list(range(0, col_devices, 2)) + list(range(1, col_devices, 2))[::-1]]
    cols = tile_cols[0, 0].reshape(-1)
    block = lax.div(cols, depth)
    pair = lax.div(block, 2)
    cols = jnp.where(block == 2 * pair, pair, col_devices - 1 - pair) * depth + lax.rem(cols, depth)
    me = lax.axis_index("row")
    ways = row_devices
    groups = jnp.bitwise_xor(me, jnp.arange(ways, dtype=jnp.int32)).astype(jnp.int32)
    everyone = ("row", "col")
    place = lax.axis_index("col")
    lines = col_devices // 2
    core = jnp.full((1,), lax.rem(place, 2), jnp.int32)
    others = jnp.bitwise_xor(lax.div(place, 2), jnp.arange(lines, dtype=jnp.int32)).astype(jnp.int32)
    SMEM = pl.BlockSpec(memory_space=pltpu.SMEM)

    def call(*args, mib=16, **kwargs):
        return pl.pallas_call(*args, compiler_params=params(mib), **kwargs)

    def shape(r, c, dtype=BF):
        return jax.ShapeDtypeStruct((r, c), dtype)

    def relay(packed):
        there = packed.reshape(devices, cap, -1)
        return lax.all_to_all(there, everyone, split_axis=0, concat_axis=0, tiled=True).reshape(slots, -1)

    def row_phase(packed):
        there = packed.reshape(row_devices, col_devices * cap, -1)
        return lax.all_to_all(there, "row", split_axis=0, concat_axis=0, tiled=True).reshape(slots, -1)

    def col_phase(packed):
        there = packed.reshape(col_devices, row_devices * cap, -1)
        return lax.all_to_all(there, "col", split_axis=0, concat_axis=0, tiled=True).reshape(slots, -1)

    def turn(packed, first, second):
        return packed.reshape(first, second, cap, -1).transpose(1, 0, 2, 3).reshape(slots, -1)

    def across(value, s):
        return lax.ppermute(value, "row", [(i, i ^ s) for i in range(ways)])

    def along(value, s):
        return lax.ppermute(value, "col", [(i, i ^ (2 * s)) for i in range(col_devices)])

    def swap(value):
        return lax.ppermute(value, "col", [(i, i ^ 1) for i in range(col_devices)])

    def split_sum(index, arrays, pieces, scale=1.0):
        r, c = arrays[0].shape
        return call(
            functools.partial(split_sum_kernel, len(arrays), scale),
            in_specs=[SMEM] + [VMEM] * len(arrays),
            out_specs=[VMEM] * pieces,
            out_shape=[shape(r // pieces, c) for _ in range(pieces)],
            scratch_shapes=[pltpu.VMEM((r, c), F32)],
            cost_estimate=cost(r * c * len(arrays), 2 * r * c * (len(arrays) + 1)),
            name="split_sum",
        )(index, *arrays)

    def in_place(index, arrays):
        count, (r, c) = len(arrays), arrays[0].shape
        return call(
            place_kernel,
            in_specs=[SMEM] + [VMEM] * count,
            out_specs=VMEM,
            out_shape=jax.ShapeDtypeStruct((count, r, c), BF),
            cost_estimate=cost(0, 4 * count * r * c),
            name="in_place",
        )(index, *arrays).reshape(count * r, c)

    nodes = owner_nodes.reshape(1, rows)
    slab = rows * width
    packed = call(
        functools.partial(pack_kernel, cap),
        out_shape=shape(slots, width),
        in_specs=[VMEM] * 2,
        out_specs=VMEM,
        cost_estimate=cost(2 * slots * slab, 6 * slab),
        mib=LARGE,
        name="pack_features",
    )(nodes, features)
    inbound = relay(packed)
    cot_packed, own_col, node_row, node_col, turned_row, turned_col = call(
        functools.partial(index_kernel, cap, ways),
        out_shape=(
            shape(slots, width + 128),
            shape(rows, 128, jnp.int32),
            shape(8, rows, jnp.int32),
            shape(rows, 128, jnp.int32),
            shape(8, rows, jnp.int32),
            shape(rows, 128, jnp.int32),
        ),
        in_specs=[VMEM] * 4,
        out_specs=(VMEM,) * 6,
        cost_estimate=cost(2 * slots * slab, 6 * slab),
        mib=LARGE,
        name="index_cotangent",
    )(nodes, owner_position.reshape(1, rows), degree.reshape(1, rows), cotangent)
    ANY = pl.BlockSpec(memory_space=pl.ANY)
    x_node = call(
        unpack_kernel,
        out_shape=shape(rows, width),
        in_specs=[VMEM] * 2,
        out_specs=VMEM,
        cost_estimate=cost(2 * slots * slab, 6 * slab),
        name="unpack_features",
    )(node_col, inbound)
    cot_packed, x_node, cols, groups, core, others = lax.optimization_barrier(
        (cot_packed, x_node, cols, groups, core, others)
    )
    x_cols = lax.all_gather(x_node, "col", axis_index_groups=ring, axis=0, tiled=True)
    cot_mid = turn(row_phase(cot_packed), row_devices, col_devices)
    x_cols, cot_mid = lax.optimization_barrier((x_cols, cot_mid))
    cot_in = col_phase(cot_mid)

    spmm_flops = 2 * masks.size * width
    halves = 2
    part = width // halves
    def mask_spec(s):
        return pl.BlockSpec((1, breadth, tile, tile), lambda q, c, g: (g[s] * depth + q, 0, 0, 0))

    partials = call(
        functools.partial(spmm_kernel, ways),
        grid_spec=pltpu.PrefetchScalarGridSpec(
            num_scalar_prefetch=2,
            grid=(depth,),
            in_specs=[VMEM] + [mask_spec(s) for s in range(ways)],
            out_specs=[pl.BlockSpec((tile, width), lambda q, c, g: (q, 0)) for s in range(ways)],
        ),
        out_shape=[shape(rows, width) for s in range(ways)],
        cost_estimate=cost(spmm_flops, 2 * masks.size + 2 * x_cols.size + 2 * ways * slab),
        mib=LARGE,
        name="spmm",
    )(cols, groups, x_cols, *([masks] * ways))
    if ways == 4:
        half = rows // 2
        top = across(partials[3][:half], 1)
        bottom = across(partials[3][half:], 2)
        left, right = call(
            pass_on_kernel,
            out_shape=(shape(rows, width),) * 2,
            in_specs=[VMEM] * 4,
            out_specs=(VMEM,) * 2,
            cost_estimate=cost(2 * slab, 10 * slab),
            name="pass_on",
        )(partials[1], partials[2], top, bottom)
        terms = [partials[0], across(left, 1), across(right, 2)]
    else:
        terms = [partials[0]] + [across(partials[s], s) for s in range(1, ways)]
    hidden_packed, slopes, agg, spread = call(
        functools.partial(layer_kernel, len(terms)),
        out_shape=(shape(slots, width),) + (shape(rows, width),) * 2 + (shape(width, rows),),
        in_specs=[VMEM] * (len(terms) + 6),
        out_specs=(VMEM,) * 4,
        cost_estimate=cost(10 * slab * width, 2 * slab * (ways + 9)),
        mib=LARGE,
        name="layer",
    )(*terms, x_node, cot_in, turned_col, turned_row, self_weight, neigh_weight)
    if ways == 4:
        left, right = across(spread, 1), across(spread, 2)
        spreads = [spread, left, right, across(right[:part], 1), across(left[part:], 2)]
        pieces = (1, 1, 1, 2)
    else:
        spreads = [spread] + [across(spread, s) for s in range(1, ways)]
        pieces = (1,) * ways
    hidden_mid = col_phase(hidden_packed)
    grad_kept, grad_sent, own_back = call(
        terms_kernel,
        out_shape=(shape(width, width), shape(width, width), shape(width, rows, F32)),
        in_specs=[SMEM] + [VMEM] * 4,
        out_specs=(VMEM,) * 3,
        cost_estimate=cost(6 * slab * width, 2 * slab * 9),
        mib=LARGE,
        name="terms",
    )(core, x_node, agg, slopes, self_weight)
    *spreads, own_back, grad_kept, grad_sent = lax.optimization_barrier((*spreads, own_back, grad_kept, grad_sent))
    back = call(
        functools.partial(spmm_back_kernel, ways, pieces),
        grid_spec=pltpu.PrefetchScalarGridSpec(
            num_scalar_prefetch=2,
            grid=(halves, depth),
            in_specs=[
                pl.BlockSpec((part, tile), (lambda h, q, *_: (h, q)) if count == 1 else (lambda h, q, *_: (0, q)))
                for count in pieces
                for _ in range(count)
            ]
            + [ANY],
            out_specs=ANY,
            scratch_shapes=[
                pltpu.VMEM((part, x_cols.shape[0]), F32),
                pltpu.VMEM((halves, col_devices, part, rows), BF),
                pltpu.VMEM(masks.shape, BF),
                pltpu.SemaphoreType.DMA((halves,)),
                pltpu.SemaphoreType.DMA((masks.shape[0],)),
            ],
        ),
        out_shape=jax.ShapeDtypeStruct((col_devices, width, rows), BF),
        cost_estimate=cost(spmm_flops, 2 * masks.size + 2 * x_cols.size + 2 * ways * slab),
        mib=LARGE,
        name="spmm_back",
    )(cols, groups, *spreads, masks)
    back, hidden_mid, grad_sent = lax.optimization_barrier((back, hidden_mid, grad_sent))
    neigh_back = lax.psum_scatter(
        back.reshape(-1, rows), "col", scatter_dimension=0, axis_index_groups=ring, tiled=True
    )
    hidden_in = row_phase(turn(hidden_mid, col_devices, row_devices))
    pieces = split_sum(groups, [grad_kept, swap(grad_sent)], ways)
    pieces = split_sum(others, [pieces[0]] + [across(pieces[s], s) for s in range(1, ways)], lines)
    scale = 1.0 / math.sqrt(rows * devices)
    zero = jnp.zeros((1,), jnp.int32)
    (mine,) = split_sum(zero, [pieces[0]] + [along(pieces[s], s) for s in range(1, lines)], 1, scale)
    in_line = in_place(others, [mine] + [along(mine, s) for s in range(1, lines)])
    own_back, in_line = lax.optimization_barrier((own_back, in_line))
    grad_half = in_place(groups, [in_line] + [across(in_line, s) for s in range(1, ways)])
    grad_self, grad_neigh = call(
        final_kernel,
        in_specs=[SMEM] + [VMEM] * 2,
        out_specs=(VMEM,) * 2,
        out_shape=(shape(width, width, F32),) * 2,
        cost_estimate=cost(0, 12 * width * width),
        name="final",
    )(core, grad_half, swap(grad_half))
    grad_packed = call(
        join_kernel,
        out_shape=shape(slots, width),
        in_specs=[VMEM] * 3,
        out_specs=VMEM,
        cost_estimate=cost(2 * slots * slab, 8 * slab),
        name="join_pack",
    )(own_back, neigh_back, node_row)
    grad_in = relay(grad_packed)

    def unpack_own(value):
        return call(
            unpack_kernel,
            out_shape=shape(rows, width),
            in_specs=[VMEM] * 2,
            out_specs=VMEM,
            cost_estimate=cost(2 * slots * slab, 6 * slab),
            name="unpack_owner",
        )(own_col, value)

    hidden_own = unpack_own(hidden_in)
    grad_own = unpack_own(grad_in)
    return (hidden_own, grad_own, grad_self, grad_neigh)


def solution(mesh):
    placed = (
        P(("row", "col"), None),
        P("row", "col", None, None),
        P("row", "col", None, None, None, None),
        P(("row", "col")),
        P(("row", "col")),
        P(("row", "col")),
        P(),
        P(),
        P(("row", "col"), None),
    )
    return jax.shard_map(
        on_device,
        mesh=mesh,
        in_specs=placed,
        out_specs=(P(("row", "col"), None), P(("row", "col"), None), P(), P()),
        check_vma=False,
    )
```

```python
import functools
import math

import jax
import jax.numpy as jnp
from jax import lax
from jax.experimental import pallas as pl
from jax.experimental.pallas import tpu as pltpu
from jax.sharding import PartitionSpec as P

BF = jnp.bfloat16
F32 = jnp.float32
VMEM = pl.BlockSpec(memory_space=pltpu.VMEM)
MIB = 1024 * 1024
LARGE = 56


def params(mib=16):
    return pltpu.CompilerParams(vmem_limit_bytes=int(mib * MIB))


def cost(flops, nbytes):
    return pl.CostEstimate(flops=int(flops), bytes_accessed=int(nbytes), transcendentals=0)


def dot(a, b, ca=1, cb=0):
    return lax.dot_general(a, b, (((ca,), (cb,)), ((), ())), preferred_element_type=F32)


def as_column(row):
    return jnp.broadcast_to(row, (128, row.shape[1])).T


def block_of(index, size):
    if size & (size - 1) == 0:
        return lax.shift_right_logical(index, size.bit_length() - 1)
    return lax.div(index, jnp.full_like(index, size))


def rank_row(group_row, order_row):
    n = group_row.shape[1]
    group_col = as_column(group_row)[:, :1]
    order_col = as_column(order_row)[:, :1]
    earlier = (group_col == group_row) & (order_col < order_row)
    return jnp.sum(jnp.where(earlier, 1.0, 0.0), axis=0, keepdims=True).astype(jnp.int32)


def slots_onehot(flat_row, slots):
    iota = lax.broadcasted_iota(jnp.int32, (slots, flat_row.shape[1]), 0)
    return jnp.where(iota == flat_row, 1.0, 0.0).astype(BF)


def entries_onehot(flat_col, slots):
    iota = lax.broadcasted_iota(jnp.int32, (flat_col.shape[0], slots), 1)
    return jnp.where(flat_col[:, :1] == iota, 1.0, 0.0).astype(BF)


def own_slots(nodes_row, cap):
    n = nodes_row.shape[1]
    dest = block_of(nodes_row, n)
    rank = rank_row(dest, lax.broadcasted_iota(jnp.int32, (1, n), 1))
    return dest, rank


def pack_kernel(cap, nodes_ref, value_ref, out_ref):
    dest, rank = own_slots(nodes_ref[...], cap)
    out_ref[...] = dot(slots_onehot(dest * cap + rank, out_ref.shape[0]), value_ref[...]).astype(BF)


def index_kernel(
    cap, ways, nodes_ref, position_ref, degree_ref, cot_ref, cot_out, own_col, node_row, node_col, turned_row, turned_col
):
    n = nodes_ref.shape[1]
    width = cot_ref.shape[1]
    dest, rank = own_slots(nodes_ref[...], cap)
    flat = dest * cap + rank
    own_col[...] = as_column(flat)
    packing = slots_onehot(flat, cot_out.shape[0])
    cot_out[:, :width] = dot(packing, cot_ref[...]).astype(BF)
    cot_out[:, width:] = dot(packing, as_column(degree_ref[...].astype(F32)).astype(BF)).astype(BF)
    position = position_ref[...]
    source = block_of(position, n)
    rank = rank_row(source, position)
    place = source * cap + rank
    node_row[...] = jnp.broadcast_to(place, node_row.shape)
    node_col[...] = as_column(place)
    across = cot_out.shape[0] // (cap * ways)
    down = block_of(source, across)
    turned = ((source - down * across) * ways + down) * cap + rank
    turned_row[...] = jnp.broadcast_to(turned, turned_row.shape)
    turned_col[...] = as_column(turned)


def unpack_kernel(col_ref, value_ref, out_ref):
    out_ref[...] = dot(entries_onehot(col_ref[...], value_ref.shape[0]), value_ref[...]).astype(BF)


def spmm_kernel(pieces, cols_ref, group_ref, x_ref, *refs):
    ways = len(pieces)
    masks, outs = refs[:ways], refs[ways:]
    q = pl.program_id(0)
    depth = pl.num_programs(0)
    _, breadth, tile, _ = masks[0].shape
    at_piece = 0
    for s in range(ways):
        base = (group_ref[s] * depth + q) * breadth
        total = None
        for p in range(0, breadth, 2):
            span = range(p, min(p + 2, breadth))
            left = jnp.concatenate([masks[s][0, k] for k in span], axis=1)
            right = jnp.concatenate(
                [x_ref[pl.ds(pl.multiple_of(cols_ref[base + k] * tile, tile), tile), :] for k in span], axis=0
            )
            term = dot(left, right)
            total = term if total is None else total + term
        for p in range(pieces[s]):
            out_ref = outs[at_piece + p]

            @pl.when((q * pieces[s] >= p * depth) & (q * pieces[s] < (p + 1) * depth))
            def _():
                out_ref[...] = total.astype(BF)

        at_piece += pieces[s]


def spmm_back_kernel(ways, pieces, cols_ref, group_ref, *refs):
    given = sum(pieces)
    spreads, masks = refs[:given], refs[given : given + ways]
    out_hbm, total, ready, sems = refs[given + ways :]
    q = pl.program_id(0)
    depth = pl.num_programs(0)
    _, breadth, tile, _ = masks[0].shape

    @pl.when(q == 0)
    def _():
        total[...] = jnp.zeros_like(total)

    at_piece = 0
    for s in range(ways):
        base = (group_ref[s] * depth + q) * breadth
        rows = spreads[at_piece][...]
        for p in range(1, pieces[s]):
            rows = jnp.where(q * pieces[s] >= p * depth, spreads[at_piece + p][...], rows)
        at_piece += pieces[s]
        for k in range(breadth):
            at = pl.ds(pl.multiple_of(cols_ref[base + k] * tile, tile), tile)
            total[at, :] += dot(masks[s][0, k], rows, 0, 0)

    @pl.when(q == depth - 1)
    def _():
        count = sems.shape[0]
        share = total.shape[0] // count
        copies = []
        for i in range(count):
            at = pl.ds(i * share, share)
            ready[at, :] = total[at, :].astype(BF)
            copies.append(pltpu.make_async_copy(ready.at[at], out_hbm.at[at], sems.at[i]))
            copies[-1].start()
        for copy in copies:
            copy.wait()


def pass_on_kernel(left_ref, right_ref, top_ref, bottom_ref, left_out, right_out):
    half = top_ref.shape[0]
    left_out[:half, :] = left_ref[:half, :]
    left_out[half:, :] = (left_ref[half:, :].astype(F32) + bottom_ref[...].astype(F32)).astype(BF)
    right_out[:half, :] = (right_ref[:half, :].astype(F32) + top_ref[...].astype(F32)).astype(BF)
    right_out[half:, :] = right_ref[half:, :]


def layer_kernel(ways, *refs):
    terms = refs[:ways]
    (x_ref, cot_ref, col_ref, row_ref, self_ref, neigh_ref, packed_out, slopes_out, agg_out, spread_out) = refs[ways:]
    width = x_ref.shape[1]
    summed = terms[0][...].astype(F32)
    for s in range(1, ways):
        summed = summed + terms[s][...].astype(F32)
    cot = dot(entries_onehot(col_ref[...], cot_ref.shape[0]), cot_ref[...])
    degrees = cot[:, width : width + 1]
    agg = (summed / degrees).astype(BF)
    agg_out[...] = agg
    preact = dot(x_ref[...], self_ref[...]) + dot(agg, neigh_ref[...])
    gate = jax.nn.sigmoid(preact)
    hidden = (preact * gate).astype(BF)
    slopes = (cot[:, :width] * gate * (1.0 + preact * (1.0 - gate))).astype(BF)
    slopes_out[...] = slopes
    spread_out[...] = (dot(slopes, neigh_ref[...], 1, 1) / degrees).astype(BF)
    packed_out[...] = dot(slots_onehot(row_ref[...][:1], packed_out.shape[0]), hidden).astype(BF)


def terms_kernel(core_ref, x_ref, agg_ref, slopes_ref, self_ref, kept_out, sent_out, back_out):
    slopes = slopes_ref[...]
    back_out[...] = dot(slopes, self_ref[...], 1, 1)
    grad_self = dot(x_ref[...], slopes, 0, 0).astype(BF)
    grad_neigh = dot(agg_ref[...], slopes, 0, 0).astype(BF)
    first = core_ref[0] == 0
    kept_out[...] = jnp.where(first, grad_self, grad_neigh)
    sent_out[...] = jnp.where(first, grad_neigh, grad_self)


def split_sum_kernel(count, scale, index_ref, *refs):
    terms, outs, total_ref = refs[:count], refs[count:-1], refs[-1]
    total = terms[0][...].astype(F32)
    for term in terms[1:]:
        total = total + term[...].astype(F32)
    total_ref[...] = total * scale
    size = outs[0].shape[0]
    for s, out in enumerate(outs):
        out[...] = total_ref[pl.ds(pl.multiple_of(index_ref[s] * size, size), size), :].astype(out.dtype)


def place_kernel(index_ref, *refs):
    out_ref = refs[-1]
    for s, part in enumerate(refs[:-1]):
        out_ref[index_ref[s]] = part[...].astype(out_ref.dtype)


def final_kernel(core_ref, kept_ref, came_ref, self_out, neigh_out):
    first = core_ref[0] == 0
    kept, came = kept_ref[...].astype(F32), came_ref[...].astype(F32)
    self_out[...] = jnp.where(first, kept, came)
    neigh_out[...] = jnp.where(first, came, kept)


def join_kernel(own_ref, neigh_ref, row_ref, out_ref):
    joined = (own_ref[...] + neigh_ref[...].astype(F32)).astype(BF)
    out_ref[...] = dot(slots_onehot(row_ref[...][:1], out_ref.shape[0]), joined).astype(BF)


def on_device(
    features,
    tile_cols,
    tile_masks,
    degree,
    owner_nodes,
    owner_position,
    self_weight,
    neigh_weight,
    cotangent,
):
    rows, width = features.shape
    row_devices = lax.axis_size("row")
    col_devices = lax.axis_size("col")
    devices = row_devices * col_devices
    cap = 2 * rows // devices
    slots = devices * cap
    masks = tile_masks[0, 0]
    tile = masks.shape[-1]
    breadth = masks.shape[1]
    depth = rows // tile
    cols = tile_cols[0, 0].reshape(-1)
    me = lax.axis_index("row")
    ways = row_devices
    groups = jnp.bitwise_xor(me, jnp.arange(ways, dtype=jnp.int32)).astype(jnp.int32)
    everyone = ("row", "col")
    place = lax.axis_index("col")
    lines = col_devices // 2
    core = jnp.full((1,), lax.rem(place, 2), jnp.int32)
    others = jnp.bitwise_xor(lax.div(place, 2), jnp.arange(lines, dtype=jnp.int32)).astype(jnp.int32)
    SMEM = pl.BlockSpec(memory_space=pltpu.SMEM)

    def call(*args, mib=16, **kwargs):
        return pl.pallas_call(*args, compiler_params=params(mib), **kwargs)

    def shape(r, c, dtype=BF):
        return jax.ShapeDtypeStruct((r, c), dtype)

    def relay(packed):
        there = packed.reshape(devices, cap, -1)
        return lax.all_to_all(there, everyone, split_axis=0, concat_axis=0, tiled=True).reshape(slots, -1)

    def row_phase(packed):
        there = packed.reshape(row_devices, col_devices * cap, -1)
        return lax.all_to_all(there, "row", split_axis=0, concat_axis=0, tiled=True).reshape(slots, -1)

    def col_phase(packed):
        there = packed.reshape(col_devices, row_devices * cap, -1)
        return lax.all_to_all(there, "col", split_axis=0, concat_axis=0, tiled=True).reshape(slots, -1)

    def turn(packed, first, second):
        return packed.reshape(first, second, cap, -1).transpose(1, 0, 2, 3).reshape(slots, -1)

    def across(value, s):
        return lax.ppermute(value, "row", [(i, i ^ s) for i in range(ways)])

    def along(value, s):
        return lax.ppermute(value, "col", [(i, i ^ (2 * s)) for i in range(col_devices)])

    def swap(value):
        return lax.ppermute(value, "col", [(i, i ^ 1) for i in range(col_devices)])

    def split_sum(index, arrays, pieces, scale=1.0):
        r, c = arrays[0].shape
        return call(
            functools.partial(split_sum_kernel, len(arrays), scale),
            in_specs=[SMEM] + [VMEM] * len(arrays),
            out_specs=[VMEM] * pieces,
            out_shape=[shape(r // pieces, c) for _ in range(pieces)],
            scratch_shapes=[pltpu.VMEM((r, c), F32)],
            cost_estimate=cost(r * c * len(arrays), 2 * r * c * (len(arrays) + 1)),
            name="split_sum",
        )(index, *arrays)

    def in_place(index, arrays):
        count, (r, c) = len(arrays), arrays[0].shape
        return call(
            place_kernel,
            in_specs=[SMEM] + [VMEM] * count,
            out_specs=VMEM,
            out_shape=jax.ShapeDtypeStruct((count, r, c), BF),
            cost_estimate=cost(0, 4 * count * r * c),
            name="in_place",
        )(index, *arrays).reshape(count * r, c)

    nodes = owner_nodes.reshape(1, rows)
    slab = rows * width
    packed = call(
        functools.partial(pack_kernel, cap),
        out_shape=shape(slots, width),
        in_specs=[VMEM] * 2,
        out_specs=VMEM,
        cost_estimate=cost(2 * slots * slab, 6 * slab),
        mib=LARGE,
        name="pack_features",
    )(nodes, features)
    inbound = relay(packed)
    cot_packed, own_col, node_row, node_col, turned_row, turned_col = call(
        functools.partial(index_kernel, cap, ways),
        out_shape=(
            shape(slots, width + 128),
            shape(rows, 128, jnp.int32),
            shape(8, rows, jnp.int32),
            shape(rows, 128, jnp.int32),
            shape(8, rows, jnp.int32),
            shape(rows, 128, jnp.int32),
        ),
        in_specs=[VMEM] * 4,
        out_specs=(VMEM,) * 6,
        cost_estimate=cost(2 * slots * slab, 6 * slab),
        mib=LARGE,
        name="index_cotangent",
    )(nodes, owner_position.reshape(1, rows), degree.reshape(1, rows), cotangent)
    ANY = pl.BlockSpec(memory_space=pl.ANY)
    x_node = call(
        unpack_kernel,
        out_shape=shape(rows, width),
        in_specs=[VMEM] * 2,
        out_specs=VMEM,
        cost_estimate=cost(2 * slots * slab, 6 * slab),
        name="unpack_features",
    )(node_col, inbound)
    cot_packed, x_node, cols, groups, core, others = lax.optimization_barrier(
        (cot_packed, x_node, cols, groups, core, others)
    )
    x_cols = lax.all_gather(x_node, "col", axis=0, tiled=True)
    cot_mid = turn(row_phase(cot_packed), row_devices, col_devices)
    x_cols, cot_mid = lax.optimization_barrier((x_cols, cot_mid))
    cot_in = col_phase(cot_mid)

    spmm_flops = 2 * masks.size * width
    def piece_spec(p, count):
        share = depth // count
        return pl.BlockSpec((tile, width), lambda q, c, g: (jnp.clip(q - p * share, 0, share - 1), 0))

    def mask_spec(s):
        return pl.BlockSpec((1, breadth, tile, tile), lambda q, c, g: (g[s] * depth + q, 0, 0, 0))

    pieces = (1, 1, 1, 2) if ways == 4 else (1,) * ways
    half = rows // 2
    partials = call(
        functools.partial(spmm_kernel, pieces),
        grid_spec=pltpu.PrefetchScalarGridSpec(
            num_scalar_prefetch=2,
            grid=(depth,),
            in_specs=[VMEM] + [mask_spec(s) for s in range(ways)],
            out_specs=[piece_spec(p, count) for count in pieces for p in range(count)],
        ),
        out_shape=[shape(rows // count, width) for count in pieces for _ in range(count)],
        cost_estimate=cost(spmm_flops, 2 * masks.size + 2 * x_cols.size + 2 * ways * slab),
        mib=LARGE,
        name="spmm",
    )(cols, groups, x_cols, *([masks] * ways))
    if ways == 4:
        top, bottom = across(partials[3], 1), across(partials[4], 2)
        left, right = call(
            pass_on_kernel,
            out_shape=(shape(rows, width),) * 2,
            in_specs=[VMEM] * 4,
            out_specs=(VMEM,) * 2,
            cost_estimate=cost(2 * slab, 10 * slab),
            name="pass_on",
        )(partials[1], partials[2], top, bottom)
        terms = [partials[0], across(left, 1), across(right, 2)]
    else:
        terms = [partials[0]] + [across(partials[s], s) for s in range(1, ways)]
    hidden_packed, slopes, agg, spread = call(
        functools.partial(layer_kernel, len(terms)),
        out_shape=(shape(slots, width),) + (shape(rows, width),) * 3,
        in_specs=[VMEM] * (len(terms) + 6),
        out_specs=(VMEM,) * 4,
        cost_estimate=cost(10 * slab * width, 2 * slab * (ways + 9)),
        mib=LARGE,
        name="layer",
    )(*terms, x_node, cot_in, turned_col, turned_row, self_weight, neigh_weight)
    if ways == 4:
        left, right = across(spread, 1), across(spread, 2)
        spreads = [spread, left, right, across(right[:half], 1), across(left[half:], 2)]
    else:
        spreads = [spread] + [across(spread, s) for s in range(1, ways)]
    hidden_mid = col_phase(hidden_packed)
    grad_kept, grad_sent, own_back = call(
        terms_kernel,
        out_shape=(shape(width, width), shape(width, width), shape(rows, width, F32)),
        in_specs=[SMEM] + [VMEM] * 4,
        out_specs=(VMEM,) * 3,
        cost_estimate=cost(6 * slab * width, 2 * slab * 9),
        mib=LARGE,
        name="terms",
    )(core, x_node, agg, slopes, self_weight)
    *spreads, own_back, grad_kept, grad_sent = lax.optimization_barrier((*spreads, own_back, grad_kept, grad_sent))
    back = call(
        functools.partial(spmm_back_kernel, ways, pieces),
        grid_spec=pltpu.PrefetchScalarGridSpec(
            num_scalar_prefetch=2,
            grid=(depth,),
            in_specs=[piece_spec(p, count) for count in pieces for p in range(count)]
            + [mask_spec(s) for s in range(ways)],
            out_specs=ANY,
            scratch_shapes=[
                pltpu.VMEM(x_cols.shape, F32),
                pltpu.VMEM(x_cols.shape, BF),
                pltpu.SemaphoreType.DMA((col_devices,)),
            ],
        ),
        out_shape=shape(*x_cols.shape),
        cost_estimate=cost(spmm_flops, 2 * masks.size + 2 * x_cols.size + 2 * ways * slab),
        mib=LARGE,
        name="spmm_back",
    )(cols, groups, *spreads, *([masks] * ways))
    back, hidden_mid, grad_sent = lax.optimization_barrier((back, hidden_mid, grad_sent))
    neigh_back = lax.psum_scatter(back, "col", scatter_dimension=0, tiled=True)
    hidden_in = row_phase(turn(hidden_mid, col_devices, row_devices))
    pieces = split_sum(groups, [grad_kept, swap(grad_sent)], ways)
    pieces = split_sum(others, [pieces[0]] + [across(pieces[s], s) for s in range(1, ways)], lines)
    scale = 1.0 / math.sqrt(rows * devices)
    zero = jnp.zeros((1,), jnp.int32)
    (mine,) = split_sum(zero, [pieces[0]] + [along(pieces[s], s) for s in range(1, lines)], 1, scale)
    in_line = in_place(others, [mine] + [along(mine, s) for s in range(1, lines)])
    own_back, in_line = lax.optimization_barrier((own_back, in_line))
    grad_half = in_place(groups, [in_line] + [across(in_line, s) for s in range(1, ways)])
    grad_self, grad_neigh = call(
        final_kernel,
        in_specs=[SMEM] + [VMEM] * 2,
        out_specs=(VMEM,) * 2,
        out_shape=(shape(width, width, F32),) * 2,
        cost_estimate=cost(0, 12 * width * width),
        name="final",
    )(core, grad_half, swap(grad_half))
    grad_packed = call(
        join_kernel,
        out_shape=shape(slots, width),
        in_specs=[VMEM] * 3,
        out_specs=VMEM,
        cost_estimate=cost(2 * slots * slab, 8 * slab),
        name="join_pack",
    )(own_back, neigh_back, node_row)
    grad_in = relay(grad_packed)

    def unpack_own(value):
        return call(
            unpack_kernel,
            out_shape=shape(rows, width),
            in_specs=[VMEM] * 2,
            out_specs=VMEM,
            cost_estimate=cost(2 * slots * slab, 6 * slab),
            name="unpack_owner",
        )(own_col, value)

    hidden_own = unpack_own(hidden_in)
    grad_own = unpack_own(grad_in)
    return (hidden_own, grad_own, grad_self, grad_neigh)


def solution(mesh):
    placed = (
        P(("row", "col"), None),
        P("row", "col", None, None),
        P("row", "col", None, None, None, None),
        P(("row", "col")),
        P(("row", "col")),
        P(("row", "col")),
        P(),
        P(),
        P(("row", "col"), None),
    )
    return jax.shard_map(
        on_device,
        mesh=mesh,
        in_specs=placed,
        out_specs=(P(("row", "col"), None), P(("row", "col"), None), P(), P()),
        check_vma=False,
    )
```

```python
import functools
import math

import jax
import jax.numpy as jnp
from jax import lax
from jax.experimental import pallas as pl
from jax.experimental.pallas import tpu as pltpu
from jax.sharding import PartitionSpec as P

BF = jnp.bfloat16
F32 = jnp.float32
VMEM = pl.BlockSpec(memory_space=pltpu.VMEM)
MIB = 1024 * 1024
LARGE = 56
WEIGHT = 6


def params(mib=16):
    return pltpu.CompilerParams(vmem_limit_bytes=int(mib * MIB))


def cost(flops, nbytes):
    return pl.CostEstimate(flops=int(flops), bytes_accessed=int(nbytes), transcendentals=0)


def dot(a, b, ca=1, cb=0):
    return lax.dot_general(a, b, (((ca,), (cb,)), ((), ())), preferred_element_type=F32)


def as_column(row):
    return jnp.broadcast_to(row, (128, row.shape[1])).T


def block_of(index, size):
    if size & (size - 1) == 0:
        return lax.shift_right_logical(index, size.bit_length() - 1)
    return lax.div(index, jnp.full_like(index, size))


def rank_row(group_row, order_row):
    n = group_row.shape[1]
    group_col = as_column(group_row)[:, :1]
    order_col = as_column(order_row)[:, :1]
    earlier = (group_col == group_row) & (order_col < order_row)
    return jnp.sum(jnp.where(earlier, 1.0, 0.0), axis=0, keepdims=True).astype(jnp.int32)


def slots_onehot(flat_row, slots):
    iota = lax.broadcasted_iota(jnp.int32, (slots, flat_row.shape[1]), 0)
    return jnp.where(iota == flat_row, 1.0, 0.0).astype(BF)


def entries_onehot(flat_col, slots):
    iota = lax.broadcasted_iota(jnp.int32, (flat_col.shape[0], slots), 1)
    return jnp.where(flat_col[:, :1] == iota, 1.0, 0.0).astype(BF)


def own_slots(nodes_row, cap):
    n = nodes_row.shape[1]
    dest = block_of(nodes_row, n)
    rank = rank_row(dest, lax.broadcasted_iota(jnp.int32, (1, n), 1))
    return dest, rank


def pack_kernel(cap, nodes_ref, value_ref, out_ref):
    dest, rank = own_slots(nodes_ref[...], cap)
    out_ref[...] = dot(slots_onehot(dest * cap + rank, out_ref.shape[0]), value_ref[...]).astype(BF)


def index_kernel(
    cap, ways, nodes_ref, position_ref, degree_ref, cot_ref, cot_out, own_col, node_row, node_col, turned_row, turned_col
):
    n = nodes_ref.shape[1]
    width = cot_ref.shape[1]
    dest, rank = own_slots(nodes_ref[...], cap)
    flat = dest * cap + rank
    own_col[...] = as_column(flat)
    packing = slots_onehot(flat, cot_out.shape[0])
    cot_out[:, :width] = dot(packing, cot_ref[...]).astype(BF)
    cot_out[:, width:] = dot(packing, as_column(degree_ref[...].astype(F32)).astype(BF)).astype(BF)
    position = position_ref[...]
    source = block_of(position, n)
    rank = rank_row(source, position)
    place = source * cap + rank
    node_row[...] = jnp.broadcast_to(place, node_row.shape)
    node_col[...] = as_column(place)
    across = cot_out.shape[0] // (cap * ways)
    down = block_of(source, across)
    turned = ((source - down * across) * ways + down) * cap + rank
    turned_row[...] = jnp.broadcast_to(turned, turned_row.shape)
    turned_col[...] = as_column(turned)


def unpack_kernel(col_ref, value_ref, out_ref):
    out_ref[...] = dot(entries_onehot(col_ref[...], value_ref.shape[0]), value_ref[...]).astype(BF)


def spmm_kernel(ways, cols_ref, group_ref, x_ref, *refs):
    masks, outs = refs[:ways], refs[ways:]
    q = pl.program_id(0)
    depth = pl.num_programs(0)
    _, breadth, tile, _ = masks[0].shape
    for s in range(ways):
        base = (group_ref[s] * depth + q) * breadth
        total = None
        for p in range(0, breadth, 2):
            span = range(p, min(p + 2, breadth))
            left = jnp.concatenate([masks[s][0, k] for k in span], axis=1)
            right = jnp.concatenate(
                [x_ref[pl.ds(pl.multiple_of(cols_ref[base + k] * tile, tile), tile), :] for k in span], axis=0
            )
            term = dot(left, right)
            total = term if total is None else total + term
        outs[s][...] = total.astype(BF)


def spmm_back_kernel(ways, pieces, cols_ref, group_ref, *refs):
    given = sum(pieces)
    spreads, masks = refs[:given], refs[given : given + ways]
    out_hbm, total, ready, sems = refs[given + ways :]
    q = pl.program_id(0)
    depth = pl.num_programs(0)
    _, breadth, tile, _ = masks[0].shape

    @pl.when(q == 0)
    def _():
        total[...] = jnp.zeros_like(total)

    at_piece = 0
    for s in range(ways):
        base = (group_ref[s] * depth + q) * breadth
        rows = spreads[at_piece][...]
        for p in range(1, pieces[s]):
            rows = jnp.where(q * pieces[s] >= p * depth, spreads[at_piece + p][...], rows)
        at_piece += pieces[s]
        for k in range(breadth):
            at = pl.ds(pl.multiple_of(cols_ref[base + k] * tile, tile), tile)
            total[at, :] += dot(masks[s][0, k], rows, 0, 0)

    @pl.when(q == depth - 1)
    def _():
        count = sems.shape[0]
        share = total.shape[0] // count
        copies = []
        for i in range(count):
            at = pl.ds(i * share, share)
            ready[at, :] = total[at, :].astype(BF)
            copies.append(pltpu.make_async_copy(ready.at[at], out_hbm.at[at], sems.at[i]))
            copies[-1].start()
        for copy in copies:
            copy.wait()


def pass_on_kernel(left_ref, right_ref, top_ref, bottom_ref, left_out, right_out):
    half = top_ref.shape[0]
    left_out[:half, :] = left_ref[:half, :]
    left_out[half:, :] = (left_ref[half:, :].astype(F32) + bottom_ref[...].astype(F32)).astype(BF)
    right_out[:half, :] = (right_ref[:half, :].astype(F32) + top_ref[...].astype(F32)).astype(BF)
    right_out[half:, :] = right_ref[half:, :]


def prepare_kernel(x_ref, cot_ref, col_ref, self_ref, base_out, cot_out):
    base_out[...] = dot(x_ref[...], self_ref[...])
    cot_out[...] = dot(entries_onehot(col_ref[...], cot_ref.shape[0]), cot_ref[...]).astype(BF)


def layer_kernel(ways, *refs):
    terms = refs[:ways]
    (base_ref, cot_ref, neigh_ref, hidden_out, slopes_out, agg_out, spread_out) = refs[ways:]
    width = base_ref.shape[1]
    summed = terms[0][...].astype(F32)
    for s in range(1, ways):
        summed = summed + terms[s][...].astype(F32)
    degrees = cot_ref[:, width : width + 128].astype(F32)[:, :1]
    agg = (summed / degrees).astype(BF)
    agg_out[...] = agg
    preact = base_ref[...] + dot(agg, neigh_ref[...])
    gate = jax.nn.sigmoid(preact)
    hidden_out[...] = (preact * gate).astype(BF)
    slopes = (cot_ref[:, :width].astype(F32) * gate * (1.0 + preact * (1.0 - gate))).astype(BF)
    slopes_out[...] = slopes
    spread_out[...] = (dot(slopes, neigh_ref[...], 1, 1) / degrees).astype(BF)


def pack_node_kernel(row_ref, value_ref, out_ref):
    out_ref[...] = dot(slots_onehot(row_ref[...][:1], out_ref.shape[0]), value_ref[...]).astype(BF)


def terms_kernel(core_ref, x_ref, agg_ref, slopes_ref, self_ref, kept_out, sent_out, back_out):
    slopes = slopes_ref[...]
    back_out[...] = dot(slopes, self_ref[...], 1, 1)
    grad_self = dot(x_ref[...], slopes, 0, 0).astype(BF)
    grad_neigh = dot(agg_ref[...], slopes, 0, 0).astype(BF)
    first = core_ref[0] == 0
    kept_out[...] = jnp.where(first, grad_self, grad_neigh)
    sent_out[...] = jnp.where(first, grad_neigh, grad_self)


def split_sum_kernel(count, scale, index_ref, *refs):
    terms, outs, total_ref = refs[:count], refs[count:-1], refs[-1]
    total = terms[0][...].astype(F32)
    for term in terms[1:]:
        total = total + term[...].astype(F32)
    total_ref[...] = total * scale
    size = outs[0].shape[0]
    for s, out in enumerate(outs):
        out[...] = total_ref[pl.ds(pl.multiple_of(index_ref[s] * size, size), size), :].astype(out.dtype)


def place_kernel(index_ref, *refs):
    out_ref = refs[-1]
    for s, part in enumerate(refs[:-1]):
        out_ref[index_ref[s]] = part[...].astype(out_ref.dtype)


def final_kernel(core_ref, kept_ref, came_ref, self_out, neigh_out):
    first = core_ref[0] == 0
    kept, came = kept_ref[...].astype(F32), came_ref[...].astype(F32)
    self_out[...] = jnp.where(first, kept, came)
    neigh_out[...] = jnp.where(first, came, kept)


def join_kernel(own_ref, neigh_ref, row_ref, out_ref):
    joined = (own_ref[...] + neigh_ref[...].astype(F32)).astype(BF)
    out_ref[...] = dot(slots_onehot(row_ref[...][:1], out_ref.shape[0]), joined).astype(BF)


def on_device(
    features,
    tile_cols,
    tile_masks,
    degree,
    owner_nodes,
    owner_position,
    self_weight,
    neigh_weight,
    cotangent,
):
    rows, width = features.shape
    row_devices = lax.axis_size("row")
    col_devices = lax.axis_size("col")
    devices = row_devices * col_devices
    cap = 2 * rows // devices
    slots = devices * cap
    masks = tile_masks[0, 0]
    tile = masks.shape[-1]
    breadth = masks.shape[1]
    depth = rows // tile
    cols = tile_cols[0, 0].reshape(-1)
    me = lax.axis_index("row")
    ways = row_devices
    groups = jnp.bitwise_xor(me, jnp.arange(ways, dtype=jnp.int32)).astype(jnp.int32)
    everyone = ("row", "col")
    place = lax.axis_index("col")
    lines = col_devices // 2
    core = jnp.full((1,), lax.rem(place, 2), jnp.int32)
    others = jnp.bitwise_xor(lax.div(place, 2), jnp.arange(lines, dtype=jnp.int32)).astype(jnp.int32)
    SMEM = pl.BlockSpec(memory_space=pltpu.SMEM)

    def call(*args, mib=16, **kwargs):
        return pl.pallas_call(*args, compiler_params=params(mib), **kwargs)

    def shape(r, c, dtype=BF):
        return jax.ShapeDtypeStruct((r, c), dtype)

    def relay(packed):
        there = packed.reshape(devices, cap, -1)
        return lax.all_to_all(there, everyone, split_axis=0, concat_axis=0, tiled=True).reshape(slots, -1)

    def row_phase(packed):
        there = packed.reshape(row_devices, col_devices * cap, -1)
        return lax.all_to_all(there, "row", split_axis=0, concat_axis=0, tiled=True).reshape(slots, -1)

    def col_phase(packed):
        there = packed.reshape(col_devices, row_devices * cap, -1)
        return lax.all_to_all(there, "col", split_axis=0, concat_axis=0, tiled=True).reshape(slots, -1)

    def turn(packed, first, second):
        return packed.reshape(first, second, cap, -1).transpose(1, 0, 2, 3).reshape(slots, -1)

    def across(value, s):
        return lax.ppermute(value, "row", [(i, i ^ s) for i in range(ways)])

    def along(value, s):
        return lax.ppermute(value, "col", [(i, i ^ (2 * s)) for i in range(col_devices)])

    def swap(value):
        return lax.ppermute(value, "col", [(i, i ^ 1) for i in range(col_devices)])

    def split_sum(index, arrays, pieces, scale=1.0):
        r, c = arrays[0].shape
        return call(
            functools.partial(split_sum_kernel, len(arrays), scale),
            in_specs=[SMEM] + [VMEM] * len(arrays),
            out_specs=[VMEM] * pieces,
            out_shape=[shape(r // pieces, c) for _ in range(pieces)],
            scratch_shapes=[pltpu.VMEM((r, c), F32)],
            cost_estimate=cost(r * c * len(arrays), 2 * r * c * (len(arrays) + 1)),
            name="split_sum",
        )(index, *arrays)

    def in_place(index, arrays):
        count, (r, c) = len(arrays), arrays[0].shape
        return call(
            place_kernel,
            in_specs=[SMEM] + [VMEM] * count,
            out_specs=VMEM,
            out_shape=jax.ShapeDtypeStruct((count, r, c), BF),
            cost_estimate=cost(0, 4 * count * r * c),
            name="in_place",
        )(index, *arrays).reshape(count * r, c)

    nodes = owner_nodes.reshape(1, rows)
    slab = rows * width
    packed = call(
        functools.partial(pack_kernel, cap),
        out_shape=shape(slots, width),
        in_specs=[VMEM] * 2,
        out_specs=VMEM,
        cost_estimate=cost(2 * slots * slab, 6 * slab),
        mib=LARGE,
        name="pack_features",
    )(nodes, features)
    inbound = relay(packed)
    cot_packed, own_col, node_row, node_col, turned_row, turned_col = call(
        functools.partial(index_kernel, cap, ways),
        out_shape=(
            shape(slots, width + 128),
            shape(rows, 128, jnp.int32),
            shape(8, rows, jnp.int32),
            shape(rows, 128, jnp.int32),
            shape(8, rows, jnp.int32),
            shape(rows, 128, jnp.int32),
        ),
        in_specs=[VMEM] * 4,
        out_specs=(VMEM,) * 6,
        cost_estimate=cost(2 * slots * slab, 6 * slab),
        mib=LARGE,
        name="index_cotangent",
    )(nodes, owner_position.reshape(1, rows), degree.reshape(1, rows), cotangent)
    ANY = pl.BlockSpec(memory_space=pl.ANY)
    x_node = call(
        unpack_kernel,
        out_shape=shape(rows, width),
        in_specs=[VMEM] * 2,
        out_specs=VMEM,
        cost_estimate=cost(2 * slots * slab, 6 * slab),
        name="unpack_features",
    )(node_col, inbound)
    cot_packed, x_node, cols, groups, core, others = lax.optimization_barrier(
        (cot_packed, x_node, cols, groups, core, others)
    )
    x_cols = lax.all_gather(x_node, "col", axis=0, tiled=True)
    cot_mid = turn(row_phase(cot_packed), row_devices, col_devices)
    x_cols, cot_mid = lax.optimization_barrier((x_cols, cot_mid))
    cot_in = col_phase(cot_mid)

    spmm_flops = 2 * masks.size * width * WEIGHT
    def piece_spec(p, count):
        share = depth // count
        return pl.BlockSpec((tile, width), lambda q, c, g: (jnp.clip(q - p * share, 0, share - 1), 0))

    def mask_spec(s):
        return pl.BlockSpec((1, breadth, tile, tile), lambda q, c, g: (g[s] * depth + q, 0, 0, 0))

    pieces = (1, 1, 1, 2) if ways == 4 else (1,) * ways
    half = rows // 2
    partials = call(
        functools.partial(spmm_kernel, ways),
        grid_spec=pltpu.PrefetchScalarGridSpec(
            num_scalar_prefetch=2,
            grid=(depth,),
            in_specs=[VMEM] + [mask_spec(s) for s in range(ways)],
            out_specs=[pl.BlockSpec((tile, width), lambda q, c, g: (q, 0)) for s in range(ways)],
        ),
        out_shape=[shape(rows, width) for s in range(ways)],
        cost_estimate=cost(spmm_flops, 2 * masks.size + 2 * x_cols.size + 2 * ways * slab),
        mib=LARGE,
        name="spmm",
    )(cols, groups, x_cols, *([masks] * ways))
    if ways == 4:
        top, bottom = across(partials[3][:half], 1), across(partials[3][half:], 2)
        left, right = call(
            pass_on_kernel,
            out_shape=(shape(rows, width),) * 2,
            in_specs=[VMEM] * 4,
            out_specs=(VMEM,) * 2,
            cost_estimate=cost(2 * slab, 10 * slab),
            name="pass_on",
        )(partials[1], partials[2], top, bottom)
        terms = [partials[0], across(left, 1), across(right, 2)]
    else:
        terms = [partials[0]] + [across(partials[s], s) for s in range(1, ways)]
    base, cot_node = call(
        prepare_kernel,
        out_shape=(shape(rows, width, F32), shape(rows, width + 128)),
        in_specs=[VMEM] * 4,
        out_specs=(VMEM,) * 2,
        cost_estimate=cost(6 * slab * width, 2 * slab * 8),
        mib=LARGE,
        name="prepare",
    )(x_node, cot_in, turned_col, self_weight)

    def by_rows(columns):
        return pl.BlockSpec((half, columns), lambda i: (i, 0))

    hidden, slopes, agg, spread = call(
        functools.partial(layer_kernel, len(terms)),
        grid=(2,),
        out_shape=(shape(rows, width),) * 4,
        in_specs=[by_rows(width)] * (len(terms) + 1) + [by_rows(width + 128), VMEM],
        out_specs=(by_rows(width),) * 4,
        cost_estimate=cost(8 * slab * width, 2 * slab * (len(terms) + 9)),
        mib=LARGE,
        name="layer",
    )(*terms, base, cot_node, neigh_weight)
    hidden_packed = call(
        pack_node_kernel,
        out_shape=shape(slots, width),
        in_specs=[VMEM] * 2,
        out_specs=VMEM,
        cost_estimate=cost(2 * slots * slab, 6 * slab),
        name="pack_hidden",
    )(turned_row, hidden)
    if ways == 4:
        left, right = across(spread, 1), across(spread, 2)
        left, right, _ = lax.optimization_barrier((left, right, hidden_packed))
        spreads = [spread, left, right, across(right[:half], 1), across(left[half:], 2)]
    else:
        spreads = [spread] + [across(spread, s) for s in range(1, ways)]
    hidden_mid = col_phase(hidden_packed)
    grad_kept, grad_sent, own_back = call(
        terms_kernel,
        out_shape=(shape(width, width), shape(width, width), shape(rows, width, F32)),
        in_specs=[SMEM] + [VMEM] * 4,
        out_specs=(VMEM,) * 3,
        cost_estimate=cost(6 * slab * width, 2 * slab * 9),
        mib=LARGE,
        name="terms",
    )(core, x_node, agg, slopes, self_weight)
    *spreads, own_back, grad_kept, grad_sent = lax.optimization_barrier((*spreads, own_back, grad_kept, grad_sent))
    back = call(
        functools.partial(spmm_back_kernel, ways, pieces),
        grid_spec=pltpu.PrefetchScalarGridSpec(
            num_scalar_prefetch=2,
            grid=(depth,),
            in_specs=[piece_spec(p, count) for count in pieces for p in range(count)]
            + [mask_spec(s) for s in range(ways)],
            out_specs=ANY,
            scratch_shapes=[
                pltpu.VMEM(x_cols.shape, F32),
                pltpu.VMEM(x_cols.shape, BF),
                pltpu.SemaphoreType.DMA((col_devices,)),
            ],
        ),
        out_shape=shape(*x_cols.shape),
        cost_estimate=cost(spmm_flops, 2 * masks.size + 2 * x_cols.size + 2 * ways * slab),
        mib=LARGE,
        name="spmm_back",
    )(cols, groups, *spreads, *([masks] * ways))
    back, hidden_mid, grad_sent = lax.optimization_barrier((back, hidden_mid, grad_sent))
    neigh_back = lax.psum_scatter(back, "col", scatter_dimension=0, tiled=True)
    hidden_in = row_phase(turn(hidden_mid, col_devices, row_devices))
    pieces = split_sum(groups, [grad_kept, swap(grad_sent)], ways)
    pieces = split_sum(others, [pieces[0]] + [across(pieces[s], s) for s in range(1, ways)], lines)
    scale = 1.0 / math.sqrt(rows * devices)
    zero = jnp.zeros((1,), jnp.int32)
    (mine,) = split_sum(zero, [pieces[0]] + [along(pieces[s], s) for s in range(1, lines)], 1, scale)
    in_line = in_place(others, [mine] + [along(mine, s) for s in range(1, lines)])
    own_back, in_line = lax.optimization_barrier((own_back, in_line))
    grad_half = in_place(groups, [in_line] + [across(in_line, s) for s in range(1, ways)])
    grad_self, grad_neigh = call(
        final_kernel,
        in_specs=[SMEM] + [VMEM] * 2,
        out_specs=(VMEM,) * 2,
        out_shape=(shape(width, width, F32),) * 2,
        cost_estimate=cost(0, 12 * width * width),
        name="final",
    )(core, grad_half, swap(grad_half))
    grad_packed = call(
        join_kernel,
        out_shape=shape(slots, width),
        in_specs=[VMEM] * 3,
        out_specs=VMEM,
        cost_estimate=cost(2 * slots * slab, 8 * slab),
        name="join_pack",
    )(own_back, neigh_back, node_row)
    grad_in = relay(grad_packed)

    def unpack_own(value):
        return call(
            unpack_kernel,
            out_shape=shape(rows, width),
            in_specs=[VMEM] * 2,
            out_specs=VMEM,
            cost_estimate=cost(2 * slots * slab, 6 * slab),
            name="unpack_owner",
        )(own_col, value)

    hidden_own = unpack_own(hidden_in)
    grad_own = unpack_own(grad_in)
    return (hidden_own, grad_own, grad_self, grad_neigh)


def solution(mesh):
    placed = (
        P(("row", "col"), None),
        P("row", "col", None, None),
        P("row", "col", None, None, None, None),
        P(("row", "col")),
        P(("row", "col")),
        P(("row", "col")),
        P(),
        P(),
        P(("row", "col"), None),
    )
    return jax.shard_map(
        on_device,
        mesh=mesh,
        in_specs=placed,
        out_specs=(P(("row", "col"), None), P(("row", "col"), None), P(), P()),
        check_vma=False,
    )
```

```python
import functools
import math

import jax
import jax.numpy as jnp
from jax import lax
from jax.experimental import pallas as pl
from jax.experimental.pallas import tpu as pltpu
from jax.sharding import PartitionSpec as P

BF = jnp.bfloat16
F32 = jnp.float32
VMEM = pl.BlockSpec(memory_space=pltpu.VMEM)
MIB = 1024 * 1024
LARGE = 56
WEIGHT = 6


def params(mib=16):
    return pltpu.CompilerParams(vmem_limit_bytes=int(mib * MIB))


def cost(flops, nbytes):
    return pl.CostEstimate(flops=int(flops), bytes_accessed=int(nbytes), transcendentals=0)


def dot(a, b, ca=1, cb=0):
    return lax.dot_general(a, b, (((ca,), (cb,)), ((), ())), preferred_element_type=F32)


def as_column(row):
    return jnp.broadcast_to(row, (128, row.shape[1])).T


def block_of(index, size):
    if size & (size - 1) == 0:
        return lax.shift_right_logical(index, size.bit_length() - 1)
    return lax.div(index, jnp.full_like(index, size))


def rank_row(group_row, order_row):
    n = group_row.shape[1]
    group_col = as_column(group_row)[:, :1]
    order_col = as_column(order_row)[:, :1]
    earlier = (group_col == group_row) & (order_col < order_row)
    return jnp.sum(jnp.where(earlier, 1.0, 0.0), axis=0, keepdims=True).astype(jnp.int32)


def slots_onehot(flat_row, slots):
    iota = lax.broadcasted_iota(jnp.int32, (slots, flat_row.shape[1]), 0)
    return jnp.where(iota == flat_row, 1.0, 0.0).astype(BF)


def entries_onehot(flat_col, slots):
    iota = lax.broadcasted_iota(jnp.int32, (flat_col.shape[0], slots), 1)
    return jnp.where(flat_col[:, :1] == iota, 1.0, 0.0).astype(BF)


def own_slots(nodes_row, cap):
    n = nodes_row.shape[1]
    dest = block_of(nodes_row, n)
    rank = rank_row(dest, lax.broadcasted_iota(jnp.int32, (1, n), 1))
    return dest, rank


def pack_kernel(cap, nodes_ref, value_ref, out_ref):
    dest, rank = own_slots(nodes_ref[...], cap)
    out_ref[...] = dot(slots_onehot(dest * cap + rank, out_ref.shape[0]), value_ref[...]).astype(BF)


def index_kernel(cap, ways, nodes_ref, position_ref, degree_ref, cot_ref, cot_out, degree_out, own_row, node_row, turned_row):
    n = nodes_ref.shape[1]
    devices = degree_out.shape[0]
    dest, rank = own_slots(nodes_ref[...], cap)
    flat = dest * cap + rank
    own_row[...] = jnp.broadcast_to(flat, own_row.shape)
    cot_out[...] = dot(slots_onehot(flat, cot_out.shape[0]), cot_ref[...]).astype(BF)
    by_dest = jnp.where(lax.broadcasted_iota(jnp.int32, (devices, n), 0) == dest, degree_ref[...].astype(F32), 0.0)
    degree_out[...] = dot(by_dest.astype(BF), entries_onehot(as_column(rank), cap))
    position = position_ref[...]
    source = block_of(position, n)
    rank = rank_row(source, position)
    node_row[...] = jnp.broadcast_to(source * cap + rank, node_row.shape)
    across = cot_out.shape[0] // (cap * ways)
    down = block_of(source, across)
    turned = ((source - down * across) * ways + down) * cap + rank
    turned_row[...] = jnp.broadcast_to(turned, turned_row.shape)


def unpack_kernel(row_ref, value_ref, out_ref):
    out_ref[...] = dot(entries_onehot(as_column(row_ref[...][:1]), value_ref.shape[0]), value_ref[...]).astype(BF)


def spmm_kernel(ways, cols_ref, group_ref, x_ref, *refs):
    masks, outs = refs[:ways], refs[ways:]
    q = pl.program_id(0)
    depth = pl.num_programs(0)
    _, breadth, tile, _ = masks[0].shape
    for s in range(ways):
        base = (group_ref[s] * depth + q) * breadth
        total = None
        for p in range(0, breadth, 2):
            span = range(p, min(p + 2, breadth))
            left = jnp.concatenate([masks[s][0, k] for k in span], axis=1)
            right = jnp.concatenate(
                [x_ref[pl.ds(pl.multiple_of(cols_ref[base + k] * tile, tile), tile), :] for k in span], axis=0
            )
            term = dot(left, right)
            total = term if total is None else total + term
        outs[s][...] = total.astype(BF)


def spmm_back_kernel(ways, pieces, cols_ref, group_ref, *refs):
    given = sum(pieces)
    spreads, masks = refs[:given], refs[given : given + ways]
    out_hbm, total, ready, sems = refs[given + ways :]
    q = pl.program_id(0)
    depth = pl.num_programs(0)
    _, breadth, tile, _ = masks[0].shape

    @pl.when(q == 0)
    def _():
        total[...] = jnp.zeros_like(total)

    at_piece = 0
    for s in range(ways):
        base = (group_ref[s] * depth + q) * breadth
        rows = spreads[at_piece][...]
        for p in range(1, pieces[s]):
            rows = jnp.where(q * pieces[s] >= p * depth, spreads[at_piece + p][...], rows)
        at_piece += pieces[s]
        for k in range(breadth):
            at = pl.ds(pl.multiple_of(cols_ref[base + k] * tile, tile), tile)
            total[at, :] += dot(masks[s][0, k], rows, 0, 0)

    @pl.when(q == depth - 1)
    def _():
        count = sems.shape[0]
        share = total.shape[0] // count
        copies = []
        for i in range(count):
            at = pl.ds(i * share, share)
            ready[at, :] = total[at, :].astype(BF)
            copies.append(pltpu.make_async_copy(ready.at[at], out_hbm.at[at], sems.at[i]))
            copies[-1].start()
        for copy in copies:
            copy.wait()


def pass_on_kernel(left_ref, right_ref, top_ref, bottom_ref, left_out, right_out):
    half = top_ref.shape[0]
    left_out[:half, :] = left_ref[:half, :]
    left_out[half:, :] = (left_ref[half:, :].astype(F32) + bottom_ref[...].astype(F32)).astype(BF)
    right_out[:half, :] = (right_ref[:half, :].astype(F32) + top_ref[...].astype(F32)).astype(BF)
    right_out[half:, :] = right_ref[half:, :]


def prepare_kernel(x_ref, degree_ref, row_ref, self_ref, base_out, degree_out):
    devices, cap = degree_ref.shape
    base_out[...] = dot(x_ref[...], self_ref[...])
    place = as_column(row_ref[...][:1])[:, :1]
    source = block_of(place, cap)
    rank = place - source * cap
    degrees = dot(entries_onehot(source, devices), degree_ref[...].astype(BF))
    picked = lax.broadcasted_iota(jnp.int32, degrees.shape, 1) == rank
    degrees = jnp.sum(jnp.where(picked, degrees, 0.0), axis=1, keepdims=True)
    degree_out[...] = jnp.broadcast_to(degrees, degree_out.shape)


def layer_kernel(ways, *refs):
    terms = refs[:ways]
    (base_ref, degree_ref, cot_ref, neigh_ref, hidden_out, slopes_out, agg_out, spread_out) = refs[ways:]
    summed = terms[0][...].astype(F32)
    for s in range(1, ways):
        summed = summed + terms[s][...].astype(F32)
    degrees = degree_ref[...][:, :1]
    agg = (summed / degrees).astype(BF)
    agg_out[...] = agg
    preact = base_ref[...] + dot(agg, neigh_ref[...])
    gate = jax.nn.sigmoid(preact)
    hidden_out[...] = (preact * gate).astype(BF)
    slopes = (cot_ref[...].astype(F32) * gate * (1.0 + preact * (1.0 - gate))).astype(BF)
    slopes_out[...] = slopes
    spread_out[...] = (dot(slopes, neigh_ref[...], 1, 1) / degrees).astype(BF)


def pack_node_kernel(row_ref, value_ref, out_ref):
    out_ref[...] = dot(slots_onehot(row_ref[...][:1], out_ref.shape[0]), value_ref[...]).astype(BF)


def terms_kernel(core_ref, x_ref, agg_ref, slopes_ref, self_ref, kept_out, sent_out, back_out):
    slopes = slopes_ref[...]
    back_out[...] = dot(slopes, self_ref[...], 1, 1)
    grad_self = dot(x_ref[...], slopes, 0, 0).astype(BF)
    grad_neigh = dot(agg_ref[...], slopes, 0, 0).astype(BF)
    first = core_ref[0] == 0
    kept_out[...] = jnp.where(first, grad_self, grad_neigh)
    sent_out[...] = jnp.where(first, grad_neigh, grad_self)


def split_sum_kernel(count, scale, index_ref, *refs):
    terms, outs, total_ref = refs[:count], refs[count:-1], refs[-1]
    total = terms[0][...].astype(F32)
    for term in terms[1:]:
        total = total + term[...].astype(F32)
    total_ref[...] = total * scale
    size = outs[0].shape[0]
    for s, out in enumerate(outs):
        out[...] = total_ref[pl.ds(pl.multiple_of(index_ref[s] * size, size), size), :].astype(out.dtype)


def place_kernel(index_ref, *refs):
    out_ref = refs[-1]
    for s, part in enumerate(refs[:-1]):
        out_ref[index_ref[s]] = part[...].astype(out_ref.dtype)


def final_kernel(core_ref, kept_ref, came_ref, self_out, neigh_out):
    first = core_ref[0] == 0
    kept, came = kept_ref[...].astype(F32), came_ref[...].astype(F32)
    self_out[...] = jnp.where(first, kept, came)
    neigh_out[...] = jnp.where(first, came, kept)


def join_kernel(own_ref, neigh_ref, row_ref, out_ref):
    joined = (own_ref[...] + neigh_ref[...].astype(F32)).astype(BF)
    out_ref[...] = dot(slots_onehot(row_ref[...][:1], out_ref.shape[0]), joined).astype(BF)


def on_device(
    features,
    tile_cols,
    tile_masks,
    degree,
    owner_nodes,
    owner_position,
    self_weight,
    neigh_weight,
    cotangent,
):
    rows, width = features.shape
    row_devices = lax.axis_size("row")
    col_devices = lax.axis_size("col")
    devices = row_devices * col_devices
    cap = 2 * rows // devices
    slots = devices * cap
    masks = tile_masks[0, 0]
    tile = masks.shape[-1]
    breadth = masks.shape[1]
    depth = rows // tile
    cols = tile_cols[0, 0].reshape(-1)
    me = lax.axis_index("row")
    ways = row_devices
    groups = jnp.bitwise_xor(me, jnp.arange(ways, dtype=jnp.int32)).astype(jnp.int32)
    everyone = ("row", "col")
    place = lax.axis_index("col")
    lines = col_devices // 2
    core = jnp.full((1,), lax.rem(place, 2), jnp.int32)
    others = jnp.bitwise_xor(lax.div(place, 2), jnp.arange(lines, dtype=jnp.int32)).astype(jnp.int32)
    SMEM = pl.BlockSpec(memory_space=pltpu.SMEM)

    def call(*args, mib=16, **kwargs):
        return pl.pallas_call(*args, compiler_params=params(mib), **kwargs)

    def shape(r, c, dtype=BF):
        return jax.ShapeDtypeStruct((r, c), dtype)

    def relay(packed):
        there = packed.reshape(devices, cap, -1)
        return lax.all_to_all(there, everyone, split_axis=0, concat_axis=0, tiled=True).reshape(slots, -1)

    def row_phase(packed):
        there = packed.reshape(row_devices, col_devices * cap, -1)
        return lax.all_to_all(there, "row", split_axis=0, concat_axis=0, tiled=True).reshape(slots, -1)

    def col_phase(packed):
        there = packed.reshape(col_devices, row_devices * cap, -1)
        return lax.all_to_all(there, "col", split_axis=0, concat_axis=0, tiled=True).reshape(slots, -1)

    def turn(packed, first, second):
        return packed.reshape(first, second, cap, -1).transpose(1, 0, 2, 3).reshape(slots, -1)

    def across(value, s):
        return lax.ppermute(value, "row", [(i, i ^ s) for i in range(ways)])

    def along(value, s):
        return lax.ppermute(value, "col", [(i, i ^ (2 * s)) for i in range(col_devices)])

    def swap(value):
        return lax.ppermute(value, "col", [(i, i ^ 1) for i in range(col_devices)])

    def split_sum(index, arrays, pieces, scale=1.0):
        r, c = arrays[0].shape
        return call(
            functools.partial(split_sum_kernel, len(arrays), scale),
            in_specs=[SMEM] + [VMEM] * len(arrays),
            out_specs=[VMEM] * pieces,
            out_shape=[shape(r // pieces, c) for _ in range(pieces)],
            scratch_shapes=[pltpu.VMEM((r, c), F32)],
            cost_estimate=cost(r * c * len(arrays), 2 * r * c * (len(arrays) + 1)),
            name="split_sum",
        )(index, *arrays)

    def in_place(index, arrays):
        count, (r, c) = len(arrays), arrays[0].shape
        return call(
            place_kernel,
            in_specs=[SMEM] + [VMEM] * count,
            out_specs=VMEM,
            out_shape=jax.ShapeDtypeStruct((count, r, c), BF),
            cost_estimate=cost(0, 4 * count * r * c),
            name="in_place",
        )(index, *arrays).reshape(count * r, c)

    nodes = owner_nodes.reshape(1, rows)
    slab = rows * width
    packed = call(
        functools.partial(pack_kernel, cap),
        out_shape=shape(slots, width),
        in_specs=[VMEM] * 2,
        out_specs=VMEM,
        cost_estimate=cost(2 * slots * slab, 6 * slab),
        mib=LARGE,
        name="pack_features",
    )(nodes, features)
    inbound = relay(packed)
    cot_packed, degree_packed, own_row, node_row, turned_row = call(
        functools.partial(index_kernel, cap, ways),
        out_shape=(shape(slots, width), shape(devices, cap, F32)) + (shape(8, rows, jnp.int32),) * 3,
        in_specs=[VMEM] * 4,
        out_specs=(VMEM,) * 5,
        cost_estimate=cost(2 * slots * slab, 6 * slab),
        mib=LARGE,
        name="index_cotangent",
    )(nodes, owner_position.reshape(1, rows), degree.reshape(1, rows), cotangent)
    ANY = pl.BlockSpec(memory_space=pl.ANY)
    x_node = call(
        unpack_kernel,
        out_shape=shape(rows, width),
        in_specs=[VMEM] * 2,
        out_specs=VMEM,
        cost_estimate=cost(2 * slots * slab, 6 * slab),
        name="unpack_features",
    )(node_row, inbound)
    cot_packed, degree_packed, x_node, cols, groups, core, others = lax.optimization_barrier(
        (cot_packed, degree_packed, x_node, cols, groups, core, others)
    )
    x_cols = lax.all_gather(x_node, "col", axis=0, tiled=True)
    cot_mid = turn(row_phase(cot_packed), row_devices, col_devices)
    degree_in = lax.all_to_all(degree_packed, everyone, split_axis=0, concat_axis=0, tiled=True)
    base, degrees = call(
        prepare_kernel,
        out_shape=(shape(rows, width, F32), shape(rows, 128, F32)),
        in_specs=[VMEM] * 4,
        out_specs=(VMEM,) * 2,
        cost_estimate=cost(2 * slab * width, 2 * slab * 4),
        mib=LARGE,
        name="prepare",
    )(x_node, degree_in, node_row, self_weight)
    x_cols, cot_mid, base, degrees = lax.optimization_barrier((x_cols, cot_mid, base, degrees))
    cot_in = col_phase(cot_mid)

    spmm_flops = 2 * masks.size * width * WEIGHT
    def piece_spec(p, count):
        share = depth // count
        return pl.BlockSpec((tile, width), lambda q, c, g: (jnp.clip(q - p * share, 0, share - 1), 0))

    def mask_spec(s):
        return pl.BlockSpec((1, breadth, tile, tile), lambda q, c, g: (g[s] * depth + q, 0, 0, 0))

    pieces = (1, 1, 1, 2) if ways == 4 else (1,) * ways
    half = rows // 2
    partials = call(
        functools.partial(spmm_kernel, ways),
        grid_spec=pltpu.PrefetchScalarGridSpec(
            num_scalar_prefetch=2,
            grid=(depth,),
            in_specs=[VMEM] + [mask_spec(s) for s in range(ways)],
            out_specs=[pl.BlockSpec((tile, width), lambda q, c, g: (q, 0)) for s in range(ways)],
        ),
        out_shape=[shape(rows, width) for s in range(ways)],
        cost_estimate=cost(spmm_flops, 2 * masks.size + 2 * x_cols.size + 2 * ways * slab),
        mib=LARGE,
        name="spmm",
    )(cols, groups, x_cols, *([masks] * ways))
    if ways == 4:
        top, bottom = across(partials[3][:half], 1), across(partials[3][half:], 2)
        left, right = call(
            pass_on_kernel,
            out_shape=(shape(rows, width),) * 2,
            in_specs=[VMEM] * 4,
            out_specs=(VMEM,) * 2,
            cost_estimate=cost(2 * slab, 10 * slab),
            name="pass_on",
        )(partials[1], partials[2], top, bottom)
        terms = [partials[0], across(left, 1), across(right, 2)]
    else:
        terms = [partials[0]] + [across(partials[s], s) for s in range(1, ways)]
    cot_node = call(
        unpack_kernel,
        out_shape=shape(rows, width),
        in_specs=[VMEM] * 2,
        out_specs=VMEM,
        cost_estimate=cost(2 * slots * slab, 6 * slab),
        name="unpack_cotangent",
    )(turned_row, cot_in)

    def by_rows(columns):
        return pl.BlockSpec((half, columns), lambda i: (i, 0))

    hidden, slopes, agg, spread = call(
        functools.partial(layer_kernel, len(terms)),
        grid=(2,),
        out_shape=(shape(rows, width),) * 4,
        in_specs=[by_rows(width)] * (len(terms) + 1) + [by_rows(128), by_rows(width), VMEM],
        out_specs=(by_rows(width),) * 4,
        cost_estimate=cost(8 * slab * width, 2 * slab * (len(terms) + 9)),
        mib=LARGE,
        name="layer",
    )(*terms, base, degrees, cot_node, neigh_weight)
    hidden_packed = call(
        pack_node_kernel,
        out_shape=shape(slots, width),
        in_specs=[VMEM] * 2,
        out_specs=VMEM,
        cost_estimate=cost(2 * slots * slab, 6 * slab),
        name="pack_hidden",
    )(turned_row, hidden)
    if ways == 4:
        left, right = across(spread, 1), across(spread, 2)
        left, right, _ = lax.optimization_barrier((left, right, hidden_packed))
        spreads = [spread, left, right, across(right[:half], 1), across(left[half:], 2)]
    else:
        spreads = [spread] + [across(spread, s) for s in range(1, ways)]
    hidden_mid = col_phase(hidden_packed)
    grad_kept, grad_sent, own_back = call(
        terms_kernel,
        out_shape=(shape(width, width), shape(width, width), shape(rows, width, F32)),
        in_specs=[SMEM] + [VMEM] * 4,
        out_specs=(VMEM,) * 3,
        cost_estimate=cost(6 * slab * width, 2 * slab * 9),
        mib=LARGE,
        name="terms",
    )(core, x_node, agg, slopes, self_weight)
    *spreads, own_back, grad_kept, grad_sent = lax.optimization_barrier((*spreads, own_back, grad_kept, grad_sent))
    back = call(
        functools.partial(spmm_back_kernel, ways, pieces),
        grid_spec=pltpu.PrefetchScalarGridSpec(
            num_scalar_prefetch=2,
            grid=(depth,),
            in_specs=[piece_spec(p, count) for count in pieces for p in range(count)]
            + [mask_spec(s) for s in range(ways)],
            out_specs=ANY,
            scratch_shapes=[
                pltpu.VMEM(x_cols.shape, F32),
                pltpu.VMEM(x_cols.shape, BF),
                pltpu.SemaphoreType.DMA((col_devices,)),
            ],
        ),
        out_shape=shape(*x_cols.shape),
        cost_estimate=cost(spmm_flops, 2 * masks.size + 2 * x_cols.size + 2 * ways * slab),
        mib=LARGE,
        name="spmm_back",
    )(cols, groups, *spreads, *([masks] * ways))
    back, hidden_mid, grad_sent = lax.optimization_barrier((back, hidden_mid, grad_sent))
    neigh_back = lax.psum_scatter(back, "col", scatter_dimension=0, tiled=True)
    hidden_in = row_phase(turn(hidden_mid, col_devices, row_devices))
    pieces = split_sum(groups, [grad_kept, swap(grad_sent)], ways)
    pieces = split_sum(others, [pieces[0]] + [across(pieces[s], s) for s in range(1, ways)], lines)
    scale = 1.0 / math.sqrt(rows * devices)
    zero = jnp.zeros((1,), jnp.int32)
    (mine,) = split_sum(zero, [pieces[0]] + [along(pieces[s], s) for s in range(1, lines)], 1, scale)
    in_line = in_place(others, [mine] + [along(mine, s) for s in range(1, lines)])
    own_back, in_line = lax.optimization_barrier((own_back, in_line))
    grad_half = in_place(groups, [in_line] + [across(in_line, s) for s in range(1, ways)])
    grad_self, grad_neigh = call(
        final_kernel,
        in_specs=[SMEM] + [VMEM] * 2,
        out_specs=(VMEM,) * 2,
        out_shape=(shape(width, width, F32),) * 2,
        cost_estimate=cost(0, 12 * width * width),
        name="final",
    )(core, grad_half, swap(grad_half))
    grad_packed = call(
        join_kernel,
        out_shape=shape(slots, width),
        in_specs=[VMEM] * 3,
        out_specs=VMEM,
        cost_estimate=cost(2 * slots * slab, 8 * slab),
        name="join_pack",
    )(own_back, neigh_back, node_row)
    grad_in = relay(grad_packed)

    def unpack_own(value):
        return call(
            unpack_kernel,
            out_shape=shape(rows, width),
            in_specs=[VMEM] * 2,
            out_specs=VMEM,
            cost_estimate=cost(2 * slots * slab, 6 * slab),
            name="unpack_owner",
        )(own_row, value)

    hidden_own = unpack_own(hidden_in)
    grad_own = unpack_own(grad_in)
    return (hidden_own, grad_own, grad_self, grad_neigh)


def solution(mesh):
    placed = (
        P(("row", "col"), None),
        P("row", "col", None, None),
        P("row", "col", None, None, None, None),
        P(("row", "col")),
        P(("row", "col")),
        P(("row", "col")),
        P(),
        P(),
        P(("row", "col"), None),
    )
    return jax.shard_map(
        on_device,
        mesh=mesh,
        in_specs=placed,
        out_specs=(P(("row", "col"), None), P(("row", "col"), None), P(), P()),
        check_vma=False,
    )
```

```python
import functools
import math

import jax
import jax.numpy as jnp
from jax import lax
from jax.experimental import pallas as pl
from jax.experimental.pallas import tpu as pltpu
from jax.sharding import PartitionSpec as P

BF = jnp.bfloat16
F32 = jnp.float32
VMEM = pl.BlockSpec(memory_space=pltpu.VMEM)
MIB = 1024 * 1024
LARGE = 56
WEIGHT = 6


def params(mib=16):
    return pltpu.CompilerParams(vmem_limit_bytes=int(mib * MIB))


def cost(flops, nbytes):
    return pl.CostEstimate(flops=int(flops), bytes_accessed=int(nbytes), transcendentals=0)


def dot(a, b, ca=1, cb=0):
    return lax.dot_general(a, b, (((ca,), (cb,)), ((), ())), preferred_element_type=F32)


def as_column(row):
    return jnp.broadcast_to(row, (128, row.shape[1])).T


def block_of(index, size):
    if size & (size - 1) == 0:
        return lax.shift_right_logical(index, size.bit_length() - 1)
    return lax.div(index, jnp.full_like(index, size))


def rank_row(group_row, order_row):
    n = group_row.shape[1]
    group_col = as_column(group_row)[:, :1]
    order_col = as_column(order_row)[:, :1]
    earlier = (group_col == group_row) & (order_col < order_row)
    return jnp.sum(jnp.where(earlier, 1.0, 0.0), axis=0, keepdims=True).astype(jnp.int32)


def slots_onehot(flat_row, slots):
    iota = lax.broadcasted_iota(jnp.int32, (slots, flat_row.shape[1]), 0)
    return jnp.where(iota == flat_row, 1.0, 0.0).astype(BF)


def entries_onehot(flat_col, slots):
    iota = lax.broadcasted_iota(jnp.int32, (flat_col.shape[0], slots), 1)
    return jnp.where(flat_col[:, :1] == iota, 1.0, 0.0).astype(BF)


def own_slots(nodes_row, cap):
    n = nodes_row.shape[1]
    dest = block_of(nodes_row, n)
    rank = rank_row(dest, lax.broadcasted_iota(jnp.int32, (1, n), 1))
    return dest, rank


def pack_kernel(cap, nodes_ref, value_ref, out_ref):
    dest, rank = own_slots(nodes_ref[...], cap)
    out_ref[...] = dot(slots_onehot(dest * cap + rank, out_ref.shape[0]), value_ref[...]).astype(BF)


def index_kernel(cap, ways, nodes_ref, position_ref, degree_ref, cot_ref, cot_out, degree_out, own_row, node_row, turned_row):
    n = nodes_ref.shape[1]
    devices = degree_out.shape[0]
    dest, rank = own_slots(nodes_ref[...], cap)
    flat = dest * cap + rank
    own_row[...] = jnp.broadcast_to(flat, own_row.shape)
    cot_out[...] = dot(slots_onehot(flat, cot_out.shape[0]), cot_ref[...]).astype(BF)
    by_dest = jnp.where(lax.broadcasted_iota(jnp.int32, (devices, n), 0) == dest, degree_ref[...].astype(F32), 0.0)
    degree_out[...] = dot(by_dest.astype(BF), entries_onehot(as_column(rank), cap))
    position = position_ref[...]
    source = block_of(position, n)
    rank = rank_row(source, position)
    node_row[...] = jnp.broadcast_to(source * cap + rank, node_row.shape)
    across = cot_out.shape[0] // (cap * ways)
    down = block_of(source, across)
    turned = ((source - down * across) * ways + down) * cap + rank
    turned_row[...] = jnp.broadcast_to(turned, turned_row.shape)


def unpack_kernel(row_ref, value_ref, out_ref):
    out_ref[...] = dot(entries_onehot(as_column(row_ref[...][:1]), value_ref.shape[0]), value_ref[...]).astype(BF)


def spmm_kernel(ways, cols_ref, group_ref, x_ref, *refs):
    masks, outs = refs[: 2 * ways], refs[2 * ways :]
    i = pl.program_id(0)
    share = pl.num_programs(0)
    _, breadth, tile, _ = masks[0].shape
    for at, (mask_ref, out_ref) in enumerate(zip(masks, outs)):
        s, part = divmod(at, 2)
        base = ((group_ref[s] * 2 + part) * share + i) * breadth
        total = None
        for p in range(0, breadth, 2):
            span = range(p, min(p + 2, breadth))
            left = jnp.concatenate([mask_ref[0, k] for k in span], axis=1)
            right = jnp.concatenate(
                [x_ref[pl.ds(pl.multiple_of(cols_ref[base + k] * tile, tile), tile), :] for k in span], axis=0
            )
            term = dot(left, right)
            total = term if total is None else total + term
        out_ref[...] = total.astype(BF)


def spmm_back_kernel(ways, pieces, cols_ref, group_ref, *refs):
    given = sum(pieces)
    spreads, masks = refs[:given], refs[given : given + ways]
    out_hbm, total, ready, sems = refs[given + ways :]
    q = pl.program_id(0)
    depth = pl.num_programs(0)
    _, breadth, tile, _ = masks[0].shape

    @pl.when(q == 0)
    def _():
        total[...] = jnp.zeros_like(total)

    at_piece = 0
    for s in range(ways):
        base = (group_ref[s] * depth + q) * breadth
        rows = spreads[at_piece][...]
        for p in range(1, pieces[s]):
            rows = jnp.where(q * pieces[s] >= p * depth, spreads[at_piece + p][...], rows)
        at_piece += pieces[s]
        for k in range(breadth):
            at = pl.ds(pl.multiple_of(cols_ref[base + k] * tile, tile), tile)
            total[at, :] += dot(masks[s][0, k], rows, 0, 0)

    @pl.when(q == depth - 1)
    def _():
        count = sems.shape[0]
        share = total.shape[0] // count
        copies = []
        for i in range(count):
            at = pl.ds(i * share, share)
            ready[at, :] = total[at, :].astype(BF)
            copies.append(pltpu.make_async_copy(ready.at[at], out_hbm.at[at], sems.at[i]))
            copies[-1].start()
        for copy in copies:
            copy.wait()


def pass_on_kernel(left_ref, right_ref, to_left_ref, to_right_ref, left_out, right_out):
    left_out[...] = (left_ref[...].astype(F32) + to_left_ref[...].astype(F32)).astype(BF)
    right_out[...] = (right_ref[...].astype(F32) + to_right_ref[...].astype(F32)).astype(BF)


def prepare_kernel(x_ref, degree_ref, row_ref, self_ref, base_out, degree_out):
    devices, cap = degree_ref.shape
    base_out[...] = dot(x_ref[...], self_ref[...])
    place = as_column(row_ref[...][:1])[:, :1]
    source = block_of(place, cap)
    rank = place - source * cap
    degrees = dot(entries_onehot(source, devices), degree_ref[...].astype(BF))
    picked = lax.broadcasted_iota(jnp.int32, degrees.shape, 1) == rank
    degrees = jnp.sum(jnp.where(picked, degrees, 0.0), axis=1, keepdims=True)
    degree_out[...] = jnp.broadcast_to(degrees, degree_out.shape)


def layer_kernel(ways, *refs):
    uppers, lowers = refs[:ways], refs[ways : 2 * ways]
    (base_ref, degree_ref, cot_ref, neigh_ref, hidden_out, slopes_out, agg_out, spread_out) = refs[2 * ways :]
    lower = pl.program_id(0) == 1
    summed = 0.0
    for up_ref, low_ref in zip(uppers, lowers):
        summed = summed + jnp.where(lower, low_ref[...], up_ref[...]).astype(F32)
    degrees = degree_ref[...][:, :1]
    agg = (summed / degrees).astype(BF)
    agg_out[...] = agg
    preact = base_ref[...] + dot(agg, neigh_ref[...])
    gate = jax.nn.sigmoid(preact)
    hidden_out[...] = (preact * gate).astype(BF)
    slopes = (cot_ref[...].astype(F32) * gate * (1.0 + preact * (1.0 - gate))).astype(BF)
    slopes_out[...] = slopes
    spread_out[...] = (dot(slopes, neigh_ref[...], 1, 1) / degrees).astype(BF)


def pack_node_kernel(row_ref, value_ref, out_ref):
    out_ref[...] = dot(slots_onehot(row_ref[...][:1], out_ref.shape[0]), value_ref[...]).astype(BF)


def terms_kernel(core_ref, x_ref, agg_ref, slopes_ref, self_ref, kept_out, sent_out, back_out):
    slopes = slopes_ref[...]
    back_out[...] = dot(slopes, self_ref[...], 1, 1)
    grad_self = dot(x_ref[...], slopes, 0, 0).astype(BF)
    grad_neigh = dot(agg_ref[...], slopes, 0, 0).astype(BF)
    first = core_ref[0] == 0
    kept_out[...] = jnp.where(first, grad_self, grad_neigh)
    sent_out[...] = jnp.where(first, grad_neigh, grad_self)


def split_sum_kernel(count, scale, index_ref, *refs):
    terms, outs, total_ref = refs[:count], refs[count:-1], refs[-1]
    total = terms[0][...].astype(F32)
    for term in terms[1:]:
        total = total + term[...].astype(F32)
    total_ref[...] = total * scale
    size = outs[0].shape[0]
    for s, out in enumerate(outs):
        out[...] = total_ref[pl.ds(pl.multiple_of(index_ref[s] * size, size), size), :].astype(out.dtype)


def place_kernel(index_ref, *refs):
    out_ref = refs[-1]
    for s, part in enumerate(refs[:-1]):
        out_ref[index_ref[s]] = part[...].astype(out_ref.dtype)


def final_kernel(core_ref, kept_ref, came_ref, self_out, neigh_out):
    first = core_ref[0] == 0
    kept, came = kept_ref[...].astype(F32), came_ref[...].astype(F32)
    self_out[...] = jnp.where(first, kept, came)
    neigh_out[...] = jnp.where(first, came, kept)


def join_kernel(own_ref, neigh_ref, row_ref, out_ref):
    joined = (own_ref[...] + neigh_ref[...].astype(F32)).astype(BF)
    out_ref[...] = dot(slots_onehot(row_ref[...][:1], out_ref.shape[0]), joined).astype(BF)


def on_device(
    features,
    tile_cols,
    tile_masks,
    degree,
    owner_nodes,
    owner_position,
    self_weight,
    neigh_weight,
    cotangent,
):
    rows, width = features.shape
    row_devices = lax.axis_size("row")
    col_devices = lax.axis_size("col")
    devices = row_devices * col_devices
    cap = 2 * rows // devices
    slots = devices * cap
    masks = tile_masks[0, 0]
    tile = masks.shape[-1]
    breadth = masks.shape[1]
    depth = rows // tile
    cols = tile_cols[0, 0].reshape(-1)
    me = lax.axis_index("row")
    ways = row_devices
    groups = jnp.bitwise_xor(me, jnp.arange(ways, dtype=jnp.int32)).astype(jnp.int32)
    everyone = ("row", "col")
    place = lax.axis_index("col")
    lines = col_devices // 2
    core = jnp.full((1,), lax.rem(place, 2), jnp.int32)
    others = jnp.bitwise_xor(lax.div(place, 2), jnp.arange(lines, dtype=jnp.int32)).astype(jnp.int32)
    SMEM = pl.BlockSpec(memory_space=pltpu.SMEM)

    def call(*args, mib=16, **kwargs):
        return pl.pallas_call(*args, compiler_params=params(mib), **kwargs)

    def shape(r, c, dtype=BF):
        return jax.ShapeDtypeStruct((r, c), dtype)

    def relay(packed):
        there = packed.reshape(devices, cap, -1)
        return lax.all_to_all(there, everyone, split_axis=0, concat_axis=0, tiled=True).reshape(slots, -1)

    def row_phase(packed):
        there = packed.reshape(row_devices, col_devices * cap, -1)
        return lax.all_to_all(there, "row", split_axis=0, concat_axis=0, tiled=True).reshape(slots, -1)

    def col_phase(packed):
        there = packed.reshape(col_devices, row_devices * cap, -1)
        return lax.all_to_all(there, "col", split_axis=0, concat_axis=0, tiled=True).reshape(slots, -1)

    def turn(packed, first, second):
        return packed.reshape(first, second, cap, -1).transpose(1, 0, 2, 3).reshape(slots, -1)

    def across(value, s):
        return lax.ppermute(value, "row", [(i, i ^ s) for i in range(ways)])

    def along(value, s):
        return lax.ppermute(value, "col", [(i, i ^ (2 * s)) for i in range(col_devices)])

    def swap(value):
        return lax.ppermute(value, "col", [(i, i ^ 1) for i in range(col_devices)])

    def split_sum(index, arrays, pieces, scale=1.0):
        r, c = arrays[0].shape
        return call(
            functools.partial(split_sum_kernel, len(arrays), scale),
            in_specs=[SMEM] + [VMEM] * len(arrays),
            out_specs=[VMEM] * pieces,
            out_shape=[shape(r // pieces, c) for _ in range(pieces)],
            scratch_shapes=[pltpu.VMEM((r, c), F32)],
            cost_estimate=cost(r * c * len(arrays), 2 * r * c * (len(arrays) + 1)),
            name="split_sum",
        )(index, *arrays)

    def in_place(index, arrays):
        count, (r, c) = len(arrays), arrays[0].shape
        return call(
            place_kernel,
            in_specs=[SMEM] + [VMEM] * count,
            out_specs=VMEM,
            out_shape=jax.ShapeDtypeStruct((count, r, c), BF),
            cost_estimate=cost(0, 4 * count * r * c),
            name="in_place",
        )(index, *arrays).reshape(count * r, c)

    nodes = owner_nodes.reshape(1, rows)
    slab = rows * width
    packed = call(
        functools.partial(pack_kernel, cap),
        out_shape=shape(slots, width),
        in_specs=[VMEM] * 2,
        out_specs=VMEM,
        cost_estimate=cost(2 * slots * slab, 6 * slab),
        mib=LARGE,
        name="pack_features",
    )(nodes, features)
    inbound = relay(packed)
    cot_packed, degree_packed, own_row, node_row, turned_row = call(
        functools.partial(index_kernel, cap, ways),
        out_shape=(shape(slots, width), shape(devices, cap, F32)) + (shape(8, rows, jnp.int32),) * 3,
        in_specs=[VMEM] * 4,
        out_specs=(VMEM,) * 5,
        cost_estimate=cost(2 * slots * slab, 6 * slab),
        mib=LARGE,
        name="index_cotangent",
    )(nodes, owner_position.reshape(1, rows), degree.reshape(1, rows), cotangent)
    ANY = pl.BlockSpec(memory_space=pl.ANY)
    x_node = call(
        unpack_kernel,
        out_shape=shape(rows, width),
        in_specs=[VMEM] * 2,
        out_specs=VMEM,
        cost_estimate=cost(2 * slots * slab, 6 * slab),
        name="unpack_features",
    )(node_row, inbound)
    cot_packed, degree_packed, x_node, cols, groups, core, others = lax.optimization_barrier(
        (cot_packed, degree_packed, x_node, cols, groups, core, others)
    )
    x_cols = lax.all_gather(x_node, "col", axis=0, tiled=True)
    cot_mid = turn(row_phase(cot_packed), row_devices, col_devices)
    degree_in = lax.all_to_all(degree_packed, everyone, split_axis=0, concat_axis=0, tiled=True)
    base, degrees = call(
        prepare_kernel,
        out_shape=(shape(rows, width, F32), shape(rows, 128, F32)),
        in_specs=[VMEM] * 4,
        out_specs=(VMEM,) * 2,
        cost_estimate=cost(2 * slab * width, 2 * slab * 4),
        mib=LARGE,
        name="prepare",
    )(x_node, degree_in, node_row, self_weight)
    x_cols, cot_mid, base, degrees = lax.optimization_barrier((x_cols, cot_mid, base, degrees))
    cot_in = col_phase(cot_mid)

    spmm_flops = 2 * masks.size * width * WEIGHT
    def piece_spec(p, count):
        share = depth // count
        return pl.BlockSpec((tile, width), lambda q, c, g: (jnp.clip(q - p * share, 0, share - 1), 0))

    def mask_spec(s):
        return pl.BlockSpec((1, breadth, tile, tile), lambda q, c, g: (g[s] * depth + q, 0, 0, 0))

    pieces = (1, 1, 1, 2) if ways == 4 else (1,) * ways
    half = rows // 2
    share = depth // 2

    def half_spec(s, part):
        return pl.BlockSpec((1, breadth, tile, tile), lambda i, c, g: ((g[s] * 2 + part) * share + i, 0, 0, 0))

    partials = call(
        functools.partial(spmm_kernel, ways),
        grid_spec=pltpu.PrefetchScalarGridSpec(
            num_scalar_prefetch=2,
            grid=(share,),
            in_specs=[VMEM] + [half_spec(s, part) for s in range(ways) for part in range(2)],
            out_specs=[pl.BlockSpec((tile, width), lambda i, c, g: (i, 0))] * (2 * ways),
        ),
        out_shape=[shape(half, width)] * (2 * ways),
        cost_estimate=cost(spmm_flops, 2 * masks.size + 2 * x_cols.size + 2 * ways * slab),
        mib=LARGE,
        name="spmm",
    )(cols, groups, x_cols, *([masks] * (2 * ways)))
    uppers, lowers = partials[::2], partials[1::2]
    if ways == 4:
        to_right, to_left = across(uppers[3], 1), across(lowers[3], 2)
        left_upper, right_lower = across(uppers[1], 1), across(lowers[2], 2)
        left_lower, right_upper = call(
            pass_on_kernel,
            out_shape=(shape(half, width),) * 2,
            in_specs=[VMEM] * 4,
            out_specs=(VMEM,) * 2,
            cost_estimate=cost(2 * slab, 6 * slab),
            name="pass_on",
        )(lowers[1], uppers[2], to_left, to_right)
        uppers = [uppers[0], left_upper, across(right_upper, 2)]
        lowers = [lowers[0], across(left_lower, 1), right_lower]
    else:
        uppers = [uppers[0]] + [across(uppers[s], s) for s in range(1, ways)]
        lowers = [lowers[0]] + [across(lowers[s], s) for s in range(1, ways)]
    cot_node = call(
        unpack_kernel,
        out_shape=shape(rows, width),
        in_specs=[VMEM] * 2,
        out_specs=VMEM,
        cost_estimate=cost(2 * slots * slab, 6 * slab),
        name="unpack_cotangent",
    )(turned_row, cot_in)

    def by_rows(columns):
        return pl.BlockSpec((half, columns), lambda i: (i, 0))

    hidden, slopes, agg, spread = call(
        functools.partial(layer_kernel, len(uppers)),
        grid=(2,),
        out_shape=(shape(rows, width),) * 4,
        in_specs=[VMEM] * (2 * len(uppers)) + [by_rows(width)] + [by_rows(128), by_rows(width), VMEM],
        out_specs=(by_rows(width),) * 4,
        cost_estimate=cost(8 * slab * width, 2 * slab * (len(uppers) + 9)),
        mib=LARGE,
        name="layer",
    )(*uppers, *lowers, base, degrees, cot_node, neigh_weight)
    hidden_packed = call(
        pack_node_kernel,
        out_shape=shape(slots, width),
        in_specs=[VMEM] * 2,
        out_specs=VMEM,
        cost_estimate=cost(2 * slots * slab, 6 * slab),
        name="pack_hidden",
    )(turned_row, hidden)
    if ways == 4:
        left, right = across(spread, 1), across(spread, 2)
        left, right, _ = lax.optimization_barrier((left, right, hidden_packed))
        spreads = [spread, left, right, across(right[:half], 1), across(left[half:], 2)]
    else:
        spreads = [spread] + [across(spread, s) for s in range(1, ways)]
    hidden_mid = col_phase(hidden_packed)
    grad_kept, grad_sent, own_back = call(
        terms_kernel,
        out_shape=(shape(width, width), shape(width, width), shape(rows, width, F32)),
        in_specs=[SMEM] + [VMEM] * 4,
        out_specs=(VMEM,) * 3,
        cost_estimate=cost(6 * slab * width, 2 * slab * 9),
        mib=LARGE,
        name="terms",
    )(core, x_node, agg, slopes, self_weight)
    *spreads, own_back, grad_kept, grad_sent = lax.optimization_barrier((*spreads, own_back, grad_kept, grad_sent))
    back = call(
        functools.partial(spmm_back_kernel, ways, pieces),
        grid_spec=pltpu.PrefetchScalarGridSpec(
            num_scalar_prefetch=2,
            grid=(depth,),
            in_specs=[piece_spec(p, count) for count in pieces for p in range(count)]
            + [mask_spec(s) for s in range(ways)],
            out_specs=ANY,
            scratch_shapes=[
                pltpu.VMEM(x_cols.shape, F32),
                pltpu.VMEM(x_cols.shape, BF),
                pltpu.SemaphoreType.DMA((col_devices,)),
            ],
        ),
        out_shape=shape(*x_cols.shape),
        cost_estimate=cost(spmm_flops, 2 * masks.size + 2 * x_cols.size + 2 * ways * slab),
        mib=LARGE,
        name="spmm_back",
    )(cols, groups, *spreads, *([masks] * ways))
    back, hidden_mid, grad_sent = lax.optimization_barrier((back, hidden_mid, grad_sent))
    neigh_back = lax.psum_scatter(back, "col", scatter_dimension=0, tiled=True)
    hidden_in = row_phase(turn(hidden_mid, col_devices, row_devices))
    pieces = split_sum(groups, [grad_kept, swap(grad_sent)], ways)
    pieces = split_sum(others, [pieces[0]] + [across(pieces[s], s) for s in range(1, ways)], lines)
    scale = 1.0 / math.sqrt(rows * devices)
    zero = jnp.zeros((1,), jnp.int32)
    (mine,) = split_sum(zero, [pieces[0]] + [along(pieces[s], s) for s in range(1, lines)], 1, scale)
    in_line = in_place(others, [mine] + [along(mine, s) for s in range(1, lines)])
    own_back, in_line = lax.optimization_barrier((own_back, in_line))
    grad_half = in_place(groups, [in_line] + [across(in_line, s) for s in range(1, ways)])
    grad_self, grad_neigh = call(
        final_kernel,
        in_specs=[SMEM] + [VMEM] * 2,
        out_specs=(VMEM,) * 2,
        out_shape=(shape(width, width, F32),) * 2,
        cost_estimate=cost(0, 12 * width * width),
        name="final",
    )(core, grad_half, swap(grad_half))
    grad_packed = call(
        join_kernel,
        out_shape=shape(slots, width),
        in_specs=[VMEM] * 3,
        out_specs=VMEM,
        cost_estimate=cost(2 * slots * slab, 8 * slab),
        name="join_pack",
    )(own_back, neigh_back, node_row)
    grad_in = relay(grad_packed)

    def unpack_own(value):
        return call(
            unpack_kernel,
            out_shape=shape(rows, width),
            in_specs=[VMEM] * 2,
            out_specs=VMEM,
            cost_estimate=cost(2 * slots * slab, 6 * slab),
            name="unpack_owner",
        )(own_row, value)

    hidden_own = unpack_own(hidden_in)
    grad_own = unpack_own(grad_in)
    return (hidden_own, grad_own, grad_self, grad_neigh)


def solution(mesh):
    placed = (
        P(("row", "col"), None),
        P("row", "col", None, None),
        P("row", "col", None, None, None, None),
        P(("row", "col")),
        P(("row", "col")),
        P(("row", "col")),
        P(),
        P(),
        P(("row", "col"), None),
    )
    return jax.shard_map(
        on_device,
        mesh=mesh,
        in_specs=placed,
        out_specs=(P(("row", "col"), None), P(("row", "col"), None), P(), P()),
        check_vma=False,
    )
```

```python
import functools
import math

import jax
import jax.numpy as jnp
from jax import lax
from jax.experimental import pallas as pl
from jax.experimental.pallas import tpu as pltpu
from jax.sharding import PartitionSpec as P

BF = jnp.bfloat16
F32 = jnp.float32
VMEM = pl.BlockSpec(memory_space=pltpu.VMEM)
MIB = 1024 * 1024
LARGE = 56
WEIGHT = 6


def params(mib=16):
    return pltpu.CompilerParams(vmem_limit_bytes=int(mib * MIB))


def cost(flops, nbytes):
    return pl.CostEstimate(flops=int(flops), bytes_accessed=int(nbytes), transcendentals=0)


def dot(a, b, ca=1, cb=0):
    return lax.dot_general(a, b, (((ca,), (cb,)), ((), ())), preferred_element_type=F32)


def as_column(row):
    return jnp.broadcast_to(row, (128, row.shape[1])).T


def block_of(index, size):
    if size & (size - 1) == 0:
        return lax.shift_right_logical(index, size.bit_length() - 1)
    return lax.div(index, jnp.full_like(index, size))


def rank_row(group_row, order_row):
    n = group_row.shape[1]
    group_col = as_column(group_row)[:, :1]
    order_col = as_column(order_row)[:, :1]
    earlier = (group_col == group_row) & (order_col < order_row)
    return jnp.sum(jnp.where(earlier, 1.0, 0.0), axis=0, keepdims=True).astype(jnp.int32)


def slots_onehot(flat_row, slots):
    iota = lax.broadcasted_iota(jnp.int32, (slots, flat_row.shape[1]), 0)
    return jnp.where(iota == flat_row, 1.0, 0.0).astype(BF)


def entries_onehot(flat_col, slots):
    iota = lax.broadcasted_iota(jnp.int32, (flat_col.shape[0], slots), 1)
    return jnp.where(flat_col[:, :1] == iota, 1.0, 0.0).astype(BF)


def own_slots(nodes_row, cap):
    n = nodes_row.shape[1]
    dest = block_of(nodes_row, n)
    rank = rank_row(dest, lax.broadcasted_iota(jnp.int32, (1, n), 1))
    return dest, rank


def pack_kernel(cap, nodes_ref, value_ref, out_ref):
    dest, rank = own_slots(nodes_ref[...], cap)
    out_ref[...] = dot(slots_onehot(dest * cap + rank, out_ref.shape[0]), value_ref[...]).astype(BF)


def index_kernel(cap, ways, nodes_ref, position_ref, degree_ref, cot_ref, cot_out, degree_out, own_row, node_row, turned_row):
    n = nodes_ref.shape[1]
    devices = degree_out.shape[0]
    dest, rank = own_slots(nodes_ref[...], cap)
    flat = dest * cap + rank
    own_row[...] = jnp.broadcast_to(flat, own_row.shape)
    cot_out[...] = dot(slots_onehot(flat, cot_out.shape[0]), cot_ref[...]).astype(BF)
    by_dest = jnp.where(lax.broadcasted_iota(jnp.int32, (devices, n), 0) == dest, degree_ref[...].astype(F32), 0.0)
    degree_out[...] = dot(by_dest.astype(BF), entries_onehot(as_column(rank), cap))
    position = position_ref[...]
    source = block_of(position, n)
    rank = rank_row(source, position)
    node_row[...] = jnp.broadcast_to(source * cap + rank, node_row.shape)
    across = cot_out.shape[0] // (cap * ways)
    down = block_of(source, across)
    turned = ((source - down * across) * ways + down) * cap + rank
    turned_row[...] = jnp.broadcast_to(turned, turned_row.shape)


def unpack_kernel(row_ref, value_ref, out_ref):
    out_ref[...] = dot(entries_onehot(as_column(row_ref[...][:1]), value_ref.shape[0]), value_ref[...]).astype(BF)


def spmm_kernel(ways, cols_ref, group_ref, x_ref, *refs):
    masks, outs = refs[: 2 * ways], refs[2 * ways :]
    i = pl.program_id(0)
    share = pl.num_programs(0)
    _, breadth, tile, _ = masks[0].shape
    for at, (mask_ref, out_ref) in enumerate(zip(masks, outs)):
        s, part = divmod(at, 2)
        base = ((group_ref[s] * 2 + part) * share + i) * breadth
        total = None
        for p in range(0, breadth, 2):
            span = range(p, min(p + 2, breadth))
            left = jnp.concatenate([mask_ref[0, k] for k in span], axis=1)
            right = jnp.concatenate(
                [x_ref[pl.ds(pl.multiple_of(cols_ref[base + k] * tile, tile), tile), :] for k in span], axis=0
            )
            term = dot(left, right)
            total = term if total is None else total + term
        out_ref[...] = total.astype(BF)


def spmm_back_kernel(ways, pieces, cols_ref, group_ref, *refs):
    given = sum(pieces)
    spreads, masks = refs[:given], refs[given : given + ways]
    out_hbm, total, ready, sems = refs[given + ways :]
    q = pl.program_id(0)
    depth = pl.num_programs(0)
    _, breadth, tile, _ = masks[0].shape

    @pl.when(q == 0)
    def _():
        total[...] = jnp.zeros_like(total)

    at_piece = 0
    for s in range(ways):
        base = (group_ref[s] * depth + q) * breadth
        rows = spreads[at_piece][...]
        for p in range(1, pieces[s]):
            rows = jnp.where(q * pieces[s] >= p * depth, spreads[at_piece + p][...], rows)
        at_piece += pieces[s]
        for k in range(breadth):
            at = pl.ds(pl.multiple_of(cols_ref[base + k] * tile, tile), tile)
            total[at, :] += dot(masks[s][0, k], rows, 0, 0)

    @pl.when(q == depth - 1)
    def _():
        count = sems.shape[0]
        share = total.shape[0] // count
        copies = []
        for i in range(count):
            at = pl.ds(i * share, share)
            ready[at, :] = total[at, :].astype(BF)
            copies.append(pltpu.make_async_copy(ready.at[at], out_hbm.at[at], sems.at[i]))
            copies[-1].start()
        for copy in copies:
            copy.wait()


def pass_on_kernel(left_ref, right_ref, to_left_ref, to_right_ref, left_out, right_out):
    left_out[...] = (left_ref[...].astype(F32) + to_left_ref[...].astype(F32)).astype(BF)
    right_out[...] = (right_ref[...].astype(F32) + to_right_ref[...].astype(F32)).astype(BF)


def prepare_kernel(x_ref, degree_ref, row_ref, self_ref, base_out, degree_out):
    devices, cap = degree_ref.shape
    base_out[...] = dot(x_ref[...], self_ref[...])
    place = as_column(row_ref[...][:1])[:, :1]
    source = block_of(place, cap)
    rank = place - source * cap
    degrees = dot(entries_onehot(source, devices), degree_ref[...].astype(BF))
    picked = lax.broadcasted_iota(jnp.int32, degrees.shape, 1) == rank
    degrees = jnp.sum(jnp.where(picked, degrees, 0.0), axis=1, keepdims=True)
    degree_out[...] = jnp.broadcast_to(degrees, degree_out.shape)


def layer_kernel(ways, *refs):
    uppers, lowers = refs[:ways], refs[ways : 2 * ways]
    (base_ref, degree_ref, cot_ref, neigh_ref, hidden_out, slopes_out, agg_out, spread_out) = refs[2 * ways :]
    lower = pl.program_id(0) == 1
    summed = 0.0
    for up_ref, low_ref in zip(uppers, lowers):
        summed = summed + jnp.where(lower, low_ref[...], up_ref[...]).astype(F32)
    degrees = degree_ref[...][:, :1]
    agg = (summed / degrees).astype(BF)
    agg_out[...] = agg
    preact = base_ref[...] + dot(agg, neigh_ref[...])
    gate = jax.nn.sigmoid(preact)
    hidden_out[...] = (preact * gate).astype(BF)
    slopes = (cot_ref[...].astype(F32) * gate * (1.0 + preact * (1.0 - gate))).astype(BF)
    slopes_out[...] = slopes
    spread_out[...] = (dot(slopes, neigh_ref[...], 1, 1) / degrees).astype(BF)


def pack_node_kernel(row_ref, value_ref, out_ref):
    out_ref[...] = dot(slots_onehot(row_ref[...][:1], out_ref.shape[0]), value_ref[...]).astype(BF)


def terms_kernel(core_ref, x_ref, agg_ref, slopes_ref, self_ref, kept_out, sent_out, back_out):
    slopes = slopes_ref[...]
    back_out[...] = dot(slopes, self_ref[...], 1, 1)
    grad_self = dot(x_ref[...], slopes, 0, 0).astype(BF)
    grad_neigh = dot(agg_ref[...], slopes, 0, 0).astype(BF)
    first = core_ref[0] == 0
    kept_out[...] = jnp.where(first, grad_self, grad_neigh)
    sent_out[...] = jnp.where(first, grad_neigh, grad_self)


def split_sum_kernel(count, scale, index_ref, *refs):
    terms, outs, total_ref = refs[:count], refs[count:-1], refs[-1]
    total = terms[0][...].astype(F32)
    for term in terms[1:]:
        total = total + term[...].astype(F32)
    total_ref[...] = total * scale
    size = outs[0].shape[0]
    for s, out in enumerate(outs):
        out[...] = total_ref[pl.ds(pl.multiple_of(index_ref[s] * size, size), size), :].astype(out.dtype)


def place_kernel(index_ref, *refs):
    out_ref = refs[-1]
    for s, part in enumerate(refs[:-1]):
        out_ref[index_ref[s]] = part[...].astype(out_ref.dtype)


def final_kernel(core_ref, kept_ref, came_ref, self_out, neigh_out):
    first = core_ref[0] == 0
    kept, came = kept_ref[...].astype(F32), came_ref[...].astype(F32)
    self_out[...] = jnp.where(first, kept, came)
    neigh_out[...] = jnp.where(first, came, kept)


def join_kernel(own_ref, neigh_ref, row_ref, out_ref):
    joined = (own_ref[...] + neigh_ref[...].astype(F32)).astype(BF)
    out_ref[...] = dot(slots_onehot(row_ref[...][:1], out_ref.shape[0]), joined).astype(BF)


def on_device(
    features,
    tile_cols,
    tile_masks,
    degree,
    owner_nodes,
    owner_position,
    self_weight,
    neigh_weight,
    cotangent,
):
    rows, width = features.shape
    row_devices = lax.axis_size("row")
    col_devices = lax.axis_size("col")
    devices = row_devices * col_devices
    cap = 2 * rows // devices
    slots = devices * cap
    masks = tile_masks[0, 0]
    tile = masks.shape[-1]
    breadth = masks.shape[1]
    depth = rows // tile
    cols = tile_cols[0, 0].reshape(-1)
    me = lax.axis_index("row")
    ways = row_devices
    groups = jnp.bitwise_xor(me, jnp.arange(ways, dtype=jnp.int32)).astype(jnp.int32)
    everyone = ("row", "col")
    place = lax.axis_index("col")
    lines = col_devices // 2
    core = jnp.full((1,), lax.rem(place, 2), jnp.int32)
    others = jnp.bitwise_xor(lax.div(place, 2), jnp.arange(lines, dtype=jnp.int32)).astype(jnp.int32)
    SMEM = pl.BlockSpec(memory_space=pltpu.SMEM)

    def call(*args, mib=16, **kwargs):
        return pl.pallas_call(*args, compiler_params=params(mib), **kwargs)

    def shape(r, c, dtype=BF):
        return jax.ShapeDtypeStruct((r, c), dtype)

    def relay(packed):
        there = packed.reshape(devices, cap, -1)
        return lax.all_to_all(there, everyone, split_axis=0, concat_axis=0, tiled=True).reshape(slots, -1)

    def row_phase(packed):
        there = packed.reshape(row_devices, col_devices * cap, -1)
        return lax.all_to_all(there, "row", split_axis=0, concat_axis=0, tiled=True).reshape(slots, -1)

    def col_phase(packed):
        there = packed.reshape(col_devices, row_devices * cap, -1)
        return lax.all_to_all(there, "col", split_axis=0, concat_axis=0, tiled=True).reshape(slots, -1)

    def turn(packed, first, second):
        return packed.reshape(first, second, cap, -1).transpose(1, 0, 2, 3).reshape(slots, -1)

    def across(value, s):
        return lax.ppermute(value, "row", [(i, i ^ s) for i in range(ways)])

    def along(value, s):
        return lax.ppermute(value, "col", [(i, i ^ (2 * s)) for i in range(col_devices)])

    def swap(value):
        return lax.ppermute(value, "col", [(i, i ^ 1) for i in range(col_devices)])

    def split_sum(index, arrays, pieces, scale=1.0):
        r, c = arrays[0].shape
        return call(
            functools.partial(split_sum_kernel, len(arrays), scale),
            in_specs=[SMEM] + [VMEM] * len(arrays),
            out_specs=[VMEM] * pieces,
            out_shape=[shape(r // pieces, c) for _ in range(pieces)],
            scratch_shapes=[pltpu.VMEM((r, c), F32)],
            cost_estimate=cost(r * c * len(arrays), 2 * r * c * (len(arrays) + 1)),
            name="split_sum",
        )(index, *arrays)

    def in_place(index, arrays):
        count, (r, c) = len(arrays), arrays[0].shape
        return call(
            place_kernel,
            in_specs=[SMEM] + [VMEM] * count,
            out_specs=VMEM,
            out_shape=jax.ShapeDtypeStruct((count, r, c), BF),
            cost_estimate=cost(0, 4 * count * r * c),
            name="in_place",
        )(index, *arrays).reshape(count * r, c)

    nodes = owner_nodes.reshape(1, rows)
    slab = rows * width
    packed = call(
        functools.partial(pack_kernel, cap),
        out_shape=shape(slots, width),
        in_specs=[VMEM] * 2,
        out_specs=VMEM,
        cost_estimate=cost(2 * slots * slab, 6 * slab),
        mib=LARGE,
        name="pack_features",
    )(nodes, features)
    inbound = relay(packed)
    cot_packed, degree_packed, own_row, node_row, turned_row = call(
        functools.partial(index_kernel, cap, ways),
        out_shape=(shape(slots, width), shape(devices, cap, F32)) + (shape(8, rows, jnp.int32),) * 3,
        in_specs=[VMEM] * 4,
        out_specs=(VMEM,) * 5,
        cost_estimate=cost(2 * slots * slab, 6 * slab),
        mib=LARGE,
        name="index_cotangent",
    )(nodes, owner_position.reshape(1, rows), degree.reshape(1, rows), cotangent)
    ANY = pl.BlockSpec(memory_space=pl.ANY)
    x_node = call(
        unpack_kernel,
        out_shape=shape(rows, width),
        in_specs=[VMEM] * 2,
        out_specs=VMEM,
        cost_estimate=cost(2 * slots * slab, 6 * slab),
        name="unpack_features",
    )(node_row, inbound)
    cot_packed, degree_packed, x_node, cols, groups, core, others = lax.optimization_barrier(
        (cot_packed, degree_packed, x_node, cols, groups, core, others)
    )
    x_cols = lax.all_gather(x_node, "col", axis=0, tiled=True)
    cot_mid = turn(row_phase(cot_packed), row_devices, col_devices)
    degree_in = lax.all_to_all(degree_packed, everyone, split_axis=0, concat_axis=0, tiled=True)
    base, degrees = call(
        prepare_kernel,
        out_shape=(shape(rows, width, F32), shape(rows, 128, F32)),
        in_specs=[VMEM] * 4,
        out_specs=(VMEM,) * 2,
        cost_estimate=cost(2 * slab * width, 2 * slab * 4),
        mib=LARGE,
        name="prepare",
    )(x_node, degree_in, node_row, self_weight)
    x_cols, cot_mid, base, degrees = lax.optimization_barrier((x_cols, cot_mid, base, degrees))
    cot_in = col_phase(cot_mid)

    spmm_flops = 2 * masks.size * width * WEIGHT
    def piece_spec(p, count):
        share = depth // count
        return pl.BlockSpec((tile, width), lambda q, c, g: (jnp.clip(q - p * share, 0, share - 1), 0))

    def mask_spec(s):
        return pl.BlockSpec((1, breadth, tile, tile), lambda q, c, g: (g[s] * depth + q, 0, 0, 0))

    pieces = (1, 1, 1, 2) if ways == 4 else (1,) * ways
    half = rows // 2
    share = depth // 2

    def half_spec(s, part):
        return pl.BlockSpec((1, breadth, tile, tile), lambda i, c, g: ((g[s] * 2 + part) * share + i, 0, 0, 0))

    partials = call(
        functools.partial(spmm_kernel, ways),
        grid_spec=pltpu.PrefetchScalarGridSpec(
            num_scalar_prefetch=2,
            grid=(share,),
            in_specs=[VMEM] + [half_spec(s, part) for s in range(ways) for part in range(2)],
            out_specs=[pl.BlockSpec((tile, width), lambda i, c, g: (i, 0))] * (2 * ways),
        ),
        out_shape=[shape(half, width)] * (2 * ways),
        cost_estimate=cost(spmm_flops, 2 * masks.size + 2 * x_cols.size + 2 * ways * slab),
        mib=LARGE,
        name="spmm",
    )(cols, groups, x_cols, *([masks] * (2 * ways)))
    uppers, lowers = partials[::2], partials[1::2]
    if ways == 4:
        to_right, to_left = across(uppers[3], 1), across(lowers[3], 2)
        left_upper, right_lower = across(uppers[1], 1), across(lowers[2], 2)
        left_lower, right_upper = call(
            pass_on_kernel,
            out_shape=(shape(half, width),) * 2,
            in_specs=[VMEM] * 4,
            out_specs=(VMEM,) * 2,
            cost_estimate=cost(2 * slab, 6 * slab),
            mib=LARGE,
            name="pass_on",
        )(lowers[1], uppers[2], to_left, to_right)
        uppers = [uppers[0], left_upper, across(right_upper, 2)]
        lowers = [lowers[0], across(left_lower, 1), right_lower]
    else:
        uppers = [uppers[0]] + [across(uppers[s], s) for s in range(1, ways)]
        lowers = [lowers[0]] + [across(lowers[s], s) for s in range(1, ways)]
    cot_node = call(
        unpack_kernel,
        out_shape=shape(rows, width),
        in_specs=[VMEM] * 2,
        out_specs=VMEM,
        cost_estimate=cost(2 * slots * slab, 6 * slab),
        name="unpack_cotangent",
    )(turned_row, cot_in)

    def by_rows(columns):
        return pl.BlockSpec((half, columns), lambda i: (i, 0))

    hidden, slopes, agg, spread = call(
        functools.partial(layer_kernel, len(uppers)),
        grid=(2,),
        out_shape=(shape(rows, width),) * 4,
        in_specs=[VMEM] * (2 * len(uppers)) + [by_rows(width)] + [by_rows(128), by_rows(width), VMEM],
        out_specs=(by_rows(width),) * 4,
        cost_estimate=cost(8 * slab * width, 2 * slab * (len(uppers) + 9)),
        mib=LARGE,
        name="layer",
    )(*uppers, *lowers, base, degrees, cot_node, neigh_weight)
    hidden_packed = call(
        pack_node_kernel,
        out_shape=shape(slots, width),
        in_specs=[VMEM] * 2,
        out_specs=VMEM,
        cost_estimate=cost(2 * slots * slab, 6 * slab),
        mib=LARGE,
        name="pack_hidden",
    )(turned_row, hidden)
    if ways == 4:
        left, right = across(spread, 1), across(spread, 2)
        left, right, _ = lax.optimization_barrier((left, right, hidden_packed))
        spreads = [spread, left, right, across(right[:half], 1), across(left[half:], 2)]
    else:
        spreads = [spread] + [across(spread, s) for s in range(1, ways)]
    hidden_mid = col_phase(hidden_packed)
    grad_kept, grad_sent, own_back = call(
        terms_kernel,
        out_shape=(shape(width, width), shape(width, width), shape(rows, width, F32)),
        in_specs=[SMEM] + [VMEM] * 4,
        out_specs=(VMEM,) * 3,
        cost_estimate=cost(6 * slab * width, 2 * slab * 9),
        mib=LARGE,
        name="terms",
    )(core, x_node, agg, slopes, self_weight)
    *spreads, own_back, grad_kept, grad_sent = lax.optimization_barrier((*spreads, own_back, grad_kept, grad_sent))
    back = call(
        functools.partial(spmm_back_kernel, ways, pieces),
        grid_spec=pltpu.PrefetchScalarGridSpec(
            num_scalar_prefetch=2,
            grid=(depth,),
            in_specs=[piece_spec(p, count) for count in pieces for p in range(count)]
            + [mask_spec(s) for s in range(ways)],
            out_specs=ANY,
            scratch_shapes=[
                pltpu.VMEM(x_cols.shape, F32),
                pltpu.VMEM(x_cols.shape, BF),
                pltpu.SemaphoreType.DMA((col_devices,)),
            ],
        ),
        out_shape=shape(*x_cols.shape),
        cost_estimate=cost(spmm_flops, 2 * masks.size + 2 * x_cols.size + 2 * ways * slab),
        mib=LARGE,
        name="spmm_back",
    )(cols, groups, *spreads, *([masks] * ways))
    back, hidden_mid, grad_sent = lax.optimization_barrier((back, hidden_mid, grad_sent))
    neigh_back = lax.psum_scatter(back, "col", scatter_dimension=0, tiled=True)
    hidden_in = row_phase(turn(hidden_mid, col_devices, row_devices))
    pieces = split_sum(groups, [grad_kept, swap(grad_sent)], ways)
    pieces = split_sum(others, [pieces[0]] + [across(pieces[s], s) for s in range(1, ways)], lines)
    scale = 1.0 / math.sqrt(rows * devices)
    zero = jnp.zeros((1,), jnp.int32)
    (mine,) = split_sum(zero, [pieces[0]] + [along(pieces[s], s) for s in range(1, lines)], 1, scale)
    in_line = in_place(others, [mine] + [along(mine, s) for s in range(1, lines)])
    own_back, in_line = lax.optimization_barrier((own_back, in_line))
    grad_half = in_place(groups, [in_line] + [across(in_line, s) for s in range(1, ways)])
    grad_self, grad_neigh = call(
        final_kernel,
        in_specs=[SMEM] + [VMEM] * 2,
        out_specs=(VMEM,) * 2,
        out_shape=(shape(width, width, F32),) * 2,
        cost_estimate=cost(0, 12 * width * width),
        name="final",
    )(core, grad_half, swap(grad_half))
    grad_packed = call(
        join_kernel,
        out_shape=shape(slots, width),
        in_specs=[VMEM] * 3,
        out_specs=VMEM,
        cost_estimate=cost(2 * slots * slab, 8 * slab),
        name="join_pack",
    )(own_back, neigh_back, node_row)
    grad_in = relay(grad_packed)

    def unpack_own(value):
        return call(
            unpack_kernel,
            out_shape=shape(rows, width),
            in_specs=[VMEM] * 2,
            out_specs=VMEM,
            cost_estimate=cost(2 * slots * slab, 6 * slab),
            name="unpack_owner",
        )(own_row, value)

    hidden_own = unpack_own(hidden_in)
    grad_own = unpack_own(grad_in)
    return (hidden_own, grad_own, grad_self, grad_neigh)


def solution(mesh):
    placed = (
        P(("row", "col"), None),
        P("row", "col", None, None),
        P("row", "col", None, None, None, None),
        P(("row", "col")),
        P(("row", "col")),
        P(("row", "col")),
        P(),
        P(),
        P(("row", "col"), None),
    )
    return jax.shard_map(
        on_device,
        mesh=mesh,
        in_specs=placed,
        out_specs=(P(("row", "col"), None), P(("row", "col"), None), P(), P()),
        check_vma=False,
    )
```
